256 devices in a mesh: db: 32 (over x, z), mp: 4 (over y), section: 2 (over core).
Axes of the slice: x: 4, y: 4, z: 8, core: 2. Of those that a mesh axis runs over, the one named last changes fastest.
Arguments:
- queries: bfloat16 [16384, 8192], P('db', ('mp', 'section')), may hold values from -6 to 6
- database: bfloat16 [128, 1024, 1024], P(None, 'db', ('mp', 'section')), may hold values from -6 to 6
- neighbour_ids: int32 [256, 2], P('db'), may hold values from 0 to 1023, as said below
- live_counts: int32 [256], P('db'), may hold values from 1 to 2
- entry_rows: int32 [1024], replicated, may hold values from 0 to 1023, as said below
- enc_gain: float32 [2, 1024], replicated, may hold values from 0.1 to 1.9
- enc_qkv: bfloat16 [2, 1024, 3, 1024], P(None, None, None, ('mp', 'section')), may hold values from -0.1875 to 0.1875
- enc_out: bfloat16 [2, 1024, 1024], replicated, may hold values from -0.1875 to 0.1875
- final_gain: float32 [1024], replicated, may hold values from 0.1 to 1.9
- kv_weight: bfloat16 [1024, 2, 8192], P(None, None, ('mp', 'section')), may hold values from -0.1875 to 0.1875
Outputs:
- retrieved: bfloat16 [16384, 8192], P('db', ('mp', 'section'))
The draws below stay inside these ranges and needn't reach their ends.
Inputs may be any that keep to these rules, and one draw needn't show every extreme that they name: `neighbour_ids`: entry c lies on db shard entry_rows[c] // 32. Of the 16 ids in the rows of one db index, at most 2 lie on one shard; one shard, the same for all db indices, holds exactly 2 of every db index's ids, and at least one other shard holds exactly 2 too. `entry_rows`: A permutation of the entry ids.
All inputs are finite; a program needn't handle non-finite values.
Results may differ from the reference program's by a relative error of at most 0.035.
Values may be sent and summed in bfloat16 or wider, within the bound.
A program may use at most 128 MiB of HBM per device.

```python
import math
import jax
import jax.numpy as jnp
from jax import lax

E = 1024
HD = 128
DM = 8192
NL = 128
BL = 64
KNB = 2
LAYERS = 2
QB_DEV = 8
DB_DEV = 32
CAP = 2
ENTRIES = 1024
QBLOCKS = 256
TOKENS = 16384
N_DB = 32


def shared_rows(key):
    return jax.random.permutation(key, ENTRIES).astype(jnp.int32)


def draw_entry_rows(key, part):
    return shared_rows(key)


def draw_neighbour_ids(key, part):
    rows_of = shared_rows(key)
    key = jax.random.fold_in(key, 5)
    subkeys = jax.random.split(key, 5)
    requests = QB_DEV * KNB
    remaining = requests - 2 * CAP
    hottest = jax.random.randint(subkeys[0], (), 0, N_DB)
    runner_up = (hottest + 1 + jax.random.randint(subkeys[1], (N_DB,), 0, N_DB - 1)) % N_DB
    lower_shard = jnp.minimum(hottest, runner_up)[:, None]
    upper_shard = jnp.maximum(hottest, runner_up)[:, None]
    drawn = jax.vmap(lambda subkey: jax.random.permutation(subkey, (N_DB - 2) * CAP))(jax.random.split(subkeys[2], N_DB))
    others = drawn[:, :remaining] // CAP
    others = others + (others >= lower_shard).astype(jnp.int32)
    others = others + (others >= upper_shard).astype(jnp.int32)
    first_part = jnp.broadcast_to(hottest, (N_DB, CAP)).astype(jnp.int32)
    second_part = jnp.broadcast_to(runner_up[:, None], (N_DB, CAP)).astype(jnp.int32)
    shard_of = jnp.concatenate([first_part, second_part, others.astype(jnp.int32)], axis=1)
    ordering = jax.vmap(lambda subkey: jax.random.permutation(subkey, requests))(jax.random.split(subkeys[3], N_DB))
    shard_of = jnp.take_along_axis(shard_of, ordering, axis=1)
    slot_index = jax.random.randint(subkeys[4], (N_DB, requests), 0, DB_DEV)
    inverse = jnp.zeros((ENTRIES,), jnp.int32).at[rows_of].set(jnp.arange(ENTRIES, dtype=jnp.int32))
    entry_ids = inverse[shard_of * DB_DEV + slot_index]
    return entry_ids.reshape(QBLOCKS, KNB).astype(jnp.int32)


def place_ends(result, own_key, least, top_value):
    dims = result.shape
    place = [jax.random.randint(jax.random.fold_in(own_key, axis), (), 0, dims[axis]) for axis in range(len(dims))]
    result = result.at[tuple(place)].set(least)
    longest = dims.index(max(dims))
    place[longest] = (place[longest] + 1) % dims[longest]
    return result.at[tuple(place)].set(top_value)


def level_of(key, extent, cuts, low, largest):
    level, own = 1.0, jax.random.fold_in(key, 6)
    for axis_at, shards_of in cuts:
        draws = jnp.exp(jax.random.uniform(jax.random.fold_in(own, axis_at), (shards_of,), jnp.float32, low / len(cuts), largest / len(cuts)))
        level = level * jnp.repeat(draws, extent[axis_at] // shards_of).reshape([-1 if axis == axis_at else 1 for axis in range(len(extent))])
    return level


def noise(rng, shape, scale, most, pieces=(), kind=jnp.bfloat16):
    gain = level_of(rng, shape, pieces, -0.22, 0.18) if pieces else 1.0
    array = jax.random.normal(rng, shape, jnp.float32) * scale * gain
    return jnp.minimum(jnp.maximum(array, -most), most).astype(kind)


def setup_inputs(seed: int = 0) -> dict:
    key_list = jax.random.split(jax.random.key(seed), 11)
    return {
        "queries": noise(key_list[0], (TOKENS, DM), 1.0, 6.0, ((0, 32), (1, 8))),
        "database": noise(key_list[1], (NL, ENTRIES, E), 1.0, 6.0, ((1, 32), (2, 8))),
        "neighbour_ids": draw_neighbour_ids(jax.random.fold_in(key_list[10], 71), 0),
        "live_counts": place_ends(jax.random.randint(key_list[3], (QBLOCKS,), 1, KNB + 1), jax.random.fold_in(key_list[3], 1), 1, KNB).astype(jnp.int32),
        "entry_rows": draw_entry_rows(jax.random.fold_in(key_list[10], 71), 0),
        "enc_gain": jnp.clip(1.0 + 0.18 * jax.random.normal(key_list[5], (LAYERS, E), jnp.float32), 0.1, 1.9),
        "enc_qkv": noise(key_list[6], (LAYERS, E, 3, E), E ** -0.5, 0.1875, ((3, 8),)),
        "enc_out": noise(key_list[7], (LAYERS, E, E), E ** -0.5, 0.1875),
        "final_gain": jnp.clip(1.0 + 0.18 * jax.random.normal(key_list[8], (E,), jnp.float32), 0.1, 1.9),
        "kv_weight": noise(key_list[9], (E, 2, DM), E ** -0.5, 0.1875, ((2, 8),)),
    }


def unit_heads(tensor):
    return tensor * lax.rsqrt(lax.optimization_barrier(jnp.mean(tensor * tensor, axis=-1, keepdims=True)) + 1e-06)

def encode_group(located, database, enc_gain, enc_qkv, enc_out, final_gain, kv_weight):
    hidden = jnp.take(database, located, axis=1).astype(jnp.float32)
    heads = E // HD
    score_scale = 3.0 / math.sqrt(HD)
    for layer_index in range(LAYERS):
        normed = (unit_heads(hidden) * enc_gain[layer_index]).astype(jnp.bfloat16)
        weight = enc_qkv[layer_index].reshape(E, 3, heads, HD).astype(jnp.float32)
        mixture = jnp.einsum('pre,ethd->prthd', normed.astype(jnp.float32), weight)
        query_unit = unit_heads(mixture[:, :, 0]).astype(jnp.bfloat16)
        key_unit = unit_heads(mixture[:, :, 1]).astype(jnp.bfloat16)
        value_rows = mixture[:, :, 2].astype(jnp.bfloat16)
        scores = jnp.einsum('prhd,srhd->rhps', query_unit.astype(jnp.float32), key_unit.astype(jnp.float32)) * score_scale
        weights = jnp.exp(scores)
        shares = (weights / lax.optimization_barrier(jnp.sum(weights, axis=3, keepdims=True))).astype(jnp.bfloat16)
        attended = jnp.einsum('rhps,srhd->prhd', shares.astype(jnp.float32), value_rows.astype(jnp.float32)).astype(jnp.bfloat16)
        flat = attended.reshape(NL, attended.shape[1], E).astype(jnp.float32)
        hidden = hidden + jnp.einsum('prf,fe->pre', flat, enc_out[layer_index].astype(jnp.float32))
    encoded = (unit_heads(hidden) * final_gain).astype(jnp.bfloat16)
    mixture = jnp.einsum('pre,etf->prtf', encoded.astype(jnp.float32), kv_weight.astype(jnp.float32))
    key_heads = unit_heads(mixture[:, :, 0].reshape(NL, -1, DM // HD, HD)).astype(jnp.bfloat16)
    value_heads = mixture[:, :, 1].reshape(NL, -1, DM // HD, HD).astype(jnp.bfloat16)
    return (key_heads, value_heads)

def cross_attend(query_rows, key_heads, value_heads, counts):
    tokens = QB_DEV * BL
    heads = DM // HD
    score_scale = 3.0 / math.sqrt(HD)
    query_heads = unit_heads(query_rows.reshape(tokens, heads, HD).astype(jnp.float32)).astype(jnp.bfloat16)
    padding = jnp.zeros((BL - 1, heads, HD), jnp.bfloat16)
    shifted = jnp.concatenate([query_heads[BL - 1:], padding], axis=0).reshape(QB_DEV, BL, heads, HD)
    key_grid = key_heads.reshape(NL, QB_DEV, KNB, heads, HD).astype(jnp.float32)
    value_grid = value_heads.reshape(NL, QB_DEV, KNB, heads, HD).astype(jnp.float32)
    scores = jnp.einsum('cqha,scnha->chqsn', shifted.astype(jnp.float32), key_grid) * score_scale
    live_mask = (jnp.arange(KNB, dtype=jnp.int32)[None, :] < counts[:, None]).astype(jnp.float32)
    weights = jnp.exp(scores) * live_mask[:, None, None, None, :]
    shares = (weights / lax.optimization_barrier(jnp.sum(weights, axis=(3, 4), keepdims=True))).astype(jnp.bfloat16)
    mixture = jnp.einsum('chqsn,scnha->cqha', shares.astype(jnp.float32), value_grid).reshape(tokens, DM)
    front = jnp.zeros((BL - 1, DM), jnp.float32)
    return jnp.concatenate([front, mixture[:tokens - BL + 1]], axis=0).astype(jnp.bfloat16)

def reference(queries, database, neighbour_ids, live_counts, entry_rows, enc_gain, enc_qkv, enc_out, final_gain, kv_weight):
    located = jnp.take(entry_rows, neighbour_ids.reshape(-1)).astype(jnp.int32)
    located = located.reshape(N_DB, QB_DEV * KNB)
    counts = live_counts.reshape(N_DB, QB_DEV)
    query_groups = queries.reshape(N_DB, QB_DEV * BL, DM)

    def per_group(inputs):
        group_rows, group_counts, group_queries = inputs
        key_heads, value_heads = encode_group(group_rows, database, enc_gain, enc_qkv, enc_out, final_gain, kv_weight)
        return cross_attend(group_queries, key_heads, value_heads, group_counts)
    retrieved = lax.map(per_group, (located, counts, query_groups))
    return retrieved.reshape(TOKENS, DM)
```

```python
import math

import jax
import jax.numpy as jnp
from jax import lax
from jax.sharding import PartitionSpec as P

BL = 64
GROUP = ("mp", "section")


def unit_heads(tensor):
    return tensor * lax.rsqrt(jnp.mean(tensor * tensor, axis=-1, keepdims=True) + 1e-06)


def on_device(
    queries,
    database,
    neighbour_ids,
    live_counts,
    entry_rows,
    enc_gain,
    enc_qkv,
    enc_out,
    final_gain,
    kv_weight,
):
    shards = lax.axis_size("db")
    per_shard = database.shape[1]
    head_size = enc_qkv.shape[3]
    score_scale = 3.0 / math.sqrt(head_size)
    weights_all = lax.all_gather(enc_qkv, GROUP, axis=0, tiled=False)
    wanted = neighbour_ids.reshape(-1)
    requests = wanted.shape[0]
    capacity = max(2, (requests + shards - 1) // shards)
    located = jnp.take(entry_rows, wanted)
    holder = located // per_shard
    within = located % per_shard
    ordinal = jnp.arange(requests)
    before = (holder[:, None] == holder[None, :]) & (ordinal[None, :] < ordinal[:, None])
    standing = jnp.sum(before.astype(jnp.int32), axis=1)
    target = holder * capacity + standing
    buckets = jnp.arange(shards * capacity)
    matched = (target[None, :] == buckets[:, None]).astype(jnp.int32)
    outgoing = jnp.sum(matched * within[None, :], axis=1).reshape(shards, capacity)
    indices = lax.all_to_all(outgoing, "db", split_axis=0, concat_axis=0, tiled=True)
    by_row = database.transpose(1, 0, 2)
    picked = by_row[indices.reshape(-1)]
    fetched = lax.all_to_all(picked, "db", split_axis=0, concat_axis=0, tiled=True)
    rows = fetched[target]
    mine = lax.all_to_all(rows, GROUP, split_axis=0, concat_axis=2, tiled=True)
    hidden = mine.astype(jnp.float32)
    for layer_index in range(enc_qkv.shape[0]):
        normed = (unit_heads(hidden) * enc_gain[layer_index]).astype(jnp.bfloat16)
        mixture = jnp.einsum(
            "rpe,heta->trhpa", normed, weights_all[:, layer_index], preferred_element_type=jnp.float32
        )
        query = unit_heads(mixture[0]).astype(jnp.bfloat16)
        key = unit_heads(mixture[1]).astype(jnp.bfloat16)
        value = mixture[2].astype(jnp.bfloat16)
        scores = (
            jnp.einsum("rhpa,rhsa->rhps", query, key, preferred_element_type=jnp.float32)
            * score_scale
        )
        weights = jnp.exp(scores)
        shares = (weights / jnp.sum(weights, axis=3, keepdims=True)).astype(jnp.bfloat16)
        attended = jnp.einsum(
            "rhps,rhsa->rpha", shares, value, preferred_element_type=jnp.float32
        ).astype(jnp.bfloat16)
        hidden = hidden + jnp.einsum(
            "rpf,fe->rpe",
            attended.reshape(hidden.shape),
            enc_out[layer_index],
            preferred_element_type=jnp.float32,
        )
    encoded = (unit_heads(hidden) * final_gain).astype(jnp.bfloat16)
    gathered = lax.all_gather(encoded, GROUP, axis=0, tiled=True)
    heads_local = kv_weight.shape[2] // head_size
    tokens, features = queries.shape
    block_total = live_counts.shape[0]
    neighbours = neighbour_ids.shape[1]
    positions = gathered.shape[1]
    flat = gathered.reshape(block_total, neighbours * positions, gathered.shape[2])
    weight_heads = kv_weight.reshape(kv_weight.shape[0], 2, heads_local, head_size)
    mixture = jnp.einsum(
        "cse,ethd->tchsd", flat, weight_heads, preferred_element_type=jnp.float32
    )
    key_heads = unit_heads(mixture[0]).astype(jnp.bfloat16)
    value_heads = mixture[1].astype(jnp.bfloat16)
    query_heads = unit_heads(
        queries.reshape(tokens, heads_local, head_size).astype(jnp.float32)
    ).astype(jnp.bfloat16)
    padding = jnp.zeros((BL - 1, heads_local, head_size), jnp.bfloat16)
    shifted = (
        jnp.concatenate([query_heads[BL - 1 :], padding], axis=0)
        .reshape(block_total, BL, heads_local, head_size)
        .transpose(0, 2, 1, 3)
    )
    scores = (
        jnp.einsum("chqa,chsa->chqs", shifted, key_heads, preferred_element_type=jnp.float32)
        * score_scale
    )
    slot = jnp.arange(neighbours * positions) // positions
    live_mask = (slot[None, :] < live_counts[:, None]).astype(jnp.float32)
    weights = jnp.exp(scores) * live_mask[:, None, None, :]
    shares = (weights / jnp.sum(weights, axis=3, keepdims=True)).astype(jnp.bfloat16)
    mixture = jnp.einsum(
        "chqs,chsa->cqha", shares, value_heads, preferred_element_type=jnp.float32
    ).reshape(tokens, features)
    front = jnp.zeros((BL - 1, features), jnp.float32)
    return jnp.concatenate([front, mixture[: tokens - BL + 1]], axis=0).astype(jnp.bfloat16)


def solution(mesh):
    return jax.shard_map(
        on_device,
        mesh=mesh,
        in_specs=(
            P("db", GROUP),
            P(None, "db", GROUP),
            P("db", None),
            P("db"),
            P(),
            P(),
            P(None, None, None, GROUP),
            P(),
            P(),
            P(None, None, GROUP),
        ),
        out_specs=P("db", GROUP),
        check_vma=False,
    )
```

```python
import functools
import math

import jax
import jax.numpy as jnp
from jax import lax
from jax.experimental import pallas as pl
from jax.experimental.pallas import tpu as pltpu
from jax.sharding import PartitionSpec as P

BL = 64
GROUP = ("mp", "section")
MESH = pl.DeviceIdType.MESH
VMEM = pl.BlockSpec(memory_space=pltpu.VMEM)
SMEM = pl.BlockSpec(memory_space=pltpu.SMEM)
ANY = pl.BlockSpec(memory_space=pl.ANY)


def unit(tensor):
    return tensor * lax.rsqrt(jnp.mean(tensor * tensor, axis=-1, keepdims=True) + 1e-06)


def remote(src, dst, send_sem, recv_sem, device):
    return pltpu.make_async_remote_copy(
        src_ref=src,
        dst_ref=dst,
        send_sem=send_sem,
        recv_sem=recv_sem,
        device_id=device,
        device_id_type=MESH,
    )


def fetch_kernel(
    shards,
    group,
    cap,
    ask_ref,
    target_ref,
    base_ref,
    out_ref,
    asked,
    asked_s,
    send,
    recv,
    rows,
    ask_send,
    ask_recv,
    row_send,
    row_recv,
    part_send,
    part_recv,
    local_sem,
):
    me = lax.axis_index("db")
    sections = 2
    lane = lax.axis_index("mp") * sections + lax.axis_index("section")

    def db_at(k):
        return {"db": lax.rem(me + k, shards)}

    def group_at(k):
        other = lax.rem(lane + k, group)
        return other, {"mp": other // sections, "section": lax.rem(other, sections)}

    barrier = pltpu.get_barrier_semaphore()

    def greet_db(k, carry):
        pl.semaphore_signal(barrier, inc=1, device_id=db_at(k), device_id_type=MESH)
        return carry

    def greet_group(k, carry):
        pl.semaphore_signal(barrier, inc=1, device_id=group_at(k)[1], device_id_type=MESH)
        return carry

    lax.fori_loop(1, shards, greet_db, 0)
    lax.fori_loop(1, group, greet_group, 0)
    pl.semaphore_wait(barrier, shards + group - 2)

    def ask(k):
        other = lax.rem(me + k, shards)
        return remote(ask_ref.at[other], asked.at[me], ask_send.at[k], ask_recv.at[k], db_at(k))

    def ask_start(k, carry):
        ask(k).start()
        return carry

    lax.fori_loop(1, shards, ask_start, 0)
    asked[pl.ds(me, 1)] = ask_ref[pl.ds(me, 1)]

    def ask_wait(k, carry):
        ask(k).wait()
        return carry

    lax.fori_loop(1, shards, ask_wait, 0)
    to_scalar = pltpu.make_async_copy(asked, asked_s, local_sem)
    to_scalar.start()
    to_scalar.wait()

    def give(k):
        other = lax.rem(me + k, shards)
        return remote(send.at[other], recv.at[me], row_send.at[k], row_recv.at[k], db_at(k))

    def pick(k, carry):
        other = lax.rem(me + k, shards)
        for slot in range(cap):
            send[other, slot] = base_ref[asked_s[other, 0, slot]]
        give(k).start()
        return carry

    lax.fori_loop(1, shards, pick, 0)
    for slot in range(cap):
        recv[me, slot] = base_ref[asked_s[me, 0, slot]]

    def give_wait(k, carry):
        give(k).wait()
        return carry

    lax.fori_loop(1, shards, give_wait, 0)

    per = rows.shape[1]

    def part(k):
        other, device = group_at(k)
        return remote(rows.at[other], out_ref.at[lane], part_send.at[k], part_recv.at[k], device)

    def choose(k, carry):
        other = lax.rem(lane + k, group)
        for slot in range(per):
            place = target_ref[other * per + slot]
            rows[other, slot] = recv[place // cap, lax.rem(place, cap)]
        part(k).start()
        return carry

    lax.fori_loop(1, group, choose, 0)
    for slot in range(per):
        place = target_ref[lane * per + slot]
        out_ref[lane, slot] = recv[place // cap, lax.rem(place, cap)]

    def part_wait(k, carry):
        part(k).wait()
        return carry

    lax.fori_loop(1, group, part_wait, 0)


def fetch(shards, group, cap, ask, target, base):
    per_shard, positions, width = base.shape
    per = target.shape[0] // group
    return pl.pallas_call(
        functools.partial(fetch_kernel, shards, group, cap),
        out_shape=jax.ShapeDtypeStruct((group, per, positions, width), base.dtype),
        in_specs=[VMEM, SMEM, VMEM],
        out_specs=VMEM,
        scratch_shapes=[
            pltpu.VMEM((shards, 1, 128), jnp.int32),
            pltpu.SMEM((shards, 1, 128), jnp.int32),
            pltpu.VMEM((shards, cap, positions, width), base.dtype),
            pltpu.VMEM((shards, cap, positions, width), base.dtype),
            pltpu.VMEM((group, per, positions, width), base.dtype),
            pltpu.SemaphoreType.DMA((shards,)),
            pltpu.SemaphoreType.DMA((shards,)),
            pltpu.SemaphoreType.DMA((shards,)),
            pltpu.SemaphoreType.DMA((shards,)),
            pltpu.SemaphoreType.DMA((group,)),
            pltpu.SemaphoreType.DMA((group,)),
            pltpu.SemaphoreType.DMA,
        ],
        compiler_params=pltpu.CompilerParams(
            collective_id=0, has_side_effects=True, vmem_limit_bytes=24 * 2**20
        ),
    )(ask, target, base)


def decode_kernel(
    group,
    scale,
    x_ref,
    live_ref,
    gain_ref,
    final_ref,
    query_ref,
    qkv0_hbm,
    qkv1_hbm,
    out_hbm,
    kv_hbm,
    mix_ref,
    qkv,
    wout,
    kv,
    hidden,
    normed,
    attended,
    queries,
    chunks,
    w_sem,
    o_sem,
    kv_sem,
    send_sem,
    recv_sem,
):
    sections = 2
    chips = group // sections
    y = lax.axis_index("mp")
    c = lax.axis_index("section")
    me = y * sections + c
    up, down, far = lax.rem(y + 1, chips), lax.rem(y + chips - 1, chips), lax.rem(y + 2, chips)
    to_up, to_down, to_twin = {"mp": up}, {"mp": down}, {"section": 1 - c}

    barrier = pltpu.get_barrier_semaphore()
    for device in (to_up, to_down, to_twin):
        pl.semaphore_signal(barrier, inc=1, device_id=device, device_id_type=MESH)

    layers = gain_ref.shape[0]
    head = x_ref.shape[3]
    per, positions = x_ref.shape[1], x_ref.shape[2]
    count = per * positions
    triple = 3 * head

    def weight_copy(source, layer, h):
        return pltpu.make_async_copy(
            source.at[h],
            qkv.at[layer, :, pl.ds(h * triple, triple)],
            w_sem.at[layer, h],
        )

    for h in range(group):
        weight_copy(qkv0_hbm, 0, h).start()
    out_copies = [
        pltpu.make_async_copy(out_hbm.at[layer], wout.at[layer], o_sem.at[layer])
        for layer in range(layers)
    ]
    out_copies[0].start()
    for h in range(group):
        weight_copy(qkv1_hbm, 1, h).start()
    out_copies[1].start()
    kv_copy = pltpu.make_async_copy(kv_hbm, kv, kv_sem)
    kv_copy.start()

    for source in range(group):
        for slot in range(per):
            hidden[pl.ds(slot * positions, positions), pl.ds(source * head, head)] = x_ref[
                source, slot
            ].astype(jnp.float32)

    for layer in range(layers):
        normed[...] = (unit(hidden[...]) * gain_ref[pl.ds(layer, 1)]).astype(jnp.bfloat16)
        for h in range(group):
            weight_copy((qkv0_hbm, qkv1_hbm)[layer], layer, h).wait()

        def heads(p, carry, layer=layer):
            start = pl.multiple_of(p * 2 * triple, 2 * triple)
            mixture = jnp.dot(
                normed[...],
                qkv[layer, :, pl.ds(start, 2 * triple)],
                preferred_element_type=jnp.float32,
            )
            for h in range(2):
                at = h * triple
                query = unit(mixture[:, at : at + head]).astype(jnp.bfloat16)
                key = unit(mixture[:, at + head : at + 2 * head]).astype(jnp.bfloat16)
                value = mixture[:, at + 2 * head : at + 3 * head].astype(jnp.bfloat16)
                for slot in range(per):
                    lo, hi = slot * positions, (slot + 1) * positions
                    scores = lax.dot_general(
                        query[lo:hi],
                        key[lo:hi],
                        (((1,), (1,)), ((), ())),
                        preferred_element_type=jnp.float32,
                    )
                    weights = jnp.exp(scores * scale)
                    shares = weights / jnp.sum(weights, axis=-1, keepdims=True)
                    attended[pl.ds(lo, positions), pl.ds(pl.multiple_of((p * 2 + h) * head, head), head)] = jnp.dot(
                        shares.astype(jnp.bfloat16), value[lo:hi], preferred_element_type=jnp.float32
                    ).astype(jnp.bfloat16)
            return carry

        lax.fori_loop(0, group // 2, heads, 0)
        out_copies[layer].wait()

        def project(t, carry, layer=layer):
            at = pl.multiple_of(t * 256, 256)
            hidden[:, pl.ds(at, 256)] += jnp.dot(
                attended[...], wout[layer, :, pl.ds(at, 256)], preferred_element_type=jnp.float32
            )
            return carry

        lax.fori_loop(0, hidden.shape[1] // 256, project, 0)

    chunks[me] = (unit(hidden[...]) * final_ref[...]).astype(jnp.bfloat16)
    half = count // 2
    pl.semaphore_wait(barrier, 3)

    def move(number, chunk, piece, device):
        place = chunks.at[chunk, pl.ds(piece * half, half)]
        return remote(place, place, send_sem.at[number], recv_sem.at[chunk, piece], device)

    def arrived(chunk, piece):
        place = chunks.at[chunk, pl.ds(piece * half, half)]
        remote(place, place, send_sem.at[0], recv_sem.at[chunk, piece], to_twin).wait_recv()

    sent = []

    def ship(chunk, piece, device):
        copy = move(len(sent), chunk, piece, device)
        copy.start()
        sent.append(copy)

    mine_up, mine_down, mine_far = up * sections + c, down * sections + c, far * sections + c
    twin = 1 - c
    for piece in range(2):
        ship(me, piece, to_up)
        ship(me, 1 - piece, to_down)
    ship(me, 0, to_twin)
    ship(me, 1, to_twin)

    blocks = live_ref.shape[0]
    queries[...] = query_ref[...]
    heads_local = query_ref.shape[1] // head
    kv_copy.wait()
    width = kv.shape[1] // 2

    def cross(chunk):
        alive = (live_ref[chunk] > 1).astype(jnp.float32)

        def pair(p, carry):
            at = pl.multiple_of(p * 2 * head, 2 * head)
            keys = jnp.dot(
                chunks[chunk], kv[:, pl.ds(at, 2 * head)], preferred_element_type=jnp.float32
            )
            values = jnp.dot(
                chunks[chunk],
                kv[:, pl.ds(pl.multiple_of(width + at, 2 * head), 2 * head)],
                preferred_element_type=jnp.float32,
            ).astype(jnp.bfloat16)
            for h in range(2):
                lanes = pl.ds(pl.multiple_of(at + h * head, head), head)
                query = unit(queries[pl.ds(pl.multiple_of(chunk * BL, BL), BL), lanes].astype(jnp.float32))
                key = unit(keys[:, h * head : (h + 1) * head]).astype(jnp.bfloat16)
                scores = lax.dot_general(
                    query.astype(jnp.bfloat16),
                    key,
                    (((1,), (1,)), ((), ())),
                    preferred_element_type=jnp.float32,
                )
                weights = jnp.exp(scores * scale)
                first, second = weights[:, :positions], weights[:, positions:] * alive
                total = jnp.sum(first + second, axis=-1, keepdims=True)
                mixed = jnp.dot(
                    (first / total).astype(jnp.bfloat16),
                    values[:positions, h * head : (h + 1) * head],
                    preferred_element_type=jnp.float32,
                ) + jnp.dot(
                    (second / total).astype(jnp.bfloat16),
                    values[positions:, h * head : (h + 1) * head],
                    preferred_element_type=jnp.float32,
                )
                mix_ref[pl.ds(pl.multiple_of(chunk * BL, BL), BL), lanes] = mixed.astype(jnp.bfloat16)
            return carry

        lax.fori_loop(0, heads_local // 2, pair, 0)

    cross(me)
    arrived(y * sections + twin, 0)
    arrived(y * sections + twin, 1)
    cross(y * sections + twin)
    arrived(mine_down, 0)
    ship(mine_down, 0, to_up)
    ship(mine_down, 0, to_twin)
    arrived(mine_up, 1)
    ship(mine_up, 1, to_down)
    ship(mine_up, 1, to_twin)
    arrived(mine_down, 1)
    ship(mine_down, 1, to_twin)
    arrived(mine_up, 0)
    ship(mine_up, 0, to_twin)
    cross(mine_down)
    cross(mine_up)
    arrived(mine_far, 0)
    ship(mine_far, 0, to_twin)
    arrived(mine_far, 1)
    ship(mine_far, 1, to_twin)
    for place in (down, up):
        arrived(place * sections + twin, 0)
        arrived(place * sections + twin, 1)
        cross(place * sections + twin)
    cross(mine_far)
    arrived(far * sections + twin, 0)
    arrived(far * sections + twin, 1)
    cross(far * sections + twin)
    for copy in sent:
        copy.wait_send()


def decode(group, x, live, gain, final, query, qkv0, qkv1, out, kv):
    head = x.shape[3]
    features = out.shape[1]
    count = x.shape[1] * x.shape[2]
    dma = pltpu.SemaphoreType.DMA
    return pl.pallas_call(
        functools.partial(decode_kernel, group, 3.0 / math.sqrt(head)),
        out_shape=jax.ShapeDtypeStruct(query.shape, jnp.bfloat16),
        in_specs=[VMEM, SMEM, VMEM, VMEM, VMEM, ANY, ANY, ANY, ANY],
        out_specs=VMEM,
        scratch_shapes=[
            pltpu.VMEM((2, features, 3 * features), jnp.bfloat16),
            pltpu.VMEM(out.shape, jnp.bfloat16),
            pltpu.VMEM(kv.shape, jnp.bfloat16),
            pltpu.VMEM((count, features), jnp.float32),
            pltpu.VMEM((count, features), jnp.bfloat16),
            pltpu.VMEM((count, features), jnp.bfloat16),
            pltpu.VMEM(query.shape, jnp.bfloat16),
            pltpu.VMEM((group, count, features), jnp.bfloat16),
            dma((2, group)),
            dma((2,)),
            dma,
            dma((14,)),
            dma((group, 2)),
        ],
        compiler_params=pltpu.CompilerParams(
            collective_id=1, has_side_effects=True, vmem_limit_bytes=52 * 2**20
        ),
    )(x, live, gain, final, query, qkv0, qkv1, out, kv)


def on_device(
    queries,
    database,
    neighbour_ids,
    live_counts,
    entry_rows,
    enc_gain,
    enc_qkv,
    enc_out,
    final_gain,
    kv_weight,
):
    shards = lax.axis_size("db")
    group = lax.axis_size(GROUP)
    per_shard = database.shape[1]
    layers, features, _, head_size = enc_qkv.shape
    own = enc_qkv.reshape(layers, features, 3 * head_size)
    qkv0 = lax.all_gather(own[0], GROUP, axis=0, tiled=False)
    qkv1 = lax.all_gather(own[1], GROUP, axis=0, tiled=False)
    wanted = neighbour_ids.reshape(-1)
    requests = wanted.shape[0]
    capacity = max(2, (requests + shards - 1) // shards)
    located = jnp.take(entry_rows, wanted)
    holder = located // per_shard
    within = located % per_shard
    ordinal = jnp.arange(requests)
    before = (holder[:, None] == holder[None, :]) & (ordinal[None, :] < ordinal[:, None])
    standing = jnp.sum(before.astype(jnp.int32), axis=1)
    target = holder * capacity + standing
    buckets = jnp.arange(shards)[:, None] * capacity + jnp.arange(128)[None, :]
    inside = jnp.arange(128)[None, :, None] < capacity
    matched = ((target[None, None, :] == buckets[:, :, None]) & inside).astype(jnp.int32)
    outgoing = jnp.sum(matched * within[None, None, :], axis=2).reshape(shards, 1, 128)
    by_row = database.transpose(1, 0, 2)
    x = fetch(shards, group, capacity, outgoing, target, by_row)

    tokens, width = queries.shape
    shifted = jnp.concatenate(
        [queries[BL - 1 :], jnp.zeros((BL - 1, width), queries.dtype)], axis=0
    )
    kv = kv_weight.reshape(kv_weight.shape[0], -1)
    mixed = decode(
        group,
        x,
        live_counts,
        enc_gain,
        final_gain.reshape(1, -1),
        shifted,
        qkv0,
        qkv1,
        enc_out,
        kv,
    )
    front = jnp.zeros((BL - 1, width), mixed.dtype)
    return jnp.concatenate([front, mixed[: tokens - BL + 1]], axis=0)


def solution(mesh):
    return jax.shard_map(
        on_device,
        mesh=mesh,
        in_specs=(
            P("db", GROUP),
            P(None, "db", GROUP),
            P("db", None),
            P("db"),
            P(),
            P(),
            P(None, None, None, GROUP),
            P(),
            P(),
            P(None, None, GROUP),
        ),
        out_specs=P("db", GROUP),
        check_vma=False,
    )
```

```python
import functools
import math

import jax
import jax.numpy as jnp
from jax import lax
from jax.experimental import pallas as pl
from jax.experimental.pallas import tpu as pltpu
from jax.sharding import PartitionSpec as P

BL = 64
GROUP = ("mp", "section")
MESH = pl.DeviceIdType.MESH
VMEM = pl.BlockSpec(memory_space=pltpu.VMEM)
SMEM = pl.BlockSpec(memory_space=pltpu.SMEM)
ANY = pl.BlockSpec(memory_space=pl.ANY)


def unit(tensor):
    return tensor * lax.rsqrt(jnp.mean(tensor * tensor, axis=-1, keepdims=True) + 1e-06)


def remote(src, dst, send_sem, recv_sem, device):
    return pltpu.make_async_remote_copy(
        src_ref=src,
        dst_ref=dst,
        send_sem=send_sem,
        recv_sem=recv_sem,
        device_id=device,
        device_id_type=MESH,
    )


def kernel(
    shards,
    group,
    cap,
    scale,
    ask_ref,
    target_ref,
    base_ref,
    live_ref,
    gain_ref,
    final_ref,
    query_ref,
    own_hbm,
    out_hbm,
    kv_hbm,
    mix_ref,
    asked,
    asked_s,
    send,
    recv,
    rows,
    parts,
    wall,
    wout,
    kv,
    hidden,
    normed,
    attended,
    stage,
    queries,
    chunks,
    ask_send,
    ask_recv,
    row_send,
    row_recv,
    part_send,
    part_recv,
    asked_sem,
    own_sem,
    out_sem,
    kv_sem,
    wall_send,
    wall_recv,
    chunk_send,
    chunk_recv,
):
    sections = 2
    chips = group // sections
    db = lax.axis_index("db")
    y = lax.axis_index("mp")
    c = lax.axis_index("section")
    me = y * sections + c
    up, down, far = lax.rem(y + 1, chips), lax.rem(y + chips - 1, chips), lax.rem(y + 2, chips)
    to_up, to_down, to_twin = {"mp": up}, {"mp": down}, {"section": 1 - c}
    at_up, at_down, at_far = up * sections + c, down * sections + c, far * sections + c
    at_twin = y * sections + 1 - c
    up_twin, down_twin, far_twin = (place * sections + 1 - c for place in (up, down, far))

    layers, features = gain_ref.shape
    positions, head = base_ref.shape[1], base_ref.shape[2]
    per = rows.shape[1]
    pair = 2 * head
    blocks = live_ref.shape[0]

    own_copies = [
        pltpu.make_async_copy(
            own_hbm.at[layer],
            wall.at[layer, :, :, pl.ds(pl.multiple_of(me * head, head), head)],
            own_sem.at[layer],
        )
        for layer in range(layers)
    ]
    out_copy = pltpu.make_async_copy(out_hbm, wout, out_sem)
    kv_copy = pltpu.make_async_copy(kv_hbm, kv, kv_sem)

    def db_at(k):
        return {"db": lax.rem(db + k, shards)}

    def group_at(k):
        other = lax.rem(me + k, group)
        return other, {"mp": other // sections, "section": lax.rem(other, sections)}

    barrier = pltpu.get_barrier_semaphore()

    def greet_db(k, carry):
        pl.semaphore_signal(barrier, inc=1, device_id=db_at(k), device_id_type=MESH)
        return carry

    def greet_group(k, carry):
        pl.semaphore_signal(barrier, inc=1, device_id=group_at(k)[1], device_id_type=MESH)
        return carry

    lax.fori_loop(1, shards, greet_db, 0)
    lax.fori_loop(1, group, greet_group, 0)
    for copy in own_copies + [out_copy, kv_copy]:
        copy.start()
    pl.semaphore_wait(barrier, shards + group - 2)

    def ask(k):
        other = lax.rem(db + k, shards)
        return remote(ask_ref.at[other], asked.at[db], ask_send.at[k], ask_recv.at[k], db_at(k))

    def ask_start(k, carry):
        ask(k).start()
        return carry

    lax.fori_loop(1, shards, ask_start, 0)
    asked[pl.ds(db, 1)] = ask_ref[pl.ds(db, 1)]

    half_rows = features // 2

    def wall_place(layer, chunk, piece):
        return wall.at[
            layer,
            :,
            pl.ds(piece * half_rows, half_rows),
            pl.ds(pl.multiple_of(chunk * head, head), head),
        ]

    def wall_ship(number, layer, chunk, piece, device, own=False):
        place = wall_place(layer, chunk, piece)
        source = own_hbm.at[layer, :, pl.ds(piece * half_rows, half_rows), :] if own else place
        copy = remote(
            source, place, wall_send.at[layer, number], wall_recv.at[layer, chunk, piece], device
        )
        copy.start()
        return copy

    def wall_arrived(layer, chunk, piece):
        place = wall_place(layer, chunk, piece)
        remote(
            place, place, wall_send.at[layer, 0], wall_recv.at[layer, chunk, piece], to_twin
        ).wait_recv()

    sent = []

    def wall_own(layer):
        for piece in range(2):
            sent.append(wall_ship(piece, layer, me, piece, to_up, True))
            sent.append(wall_ship(2 + piece, layer, me, 1 - piece, to_down, True))
        for piece in range(2):
            sent.append(wall_ship(4 + piece, layer, me, piece, to_twin, True))

    def wall_near(layer):
        wall_arrived(layer, at_down, 0)
        sent.append(wall_ship(6, layer, at_down, 0, to_up))
        sent.append(wall_ship(7, layer, at_down, 0, to_twin))
        wall_arrived(layer, at_up, 1)
        sent.append(wall_ship(8, layer, at_up, 1, to_down))
        sent.append(wall_ship(9, layer, at_up, 1, to_twin))
        wall_arrived(layer, at_down, 1)
        sent.append(wall_ship(10, layer, at_down, 1, to_twin))
        wall_arrived(layer, at_up, 0)
        sent.append(wall_ship(11, layer, at_up, 0, to_twin))

    def wall_far(layer):
        for piece in range(2):
            wall_arrived(layer, at_far, piece)
            sent.append(wall_ship(12 + piece, layer, at_far, piece, to_twin))

    def ask_wait(k, carry):
        ask(k).wait()
        return carry

    lax.fori_loop(1, shards, ask_wait, 0)
    to_scalar = pltpu.make_async_copy(asked, asked_s, asked_sem)
    to_scalar.start()
    to_scalar.wait()

    def give(k):
        other = lax.rem(db + k, shards)
        return remote(send.at[other], recv.at[db], row_send.at[k], row_recv.at[k], db_at(k))

    def pick(k, carry):
        other = lax.rem(db + k, shards)
        for slot in range(cap):
            send[other, slot] = base_ref[asked_s[other, 0, slot]]
        give(k).start()
        return carry

    lax.fori_loop(1, shards, pick, 0)
    for slot in range(cap):
        recv[db, slot] = base_ref[asked_s[db, 0, slot]]

    wall_own(0)

    heads_local = query_ref.shape[1] // head
    tokens = query_ref.shape[0]

    def prepare(h, carry):
        lanes = pl.ds(pl.multiple_of(h * head, head), head)
        stage[pl.ds(0, tokens)] = unit(query_ref[:, lanes].astype(jnp.float32)) * scale
        stage[pl.ds(tokens, BL)] = jnp.zeros((BL, head), jnp.float32)
        queries[:, lanes] = stage[pl.ds(BL - 1, tokens)].astype(jnp.bfloat16)
        return carry

    lax.fori_loop(0, heads_local, prepare, 0)

    wall_near(0)
    wall_own(1)
    wall_far(0)
    wall_near(1)
    wall_far(1)

    def give_wait(k, carry):
        give(k).wait()
        return carry

    lax.fori_loop(1, shards, give_wait, 0)

    def part(k):
        other, device = group_at(k)
        return remote(rows.at[other], parts.at[me], part_send.at[k], part_recv.at[k], device)

    def choose(k, carry):
        other = lax.rem(me + k, group)
        for slot in range(per):
            place = target_ref[other * per + slot]
            rows[other, slot] = recv[place // cap, lax.rem(place, cap)]
        part(k).start()
        return carry

    lax.fori_loop(1, group, choose, 0)
    for slot in range(per):
        place = target_ref[me * per + slot]
        parts[me, slot] = recv[place // cap, lax.rem(place, cap)]

    def part_wait(k, carry):
        part(k).wait()
        return carry

    lax.fori_loop(1, group, part_wait, 0)

    for source in range(group):
        for slot in range(per):
            hidden[pl.ds(slot * positions, positions), pl.ds(source * head, head)] = parts[
                source, slot
            ].astype(jnp.float32)

    same = lax.broadcasted_iota(jnp.int32, (pair, pair), 0) // head == (
        lax.broadcasted_iota(jnp.int32, (pair, pair), 1) // head
    )
    average = jnp.where(same, 1.0 / head, 0.0).astype(jnp.bfloat16)
    ones = jnp.ones((positions, head), jnp.bfloat16)

    def unit_pair(tensor):
        square = (tensor * tensor).astype(jnp.bfloat16)
        return tensor * lax.rsqrt(
            jnp.dot(square, average, preferred_element_type=jnp.float32) + 1e-06
        )

    def product(left, right):
        return jnp.dot(left, right, preferred_element_type=jnp.float32)

    def against(left, right):
        return lax.dot_general(
            left, right, (((1,), (1,)), ((), ())), preferred_element_type=jnp.float32
        )

    out_copy.wait()
    for layer in range(layers):
        own_copies[layer].wait()
        for chunk in (at_twin, up_twin, down_twin, far_twin):
            for piece in range(2):
                wall_arrived(layer, chunk, piece)

    def encode(layer, carry):
        normed[...] = (unit(hidden[...]) * gain_ref[pl.ds(layer, 1)]).astype(jnp.bfloat16)
        for p in range(group // 2):
            lanes = pl.ds(p * pair, pair)
            query = unit_pair(product(normed[...], wall[layer, 0, :, lanes])) * scale
            key = unit_pair(product(normed[...], wall[layer, 1, :, lanes])).astype(jnp.bfloat16)
            value = product(normed[...], wall[layer, 2, :, lanes]).astype(jnp.bfloat16)
            query = query.astype(jnp.bfloat16)
            for h in range(2):
                here = slice(h * head, (h + 1) * head)
                for slot in range(per):
                    span = slice(slot * positions, (slot + 1) * positions)
                    weights = jnp.exp2(against(query[span, here], key[span, here]))
                    mixed = product(
                        weights.astype(jnp.bfloat16),
                        jnp.concatenate([value[span, here], ones], axis=1),
                    )
                    attended[
                        pl.ds(slot * positions, positions), pl.ds(p * pair + h * head, head)
                    ] = (mixed[:, :head] / mixed[:, head:]).astype(jnp.bfloat16)
        for t in range(features // 256):
            lanes = pl.ds(t * 256, 256)
            hidden[:, lanes] += product(attended[...], wout[layer, :, lanes])
        return carry

    lax.fori_loop(0, layers, encode, 0)
    chunks[me] = (unit(hidden[...]) * final_ref[...]).astype(jnp.bfloat16)
    half = chunks.shape[1] // 2

    def ship(number, chunk, piece, device):
        place = chunks.at[chunk, pl.ds(piece * half, half)]
        remote(place, place, chunk_send.at[number], chunk_recv.at[chunk, piece], device).start()

    def arrived(chunk, piece):
        place = chunks.at[chunk, pl.ds(piece * half, half)]
        remote(
            place, place, chunk_send.at[0], chunk_recv.at[chunk, piece], to_twin
        ).wait_recv()

    for piece in range(2):
        ship(piece, me, piece, to_up)
        ship(2 + piece, me, 1 - piece, to_down)
    for piece in range(2):
        ship(4 + piece, me, piece, to_twin)
    kv_copy.wait()

    def cross(step, carry):
        @pl.when(step == 1)
        def _():
            for piece in range(2):
                arrived(at_twin, piece)

        @pl.when(step == 2)
        def _():
            arrived(at_down, 0)
            ship(6, at_down, 0, to_up)
            ship(7, at_down, 0, to_twin)
            arrived(at_up, 1)
            ship(8, at_up, 1, to_down)
            ship(9, at_up, 1, to_twin)
            arrived(at_down, 1)
            ship(10, at_down, 1, to_twin)

        @pl.when(step == 3)
        def _():
            arrived(at_up, 0)
            ship(11, at_up, 0, to_twin)

        @pl.when(step == 4)
        def _():
            for piece in range(2):
                arrived(down_twin, piece)

        @pl.when(step == 5)
        def _():
            for piece in range(2):
                arrived(up_twin, piece)

        @pl.when(step == 6)
        def _():
            for piece in range(2):
                arrived(at_far, piece)
                ship(12 + piece, at_far, piece, to_twin)

        @pl.when(step == 7)
        def _():
            for piece in range(2):
                arrived(far_twin, piece)

        chunk = at_far
        for number, place in enumerate(
            (me, at_twin, at_down, at_up, down_twin, up_twin, at_far, far_twin)
        ):
            chunk = jnp.where(step == number, place, chunk)
        alive = (live_ref[chunk] > 1).astype(jnp.float32)
        span = pl.ds(pl.multiple_of(chunk * BL, BL), BL)
        for p in range(heads_local // 2):
            lanes = pl.ds(p * pair, pair)
            key = unit_pair(product(chunks[chunk], kv[0, :, lanes])).astype(jnp.bfloat16)
            value = product(chunks[chunk], kv[1, :, lanes]).astype(jnp.bfloat16)
            for h in range(2):
                here = slice(h * head, (h + 1) * head)
                weights = jnp.exp2(
                    against(queries[span, pl.ds(p * pair + h * head, head)], key[:, here])
                )
                weights = jnp.concatenate(
                    [weights[:, :positions], weights[:, positions:] * alive], axis=1
                ).astype(jnp.bfloat16)
                mixed = product(
                    weights,
                    jnp.concatenate(
                        [value[:, here], jnp.concatenate([ones, ones], axis=0)], axis=1
                    ),
                )
                mix_ref[span, pl.ds(p * pair + h * head, head)] = (
                    mixed[:, :head] / mixed[:, head:]
                ).astype(jnp.bfloat16)
        return carry

    lax.fori_loop(0, blocks, cross, 0)
    for number in range(14):
        place = chunks.at[me, pl.ds(0, half)]
        remote(place, place, chunk_send.at[number], chunk_recv.at[me, 0], to_twin).wait_send()
    for copy in sent:
        copy.wait_send()


def retrieve(shards, group, cap, ask, target, base, live, gain, final, query, own, out, kv):
    _, positions, head = base.shape
    layers, features = gain.shape
    per = target.shape[0] // group
    tokens = query.shape[0]
    dma = pltpu.SemaphoreType.DMA
    bf16, f32 = jnp.bfloat16, jnp.float32
    return pl.pallas_call(
        functools.partial(kernel, shards, group, cap, 3.0 / math.sqrt(head) * math.log2(math.e)),
        out_shape=jax.ShapeDtypeStruct(query.shape, bf16),
        in_specs=[VMEM, SMEM, VMEM, SMEM, VMEM, VMEM, VMEM, ANY, ANY, ANY],
        out_specs=VMEM,
        scratch_shapes=[
            pltpu.VMEM((shards, 1, 128), jnp.int32),
            pltpu.SMEM((shards, 1, 128), jnp.int32),
            pltpu.VMEM((shards, cap, positions, head), bf16),
            pltpu.VMEM((shards, cap, positions, head), bf16),
            pltpu.VMEM((group, per, positions, head), bf16),
            pltpu.VMEM((group, per, positions, head), bf16),
            pltpu.VMEM((layers, 3, features, features), bf16),
            pltpu.VMEM(out.shape, bf16),
            pltpu.VMEM(kv.shape, bf16),
            pltpu.VMEM((per * positions, features), f32),
            pltpu.VMEM((per * positions, features), bf16),
            pltpu.VMEM((per * positions, features), bf16),
            pltpu.VMEM((tokens + BL, head), f32),
            pltpu.VMEM(query.shape, bf16),
            pltpu.VMEM((group, per * positions, features), bf16),
            dma((shards,)),
            dma((shards,)),
            dma((shards,)),
            dma((shards,)),
            dma((group,)),
            dma((group,)),
            dma,
            dma((layers,)),
            dma,
            dma,
            dma((layers, 14)),
            dma((layers, group, 2)),
            dma((14,)),
            dma((group, 2)),
        ],
        compiler_params=pltpu.CompilerParams(
            collective_id=0, has_side_effects=True, vmem_limit_bytes=52 * 2**20
        ),
    )(ask, target, base, live, gain, final, query, own, out, kv)


def on_device(
    queries,
    database,
    neighbour_ids,
    live_counts,
    entry_rows,
    enc_gain,
    enc_qkv,
    enc_out,
    final_gain,
    kv_weight,
):
    shards = lax.axis_size("db")
    group = lax.axis_size(GROUP)
    per_shard = database.shape[1]
    wanted = neighbour_ids.reshape(-1)
    requests = wanted.shape[0]
    capacity = max(2, (requests + shards - 1) // shards)
    located = jnp.take(entry_rows, wanted)
    holder = located // per_shard
    within = located % per_shard
    ordinal = jnp.arange(requests)
    before = (holder[:, None] == holder[None, :]) & (ordinal[None, :] < ordinal[:, None])
    standing = jnp.sum(before.astype(jnp.int32), axis=1)
    target = holder * capacity + standing
    buckets = jnp.arange(shards)[:, None] * capacity + jnp.arange(128)[None, :]
    inside = jnp.arange(128)[None, :, None] < capacity
    matched = ((target[None, None, :] == buckets[:, :, None]) & inside).astype(jnp.int32)
    outgoing = jnp.sum(matched * within[None, None, :], axis=2).reshape(shards, 1, 128)
    by_row = database.transpose(1, 0, 2)
    mixed = retrieve(
        shards,
        group,
        capacity,
        outgoing,
        target,
        by_row,
        live_counts,
        enc_gain,
        final_gain.reshape(1, -1),
        queries,
        enc_qkv.transpose(0, 2, 1, 3),
        enc_out,
        kv_weight.transpose(1, 0, 2),
    )
    tokens, width = queries.shape
    front = jnp.zeros((BL - 1, width), mixed.dtype)
    return jnp.concatenate([front, mixed[: tokens - BL + 1]], axis=0)


def solution(mesh):
    return jax.shard_map(
        on_device,
        mesh=mesh,
        in_specs=(
            P("db", GROUP),
            P(None, "db", GROUP),
            P("db", None),
            P("db"),
            P(),
            P(),
            P(None, None, None, GROUP),
            P(),
            P(),
            P(None, None, GROUP),
        ),
        out_specs=P("db", GROUP),
        check_vma=False,
    )
```

```python
import functools
import math

import jax
import jax.numpy as jnp
from jax import lax
from jax.experimental import pallas as pl
from jax.experimental.pallas import tpu as pltpu
from jax.sharding import PartitionSpec as P

BL = 64
GROUP = ("mp", "section")
MESH = pl.DeviceIdType.MESH
VMEM = pl.BlockSpec(memory_space=pltpu.VMEM)
SMEM = pl.BlockSpec(memory_space=pltpu.SMEM)
ANY = pl.BlockSpec(memory_space=pl.ANY)


def unit(tensor):
    return tensor * lax.rsqrt(jnp.mean(tensor * tensor, axis=-1, keepdims=True) + 1e-06)


def remote(src, dst, send_sem, recv_sem, device):
    return pltpu.make_async_remote_copy(
        src_ref=src,
        dst_ref=dst,
        send_sem=send_sem,
        recv_sem=recv_sem,
        device_id=device,
        device_id_type=MESH,
    )


def kernel(
    shards,
    group,
    cap,
    scale,
    ask_ref,
    target_ref,
    data_ref,
    live_ref,
    gain_ref,
    final_ref,
    query_ref,
    own_hbm,
    out_hbm,
    kv_hbm,
    mix_ref,
    base,
    asked,
    asked_s,
    send,
    recv,
    rows,
    parts,
    own_raw,
    own,
    wall,
    wout,
    kv_raw,
    kv,
    hidden,
    normed,
    attended,
    stage,
    queries,
    query_s,
    key_s,
    value_s,
    chunks,
    ask_send,
    ask_recv,
    row_send,
    row_recv,
    part_send,
    part_recv,
    asked_sem,
    own_sem,
    out_sem,
    kv_sem,
    wall_send,
    wall_recv,
    chunk_send,
    chunk_recv,
):
    sections = 2
    chips = group // sections
    db = lax.axis_index("db")
    y = lax.axis_index("mp")
    c = lax.axis_index("section")
    me = y * sections + c
    up, down, far = lax.rem(y + 1, chips), lax.rem(y + chips - 1, chips), lax.rem(y + 2, chips)
    to_up, to_down, to_twin = {"mp": up}, {"mp": down}, {"section": 1 - c}
    at_up, at_down, at_far = up * sections + c, down * sections + c, far * sections + c
    at_twin = y * sections + 1 - c
    up_twin, down_twin, far_twin = (place * sections + 1 - c for place in (up, down, far))

    layers, features = gain_ref.shape
    positions, head = base.shape[1], base.shape[2]
    per = rows.shape[1]
    pair = 2 * head
    blocks = live_ref.shape[0]

    own_copy = pltpu.make_async_copy(own_hbm, own_raw, own_sem)
    out_copy = pltpu.make_async_copy(out_hbm, wout, out_sem)
    kv_copy = pltpu.make_async_copy(kv_hbm, kv_raw, kv_sem)
    for copy in (own_copy, out_copy, kv_copy):
        copy.start()

    def db_at(k):
        return {"db": lax.rem(db + k, shards)}

    def group_at(k):
        other = lax.rem(me + k, group)
        return other, {"mp": other // sections, "section": lax.rem(other, sections)}

    barrier = pltpu.get_barrier_semaphore()

    def greet_db(k, carry):
        pl.semaphore_signal(barrier, inc=1, device_id=db_at(k), device_id_type=MESH)
        return carry

    def greet_group(k, carry):
        pl.semaphore_signal(barrier, inc=1, device_id=group_at(k)[1], device_id_type=MESH)
        return carry

    lax.fori_loop(1, shards, greet_db, 0)
    lax.fori_loop(1, group, greet_group, 0)
    mine = pl.ds(pl.multiple_of(me * head, head), head)
    own_copy.wait()
    for layer in range(layers):
        own[layer] = jnp.transpose(own_raw[layer], (1, 0, 2))
        wall[layer, :, :, mine] = own[layer]
    base[...] = jnp.transpose(data_ref[...], (1, 0, 2))
    pl.semaphore_wait(barrier, shards + group - 2)

    def ask(k):
        other = lax.rem(db + k, shards)
        return remote(ask_ref.at[other], asked.at[db], ask_send.at[k], ask_recv.at[k], db_at(k))

    def ask_start(k, carry):
        ask(k).start()
        return carry

    lax.fori_loop(1, shards, ask_start, 0)
    asked[pl.ds(db, 1)] = ask_ref[pl.ds(db, 1)]

    half_rows = features // 2

    def wall_place(layer, chunk, piece):
        return wall.at[
            layer,
            :,
            pl.ds(piece * half_rows, half_rows),
            pl.ds(pl.multiple_of(chunk * head, head), head),
        ]

    def wall_ship(number, layer, chunk, piece, device, local=False):
        place = wall_place(layer, chunk, piece)
        source = own.at[layer, :, pl.ds(piece * half_rows, half_rows), :] if local else place
        copy = remote(
            source, place, wall_send.at[layer, number], wall_recv.at[layer, chunk, piece], device
        )
        copy.start()
        return copy

    def wall_arrived(layer, chunk, piece):
        place = wall_place(layer, chunk, piece)
        remote(
            place, place, wall_send.at[layer, 0], wall_recv.at[layer, chunk, piece], to_twin
        ).wait_recv()

    sent = []

    def wall_own(layer):
        for piece in range(2):
            sent.append(wall_ship(piece, layer, me, piece, to_up, True))
            sent.append(wall_ship(2 + piece, layer, me, 1 - piece, to_down, True))
        for piece in range(2):
            sent.append(wall_ship(4 + piece, layer, me, piece, to_twin, True))

    def wall_near(layer):
        wall_arrived(layer, at_down, 0)
        sent.append(wall_ship(6, layer, at_down, 0, to_up))
        sent.append(wall_ship(7, layer, at_down, 0, to_twin))
        wall_arrived(layer, at_up, 1)
        sent.append(wall_ship(8, layer, at_up, 1, to_down))
        sent.append(wall_ship(9, layer, at_up, 1, to_twin))
        wall_arrived(layer, at_down, 1)
        sent.append(wall_ship(10, layer, at_down, 1, to_twin))
        wall_arrived(layer, at_up, 0)
        sent.append(wall_ship(11, layer, at_up, 0, to_twin))

    def wall_far(layer):
        for piece in range(2):
            wall_arrived(layer, at_far, piece)
            sent.append(wall_ship(12 + piece, layer, at_far, piece, to_twin))

    wall_own(0)

    def ask_wait(k, carry):
        ask(k).wait()
        return carry

    lax.fori_loop(1, shards, ask_wait, 0)
    to_scalar = pltpu.make_async_copy(asked, asked_s, asked_sem)
    to_scalar.start()
    to_scalar.wait()

    def give(k):
        other = lax.rem(db + k, shards)
        return remote(send.at[other], recv.at[db], row_send.at[k], row_recv.at[k], db_at(k))

    def pick(k, carry):
        other = lax.rem(db + k, shards)
        for slot in range(cap):
            send[other, slot] = base[asked_s[other, 0, slot]]
        give(k).start()
        return carry

    lax.fori_loop(1, shards, pick, 0)
    for slot in range(cap):
        recv[db, slot] = base[asked_s[db, 0, slot]]

    heads_local = query_ref.shape[1] // head
    tokens = query_ref.shape[0]

    def prepare(h, carry):
        lanes = pl.ds(pl.multiple_of(h * head, head), head)
        stage[pl.ds(0, tokens)] = unit(query_ref[:, lanes].astype(jnp.float32)) * scale
        stage[pl.ds(tokens, BL)] = jnp.zeros((BL, head), jnp.float32)
        queries[:, lanes] = stage[pl.ds(BL - 1, tokens)].astype(jnp.bfloat16)
        return carry

    lax.fori_loop(0, heads_local, prepare, 0)
    kv_copy.wait()

    def split(t, carry):
        span = pl.ds(pl.multiple_of(t * 32, 32), 32)
        kv[:, span, :] = jnp.transpose(kv_raw[span], (1, 0, 2))
        return carry

    lax.fori_loop(0, features // 32, split, 0)
    for h in range(group):
        value_s[:, pl.ds(h * pair + head, head)] = jnp.ones((per * positions, head), jnp.bfloat16)

    wall_near(0)
    wall_own(1)
    wall_far(0)
    wall_near(1)

    def give_wait(k, carry):
        give(k).wait()
        return carry

    lax.fori_loop(1, shards, give_wait, 0)

    def part(k):
        other, device = group_at(k)
        return remote(rows.at[other], parts.at[me], part_send.at[k], part_recv.at[k], device)

    def choose(k, carry):
        other = lax.rem(me + k, group)
        for slot in range(per):
            place = target_ref[other * per + slot]
            rows[other, slot] = recv[place // cap, lax.rem(place, cap)]
        part(k).start()
        return carry

    lax.fori_loop(1, group, choose, 0)
    wall_far(1)
    for slot in range(per):
        place = target_ref[me * per + slot]
        parts[me, slot] = recv[place // cap, lax.rem(place, cap)]

    def part_wait(k, carry):
        part(k).wait()
        return carry

    lax.fori_loop(1, group, part_wait, 0)

    for source in range(group):
        for slot in range(per):
            hidden[pl.ds(slot * positions, positions), pl.ds(source * head, head)] = parts[
                source, slot
            ].astype(jnp.float32)

    same = lax.broadcasted_iota(jnp.int32, (pair, pair), 0) // head == (
        lax.broadcasted_iota(jnp.int32, (pair, pair), 1) // head
    )
    average = jnp.where(same, 1.0 / head, 0.0).astype(jnp.bfloat16)

    def unit_pair(tensor):
        square = (tensor * tensor).astype(jnp.bfloat16)
        return tensor * lax.rsqrt(
            jnp.dot(square, average, preferred_element_type=jnp.float32) + 1e-06
        )

    def product(left, right):
        return jnp.dot(left, right, preferred_element_type=jnp.float32)

    def against(left, right):
        return lax.dot_general(
            left, right, (((1,), (1,)), ((), ())), preferred_element_type=jnp.float32
        )

    def put_values(p, value):
        value_s[:, pl.ds(2 * p * pair, head)] = value[:, :head]
        value_s[:, pl.ds((2 * p + 1) * pair, head)] = value[:, head:]

    out_copy.wait()
    for layer in range(layers):
        for chunk in (at_twin, up_twin, down_twin, far_twin):
            for piece in range(2):
                wall_arrived(layer, chunk, piece)

    def encode(layer, carry):
        normed[...] = (unit(hidden[...]) * gain_ref[pl.ds(layer, 1)]).astype(jnp.bfloat16)
        for p in range(group // 2):
            lanes = pl.ds(p * pair, pair)
            query = unit_pair(product(normed[...], wall[layer, 0, :, lanes])) * scale
            query_s[:, lanes] = query.astype(jnp.bfloat16)
            key = unit_pair(product(normed[...], wall[layer, 1, :, lanes]))
            key_s[:, lanes] = key.astype(jnp.bfloat16)
            value = product(normed[...], wall[layer, 2, :, lanes]).astype(jnp.bfloat16)
            put_values(p, value)
        for h in range(group):
            lanes = pl.ds(h * head, head)
            for slot in range(per):
                span = pl.ds(slot * positions, positions)
                weights = jnp.exp2(against(query_s[span, lanes], key_s[span, lanes]))
                mixed = product(weights.astype(jnp.bfloat16), value_s[span, pl.ds(h * pair, pair)])
                attended[span, lanes] = (mixed[:, :head] / mixed[:, head:]).astype(jnp.bfloat16)
        for t in range(features // 256):
            lanes = pl.ds(t * 256, 256)
            hidden[:, lanes] += product(attended[...], wout[layer, :, lanes])
        return carry

    lax.fori_loop(0, layers, encode, 0)
    chunks[me] = (unit(hidden[...]) * final_ref[...]).astype(jnp.bfloat16)
    half = chunks.shape[1] // 2

    def ship(number, chunk, piece, device):
        place = chunks.at[chunk, pl.ds(piece * half, half)]
        remote(place, place, chunk_send.at[number], chunk_recv.at[chunk, piece], device).start()

    def arrived(chunk, piece):
        place = chunks.at[chunk, pl.ds(piece * half, half)]
        remote(
            place, place, chunk_send.at[0], chunk_recv.at[chunk, piece], to_twin
        ).wait_recv()

    for piece in range(2):
        ship(piece, me, piece, to_up)
        ship(2 + piece, me, 1 - piece, to_down)
    for piece in range(2):
        ship(4 + piece, me, piece, to_twin)

    def cross(step, carry):
        @pl.when(step == 1)
        def _():
            for piece in range(2):
                arrived(at_twin, piece)

        @pl.when(step == 2)
        def _():
            arrived(at_down, 0)
            ship(6, at_down, 0, to_up)
            ship(7, at_down, 0, to_twin)
            arrived(at_up, 1)
            ship(8, at_up, 1, to_down)
            ship(9, at_up, 1, to_twin)
            arrived(at_down, 1)
            ship(10, at_down, 1, to_twin)

        @pl.when(step == 3)
        def _():
            arrived(at_up, 0)
            ship(11, at_up, 0, to_twin)

        @pl.when(step == 4)
        def _():
            for piece in range(2):
                arrived(down_twin, piece)

        @pl.when(step == 5)
        def _():
            for piece in range(2):
                arrived(up_twin, piece)

        @pl.when(step == 6)
        def _():
            for piece in range(2):
                arrived(at_far, piece)
                ship(12 + piece, at_far, piece, to_twin)

        @pl.when(step == 7)
        def _():
            for piece in range(2):
                arrived(far_twin, piece)

        chunk = at_far
        for number, place in enumerate(
            (me, at_twin, at_down, at_up, down_twin, up_twin, at_far, far_twin)
        ):
            chunk = jnp.where(step == number, place, chunk)
        alive = (live_ref[chunk] > 1).astype(jnp.float32)
        span = pl.ds(pl.multiple_of(chunk * BL, BL), BL)
        for p in range(heads_local // 2):
            lanes = pl.ds(p * pair, pair)
            key = unit_pair(product(chunks[chunk], kv[0, :, lanes]))
            key_s[:, lanes] = key.astype(jnp.bfloat16)
            put_values(p, product(chunks[chunk], kv[1, :, lanes]).astype(jnp.bfloat16))
        for h in range(heads_local):
            lanes = pl.ds(h * head, head)
            weights = jnp.exp2(against(queries[span, lanes], key_s[:, lanes]))
            weights = jnp.concatenate(
                [weights[:, :positions], weights[:, positions:] * alive], axis=1
            )
            mixed = product(weights.astype(jnp.bfloat16), value_s[:, pl.ds(h * pair, pair)])
            mix_ref[span, lanes] = (mixed[:, :head] / mixed[:, head:]).astype(jnp.bfloat16)
        return carry

    lax.fori_loop(0, blocks, cross, 0)
    for number in range(14):
        place = chunks.at[me, pl.ds(0, half)]
        remote(place, place, chunk_send.at[number], chunk_recv.at[me, 0], to_twin).wait_send()
    for copy in sent:
        copy.wait_send()


def retrieve(shards, group, cap, ask, target, data, live, gain, final, query, own, out, kv):
    positions, per_shard, head = data.shape
    layers, features = gain.shape
    per = target.shape[0] // group
    tokens = query.shape[0]
    dma = pltpu.SemaphoreType.DMA
    bf16, f32 = jnp.bfloat16, jnp.float32
    return pl.pallas_call(
        functools.partial(kernel, shards, group, cap, 3.0 / math.sqrt(head) * math.log2(math.e)),
        out_shape=jax.ShapeDtypeStruct(query.shape, bf16),
        in_specs=[VMEM, SMEM, VMEM, SMEM, VMEM, VMEM, VMEM, ANY, ANY, ANY],
        out_specs=VMEM,
        scratch_shapes=[
            pltpu.VMEM((per_shard, positions, head), bf16),
            pltpu.VMEM((shards, 1, 128), jnp.int32),
            pltpu.SMEM((shards, 1, 128), jnp.int32),
            pltpu.VMEM((shards, cap, positions, head), bf16),
            pltpu.VMEM((shards, cap, positions, head), bf16),
            pltpu.VMEM((group, per, positions, head), bf16),
            pltpu.VMEM((group, per, positions, head), bf16),
            pltpu.VMEM(own.shape, bf16),
            pltpu.VMEM((layers, 3, features, head), bf16),
            pltpu.VMEM((layers, 3, features, features), bf16),
            pltpu.VMEM(out.shape, bf16),
            pltpu.VMEM(kv.shape, bf16),
            pltpu.VMEM((2, features, kv.shape[2]), bf16),
            pltpu.VMEM((per * positions, features), f32),
            pltpu.VMEM((per * positions, features), bf16),
            pltpu.VMEM((per * positions, features), bf16),
            pltpu.VMEM((tokens + BL, head), f32),
            pltpu.VMEM(query.shape, bf16),
            pltpu.VMEM((per * positions, group * head), bf16),
            pltpu.VMEM((per * positions, group * head), bf16),
            pltpu.VMEM((per * positions, group * 2 * head), bf16),
            pltpu.VMEM((group, per * positions, features), bf16),
            dma((shards,)),
            dma((shards,)),
            dma((shards,)),
            dma((shards,)),
            dma((group,)),
            dma((group,)),
            dma,
            dma,
            dma,
            dma,
            dma((layers, 14)),
            dma((layers, group, 2)),
            dma((14,)),
            dma((group, 2)),
        ],
        compiler_params=pltpu.CompilerParams(
            collective_id=0, has_side_effects=True, vmem_limit_bytes=52 * 2**20
        ),
    )(ask, target, data, live, gain, final, query, own, out, kv)


def on_device(
    queries,
    database,
    neighbour_ids,
    live_counts,
    entry_rows,
    enc_gain,
    enc_qkv,
    enc_out,
    final_gain,
    kv_weight,
):
    shards = lax.axis_size("db")
    group = lax.axis_size(GROUP)
    per_shard = database.shape[1]
    wanted = neighbour_ids.reshape(-1)
    requests = wanted.shape[0]
    capacity = max(2, (requests + shards - 1) // shards)
    located = jnp.take(entry_rows, wanted)
    holder = located // per_shard
    within = located % per_shard
    ordinal = jnp.arange(requests)
    before = (holder[:, None] == holder[None, :]) & (ordinal[None, :] < ordinal[:, None])
    standing = jnp.sum(before.astype(jnp.int32), axis=1)
    target = holder * capacity + standing
    buckets = jnp.arange(shards)[:, None] * capacity + jnp.arange(128)[None, :]
    inside = jnp.arange(128)[None, :, None] < capacity
    matched = ((target[None, None, :] == buckets[:, :, None]) & inside).astype(jnp.int32)
    outgoing = jnp.sum(matched * within[None, None, :], axis=2).reshape(shards, 1, 128)
    mixed = retrieve(
        shards,
        group,
        capacity,
        outgoing,
        target,
        database,
        live_counts,
        enc_gain,
        final_gain.reshape(1, -1),
        queries,
        enc_qkv,
        enc_out,
        kv_weight,
    )
    tokens, width = queries.shape
    front = jnp.zeros((BL - 1, width), mixed.dtype)
    return jnp.concatenate([front, mixed[: tokens - BL + 1]], axis=0)


def solution(mesh):
    return jax.shard_map(
        on_device,
        mesh=mesh,
        in_specs=(
            P("db", GROUP),
            P(None, "db", GROUP),
            P("db", None),
            P("db"),
            P(),
            P(),
            P(None, None, None, GROUP),
            P(),
            P(),
            P(None, None, GROUP),
        ),
        out_specs=P("db", GROUP),
        check_vma=False,
    )
```

```python
import functools
import math

import jax
import jax.numpy as jnp
from jax import lax
from jax.experimental import pallas as pl
from jax.experimental.pallas import tpu as pltpu
from jax.sharding import PartitionSpec as P

BL = 64
GROUP = ("mp", "section")
MESH = pl.DeviceIdType.MESH
VMEM = pl.BlockSpec(memory_space=pltpu.VMEM)
SMEM = pl.BlockSpec(memory_space=pltpu.SMEM)
ANY = pl.BlockSpec(memory_space=pl.ANY)


def unit(tensor):
    return tensor * lax.rsqrt(jnp.mean(tensor * tensor, axis=-1, keepdims=True) + 1e-06)


def remote(src, dst, send_sem, recv_sem, device):
    return pltpu.make_async_remote_copy(
        src_ref=src,
        dst_ref=dst,
        send_sem=send_sem,
        recv_sem=recv_sem,
        device_id=device,
        device_id_type=MESH,
    )


def kernel(
    shards,
    group,
    cap,
    scale,
    ask_ref,
    plan_ref,
    data_ref,
    live_ref,
    gain_ref,
    final_ref,
    query_ref,
    own_hbm,
    out_hbm,
    kv_hbm,
    mix_ref,
    base,
    asked,
    asked_s,
    send,
    early,
    late,
    rows,
    parts,
    own,
    wall,
    wout,
    kv_raw,
    kv,
    hidden,
    normed,
    attended,
    stage,
    queries,
    query_s,
    key_s,
    value_s,
    chunks,
    sums,
    ask_send,
    ask_recv,
    row_send,
    row_recv,
    part_send,
    part_recv,
    asked_sem,
    own_sem,
    out_sem,
    kv_sem,
    wall_send,
    wall_recv,
    chunk_send,
    chunk_recv,
):
    sections = 2
    chips = group // sections
    db = lax.axis_index("db")
    y = lax.axis_index("mp")
    c = lax.axis_index("section")
    me = y * sections + c
    up, down, far = lax.rem(y + 1, chips), lax.rem(y + chips - 1, chips), lax.rem(y + 2, chips)
    to_up, to_down, to_twin = {"mp": up}, {"mp": down}, {"section": 1 - c}
    at_up, at_down, at_far = up * sections + c, down * sections + c, far * sections + c
    at_twin = y * sections + 1 - c
    up_twin, down_twin, far_twin = (place * sections + 1 - c for place in (up, down, far))

    layers, features = gain_ref.shape
    positions, head = base.shape[1], base.shape[2]
    batches = rows.shape[0]
    first = cap // batches
    pair = 2 * head
    blocks = live_ref.shape[0]

    own_copy = pltpu.make_async_copy(own_hbm, own, own_sem)
    out_copy = pltpu.make_async_copy(out_hbm, wout, out_sem)
    kv_copy = pltpu.make_async_copy(kv_hbm, kv_raw, kv_sem)
    for copy in (own_copy, out_copy, kv_copy):
        copy.start()

    def db_at(k):
        return {"db": lax.rem(db + k, shards)}

    def group_at(k):
        other = lax.rem(me + k, group)
        return other, {"mp": other // sections, "section": lax.rem(other, sections)}

    barrier = pltpu.get_barrier_semaphore()

    def greet_db(k, carry):
        pl.semaphore_signal(barrier, inc=1, device_id=db_at(k), device_id_type=MESH)
        return carry

    def greet_group(k, carry):
        pl.semaphore_signal(barrier, inc=1, device_id=group_at(k)[1], device_id_type=MESH)
        return carry

    lax.fori_loop(1, shards, greet_db, 0)
    lax.fori_loop(1, group, greet_group, 0)
    mine = pl.ds(pl.multiple_of(me * head, head), head)
    own_copy.wait()
    for layer in range(layers):
        wall[layer, :, :, mine] = own[layer]
    base[...] = jnp.transpose(data_ref[...], (1, 0, 2))
    pl.semaphore_wait(barrier, shards + group - 2)

    def ask(k):
        other = lax.rem(db + k, shards)
        return remote(ask_ref.at[other], asked.at[db], ask_send.at[k], ask_recv.at[k], db_at(k))

    def ask_start(k, carry):
        ask(k).start()
        return carry

    lax.fori_loop(1, shards, ask_start, 0)
    asked[pl.ds(db, 1)] = ask_ref[pl.ds(db, 1)]

    half_rows = features // 2

    def wall_place(layer, chunk, piece):
        return wall.at[
            layer,
            :,
            pl.ds(piece * half_rows, half_rows),
            pl.ds(pl.multiple_of(chunk * head, head), head),
        ]

    def wall_ship(number, layer, chunk, piece, device, local=False):
        place = wall_place(layer, chunk, piece)
        source = own.at[layer, :, pl.ds(piece * half_rows, half_rows), :] if local else place
        copy = remote(
            source, place, wall_send.at[layer, number], wall_recv.at[layer, chunk, piece], device
        )
        copy.start()
        return copy

    def wall_arrived(layer, chunk, piece):
        place = wall_place(layer, chunk, piece)
        remote(
            place, place, wall_send.at[layer, 0], wall_recv.at[layer, chunk, piece], to_twin
        ).wait_recv()

    sent = []

    def wall_own(layer):
        for piece in range(2):
            sent.append(wall_ship(piece, layer, me, piece, to_up, True))
            sent.append(wall_ship(2 + piece, layer, me, 1 - piece, to_down, True))
        for piece in range(2):
            sent.append(wall_ship(4 + piece, layer, me, piece, to_twin, True))

    def wall_near(layer):
        wall_arrived(layer, at_down, 0)
        sent.append(wall_ship(6, layer, at_down, 0, to_up))
        sent.append(wall_ship(7, layer, at_down, 0, to_twin))
        wall_arrived(layer, at_up, 1)
        sent.append(wall_ship(8, layer, at_up, 1, to_down))
        sent.append(wall_ship(9, layer, at_up, 1, to_twin))
        wall_arrived(layer, at_down, 1)
        sent.append(wall_ship(10, layer, at_down, 1, to_twin))
        wall_arrived(layer, at_up, 0)
        sent.append(wall_ship(11, layer, at_up, 0, to_twin))

    def wall_far(layer):
        for piece in range(2):
            wall_arrived(layer, at_far, piece)
            sent.append(wall_ship(12 + piece, layer, at_far, piece, to_twin))

    wall_own(0)

    def ask_wait(k, carry):
        ask(k).wait()
        return carry

    lax.fori_loop(1, shards, ask_wait, 0)
    to_scalar = pltpu.make_async_copy(asked, asked_s, asked_sem)
    to_scalar.start()
    to_scalar.wait()

    def give(k, batch):
        other = lax.rem(db + k, shards)
        return remote(
            send.at[other, pl.ds(batch * first, first)],
            (early, late)[batch].at[db],
            row_send.at[batch, k],
            row_recv.at[batch, k],
            db_at(k),
        )

    for batch in range(batches):

        def pick(k, carry, batch=batch):
            other = lax.rem(db + k, shards)
            for slot in range(batch * first, (batch + 1) * first):
                send[other, slot] = base[asked_s[other, 0, slot]]
            give(k, batch).start()
            return carry

        lax.fori_loop(1, shards, pick, 0)
    for slot in range(first):
        early[db, slot] = base[asked_s[db, 0, slot]]
        late[db, slot] = base[asked_s[db, 0, first + slot]]

    heads_local = query_ref.shape[1] // head
    tokens = query_ref.shape[0]

    def prepare(h, carry):
        lanes = pl.ds(pl.multiple_of(h * head, head), head)
        stage[pl.ds(0, tokens)] = unit(query_ref[:, lanes].astype(jnp.float32)) * scale
        stage[pl.ds(tokens, BL)] = jnp.zeros((BL, head), jnp.float32)
        shifted = stage[pl.ds(BL - 1, tokens)].astype(jnp.bfloat16)
        queries[:, :, lanes] = shifted.reshape(blocks, BL, head)
        return carry

    lax.fori_loop(0, heads_local, prepare, 0)
    kv_copy.wait()

    def split(t, carry):
        span = pl.ds(pl.multiple_of(t * 32, 32), 32)
        kv[:, span, :] = jnp.transpose(kv_raw[span], (1, 0, 2))
        return carry

    lax.fori_loop(0, features // 32, split, 0)
    for h in range(group):
        value_s[:, pl.ds(h * pair + head, head)] = jnp.ones((value_s.shape[0], head), jnp.bfloat16)

    wall_near(0)
    wall_own(1)
    wall_far(0)

    def give_wait(batch):
        def one(k, carry):
            give(k, batch).wait()
            return carry

        lax.fori_loop(1, shards, one, 0)

    def part(k, batch):
        other, device = group_at(k)
        return remote(
            rows.at[batch, other],
            parts.at[batch, me],
            part_send.at[batch, k],
            part_recv.at[batch, k],
            device,
        )

    def chosen(batch, number):
        place = plan_ref[batch * group + number]
        holder, slot = place // cap, lax.rem(place, cap)
        row = early[holder, jnp.minimum(slot, first - 1)]
        if batch == 0:
            return row
        return jnp.where(slot < first, row, late[holder, jnp.maximum(slot - first, 0)])

    def part_start(batch):
        def one(k, carry):
            other = lax.rem(me + k, group)
            rows[batch, other] = chosen(batch, other)
            part(k, batch).start()
            return carry

        lax.fori_loop(1, group, one, 0)
        parts[batch, me] = chosen(batch, me)

    def part_wait(batch):
        def one(k, carry):
            part(k, batch).wait()
            return carry

        lax.fori_loop(1, group, one, 0)
        for source in range(group):
            hidden[batch, :, pl.ds(source * head, head)] = parts[batch, source].astype(jnp.float32)

    same = lax.broadcasted_iota(jnp.int32, (pair, pair), 0) // head == (
        lax.broadcasted_iota(jnp.int32, (pair, pair), 1) // head
    )
    average = jnp.where(same, 1.0 / head, 0.0).astype(jnp.bfloat16)

    def unit_pair(tensor):
        square = (tensor * tensor).astype(jnp.bfloat16)
        return tensor * lax.rsqrt(
            jnp.dot(square, average, preferred_element_type=jnp.float32) + 1e-06
        )

    def product(left, right):
        return jnp.dot(left, right, preferred_element_type=jnp.float32)

    def against(left, right):
        return lax.dot_general(
            left, right, (((1,), (1,)), ((), ())), preferred_element_type=jnp.float32
        )

    def put_values(p, value):
        rows_of = pl.ds(0, value.shape[0])
        value_s[rows_of, pl.ds(2 * p * pair, head)] = value[:, :head]
        value_s[rows_of, pl.ds((2 * p + 1) * pair, head)] = value[:, head:]

    def wall_wait(layer):
        for chunk in (at_twin, up_twin, down_twin, far_twin):
            for piece in range(2):
                wall_arrived(layer, chunk, piece)

    span = pl.ds(0, positions)

    def encode(batch, layer):
        normed[...] = (unit(hidden[batch]) * gain_ref[pl.ds(layer, 1)]).astype(jnp.bfloat16)
        for p in range(group // 2):
            lanes = pl.ds(p * pair, pair)
            query = unit_pair(product(normed[...], wall[layer, 0, :, lanes])) * scale
            query_s[:, lanes] = query.astype(jnp.bfloat16)
            key = unit_pair(product(normed[...], wall[layer, 1, :, lanes]))
            key_s[span, lanes] = key.astype(jnp.bfloat16)
            put_values(p, product(normed[...], wall[layer, 2, :, lanes]).astype(jnp.bfloat16))
        for h in range(group):
            lanes = pl.ds(h * head, head)
            weights = jnp.exp2(against(query_s[:, lanes], key_s[span, lanes]))
            mixed = product(weights.astype(jnp.bfloat16), value_s[span, pl.ds(h * pair, pair)])
            attended[:, lanes] = (mixed[:, :head] / mixed[:, head:]).astype(jnp.bfloat16)
        for t in range(features // 256):
            lanes = pl.ds(t * 256, 256)
            hidden[batch, :, lanes] += product(attended[...], wout[layer, :, lanes])

    half = positions // 2

    def chunk_place(batch, chunk, piece):
        return chunks.at[
            batch, chunk // sections, pl.ds(lax.rem(chunk, sections) * positions + piece * half, half)
        ]

    def ship(number, batch, chunk, piece, device):
        place = chunk_place(batch, chunk, piece)
        remote(
            place, place, chunk_send.at[batch, number], chunk_recv.at[batch, chunk, piece], device
        ).start()

    def arrived(batch, chunk, piece):
        place = chunk_place(batch, chunk, piece)
        remote(
            place, place, chunk_send.at[batch, 0], chunk_recv.at[batch, chunk, piece], to_twin
        ).wait_recv()

    def finish(batch):
        encoded = (unit(hidden[batch]) * final_ref[...]).astype(jnp.bfloat16)
        chunks[batch, y, pl.ds(pl.multiple_of(c * positions, positions), positions)] = encoded
        for piece in range(2):
            ship(piece, batch, me, piece, to_up)
            ship(2 + piece, batch, me, 1 - piece, to_down)
        for piece in range(2):
            ship(4 + piece, batch, me, piece, to_twin)

    def relay_near(batch):
        arrived(batch, at_down, 0)
        ship(6, batch, at_down, 0, to_up)
        ship(7, batch, at_down, 0, to_twin)
        arrived(batch, at_up, 1)
        ship(8, batch, at_up, 1, to_down)
        ship(9, batch, at_up, 1, to_twin)
        arrived(batch, at_down, 1)
        ship(10, batch, at_down, 1, to_twin)
        arrived(batch, at_up, 0)
        ship(11, batch, at_up, 0, to_twin)

    def relay_far(batch):
        for piece in range(2):
            arrived(batch, at_far, piece)
            ship(12 + piece, batch, at_far, piece, to_twin)

    def twin_wait(batch, chunk):
        for piece in range(2):
            arrived(batch, chunk, piece)

    def cross(batch, chip):
        tokens_here = chunks.at[batch, chip]
        for p in range(heads_local // 2):
            lanes = pl.ds(p * pair, pair)
            key = unit_pair(product(tokens_here[...], kv[0, :, lanes]))
            key_s[:, lanes] = key.astype(jnp.bfloat16)
            put_values(p, product(tokens_here[...], kv[1, :, lanes]).astype(jnp.bfloat16))
        for core in range(sections):
            place = batch * group + chip * sections + core
            block = plan_ref[batches * group + place]
            here = pl.ds(core * positions, positions)
            for h in range(heads_local):
                lanes = pl.ds(h * head, head)
                weights = jnp.exp2(against(queries[block, :, lanes], key_s[here, lanes]))
                sums[place, :, pl.ds(h * pair, pair)] = product(
                    weights.astype(jnp.bfloat16), value_s[here, pl.ds(h * pair, pair)]
                )

    give_wait(0)
    part_start(0)
    out_copy.wait()
    wall_wait(0)
    part_wait(0)
    encode(0, 0)
    wall_near(1)
    wall_far(1)
    give_wait(1)
    part_start(1)
    wall_wait(1)
    encode(0, 1)
    finish(0)
    part_wait(1)
    encode(1, 0)
    relay_near(0)
    encode(1, 1)
    finish(1)
    relay_far(0)

    def step(number, carry):
        batch = number // chips
        turn = lax.rem(number, chips)

        @pl.when(number == 0)
        def _():
            twin_wait(0, at_twin)

        @pl.when(number == 1)
        def _():
            twin_wait(0, down_twin)

        @pl.when(number == 2)
        def _():
            twin_wait(0, up_twin)
            relay_near(1)

        @pl.when(number == 3)
        def _():
            twin_wait(0, far_twin)

        @pl.when(number == 4)
        def _():
            twin_wait(1, at_twin)
            relay_far(1)

        @pl.when(number == 5)
        def _():
            twin_wait(1, down_twin)

        @pl.when(number == 6)
        def _():
            twin_wait(1, up_twin)

        @pl.when(number == 7)
        def _():
            twin_wait(1, far_twin)

        chip = jnp.where(
            turn == 0, y, jnp.where(turn == 1, down, jnp.where(turn == 2, up, far))
        )
        cross(batch, chip)
        return carry

    lax.fori_loop(0, batches * chips, step, 0)

    def combine(block, carry):
        at = 2 * batches * group + 2 * block
        one, two = plan_ref[at], plan_ref[at + 1]
        alive = (live_ref[block] > 1).astype(jnp.float32)
        span = pl.ds(pl.multiple_of(block * BL, BL), BL)
        for h in range(heads_local):
            lanes = pl.ds(h * pair, pair)
            mixed = sums[one, :, lanes] + sums[two, :, lanes] * alive
            mix_ref[span, pl.ds(h * head, head)] = (mixed[:, :head] / mixed[:, head:]).astype(
                jnp.bfloat16
            )
        return carry

    lax.fori_loop(0, blocks, combine, 0)
    for batch in range(batches):
        for number in range(14):
            place = chunk_place(batch, me, 0)
            remote(
                place, place, chunk_send.at[batch, number], chunk_recv.at[batch, me, 0], to_twin
            ).wait_send()
    for copy in sent:
        copy.wait_send()


def retrieve(shards, group, cap, ask, plan, data, live, gain, final, query, own, out, kv):
    positions, per_shard, head = data.shape
    layers, features = gain.shape
    batches = 2
    blocks = live.shape[0]
    tokens = query.shape[0]
    chips = group // 2
    dma = pltpu.SemaphoreType.DMA
    bf16, f32 = jnp.bfloat16, jnp.float32
    return pl.pallas_call(
        functools.partial(kernel, shards, group, cap, 3.0 / math.sqrt(head) * math.log2(math.e)),
        out_shape=jax.ShapeDtypeStruct(query.shape, bf16),
        in_specs=[VMEM, SMEM, VMEM, SMEM, VMEM, VMEM, VMEM, ANY, ANY, ANY],
        out_specs=VMEM,
        scratch_shapes=[
            pltpu.VMEM((per_shard, positions, head), bf16),
            pltpu.VMEM((shards, 1, 128), jnp.int32),
            pltpu.SMEM((shards, 1, 128), jnp.int32),
            pltpu.VMEM((shards, cap, positions, head), bf16),
            pltpu.VMEM((shards, cap // 2, positions, head), bf16),
            pltpu.VMEM((shards, cap // 2, positions, head), bf16),
            pltpu.VMEM((batches, group, positions, head), bf16),
            pltpu.VMEM((batches, group, positions, head), bf16),
            pltpu.VMEM(own.shape, bf16),
            pltpu.VMEM((layers, 3, features, features), bf16),
            pltpu.VMEM(out.shape, bf16),
            pltpu.VMEM(kv.shape, bf16),
            pltpu.VMEM((2, features, kv.shape[2]), bf16),
            pltpu.VMEM((batches, positions, features), f32),
            pltpu.VMEM((positions, features), bf16),
            pltpu.VMEM((positions, features), bf16),
            pltpu.VMEM((tokens + BL, head), f32),
            pltpu.VMEM((blocks, BL, query.shape[1]), bf16),
            pltpu.VMEM((positions, group * head), bf16),
            pltpu.VMEM((2 * positions, group * head), bf16),
            pltpu.VMEM((2 * positions, group * 2 * head), bf16),
            pltpu.VMEM((batches, chips, 2 * positions, features), bf16),
            pltpu.VMEM((batches * group, BL, 2 * query.shape[1]), f32),
            dma((shards,)),
            dma((shards,)),
            dma((batches, shards)),
            dma((batches, shards)),
            dma((batches, group)),
            dma((batches, group)),
            dma,
            dma,
            dma,
            dma,
            dma((layers, 14)),
            dma((layers, group, 2)),
            dma((batches, 14)),
            dma((batches, group, 2)),
        ],
        compiler_params=pltpu.CompilerParams(
            collective_id=0, has_side_effects=True, vmem_limit_bytes=60 * 2**20
        ),
    )(ask, plan, data, live, gain, final, query, own, out, kv)


def on_device(
    queries,
    database,
    neighbour_ids,
    live_counts,
    entry_rows,
    enc_gain,
    enc_qkv,
    enc_out,
    final_gain,
    kv_weight,
):
    shards = lax.axis_size("db")
    group = lax.axis_size(GROUP)
    per_shard = database.shape[1]
    wanted = neighbour_ids.reshape(-1)
    requests = wanted.shape[0]
    capacity = max(2, (requests + shards - 1) // shards)
    located = jnp.take(entry_rows, wanted)
    holder = located // per_shard
    within = located % per_shard
    ordinal = jnp.arange(requests)
    before = (holder[:, None] == holder[None, :]) & (ordinal[None, :] < ordinal[:, None])
    standing = jnp.sum(before.astype(jnp.int32), axis=1)
    target = holder * capacity + standing
    early = standing < capacity // 2
    earlier = jnp.sum((early[None, :] & (ordinal[None, :] < ordinal[:, None])).astype(jnp.int32), axis=1)
    batch_size = requests // 2
    place = jnp.where(
        early & (earlier < batch_size),
        earlier,
        batch_size + ordinal - jnp.minimum(earlier, batch_size),
    )
    seated = (place[None, :] == ordinal[:, None]).astype(jnp.int32)
    block_of = ordinal // neighbour_ids.shape[1]
    plan = jnp.concatenate(
        [jnp.sum(seated * target[None, :], axis=1), jnp.sum(seated * block_of[None, :], axis=1), place]
    )
    buckets = jnp.arange(shards)[:, None] * capacity + jnp.arange(128)[None, :]
    inside = jnp.arange(128)[None, :, None] < capacity
    matched = ((target[None, None, :] == buckets[:, :, None]) & inside).astype(jnp.int32)
    outgoing = jnp.sum(matched * within[None, None, :], axis=2).reshape(shards, 1, 128)
    mixed = retrieve(
        shards,
        group,
        capacity,
        outgoing,
        plan,
        database,
        live_counts,
        enc_gain,
        final_gain.reshape(1, -1),
        queries,
        enc_qkv.transpose(0, 2, 1, 3),
        enc_out,
        kv_weight,
    )
    tokens, width = queries.shape
    front = jnp.zeros((BL - 1, width), mixed.dtype)
    return jnp.concatenate([front, mixed[: tokens - BL + 1]], axis=0)


def solution(mesh):
    return jax.shard_map(
        on_device,
        mesh=mesh,
        in_specs=(
            P("db", GROUP),
            P(None, "db", GROUP),
            P("db", None),
            P("db"),
            P(),
            P(),
            P(None, None, None, GROUP),
            P(),
            P(),
            P(None, None, GROUP),
        ),
        out_specs=P("db", GROUP),
        check_vma=False,
    )
```

```python
import functools
import math

import jax
import jax.numpy as jnp
from jax import lax
from jax.experimental import pallas as pl
from jax.experimental.pallas import tpu as pltpu
from jax.sharding import PartitionSpec as P

BL = 64
GROUP = ("mp", "section")
MESH = pl.DeviceIdType.MESH
VMEM = pl.BlockSpec(memory_space=pltpu.VMEM)
SMEM = pl.BlockSpec(memory_space=pltpu.SMEM)
ANY = pl.BlockSpec(memory_space=pl.ANY)


def unit(tensor):
    return tensor * lax.rsqrt(jnp.mean(tensor * tensor, axis=-1, keepdims=True) + 1e-06)


def remote(src, dst, send_sem, recv_sem, device):
    return pltpu.make_async_remote_copy(
        src_ref=src,
        dst_ref=dst,
        send_sem=send_sem,
        recv_sem=recv_sem,
        device_id=device,
        device_id_type=MESH,
    )


def kernel(
    shards,
    group,
    cap,
    scale,
    ask_ref,
    plan_ref,
    data_ref,
    live_ref,
    gain_ref,
    final_ref,
    query_ref,
    own_hbm,
    out_hbm,
    kv_hbm,
    mix_ref,
    base,
    asked,
    asked_s,
    send,
    early,
    both,
    rows,
    parts,
    own,
    wall,
    wout,
    kv_raw,
    kv,
    hidden,
    normed,
    attended,
    stage,
    queries,
    enc_q,
    enc_k,
    enc_v,
    key_s,
    value_s,
    chunks,
    sums,
    ask_send,
    ask_recv,
    row_send,
    row_recv,
    part_send,
    part_recv,
    asked_sem,
    own_sem,
    out_sem,
    kv_sem,
    wall_send,
    wall_recv,
    chunk_send,
    chunk_recv,
):
    sections = 2
    chips = group // sections
    db = lax.axis_index("db")
    y = lax.axis_index("mp")
    c = lax.axis_index("section")
    me = y * sections + c
    up, down, far = lax.rem(y + 1, chips), lax.rem(y + chips - 1, chips), lax.rem(y + 2, chips)
    to_up, to_down, to_twin = {"mp": up}, {"mp": down}, {"section": 1 - c}
    at_up, at_down, at_far = up * sections + c, down * sections + c, far * sections + c
    at_twin = y * sections + 1 - c
    up_twin, down_twin, far_twin = (place * sections + 1 - c for place in (up, down, far))

    layers, features = gain_ref.shape
    positions, head = base.shape[1], base.shape[2]
    batches = rows.shape[0]
    first = cap // batches
    pair = 2 * head
    blocks = live_ref.shape[0]

    own_copy = pltpu.make_async_copy(own_hbm, own, own_sem)
    out_copy = pltpu.make_async_copy(out_hbm, wout, out_sem)
    kv_copy = pltpu.make_async_copy(kv_hbm, kv_raw, kv_sem)
    for copy in (own_copy, out_copy, kv_copy):
        copy.start()

    def db_at(k):
        return {"db": lax.rem(db + k, shards)}

    def group_at(k):
        other = lax.rem(me + k, group)
        return other, {"mp": other // sections, "section": lax.rem(other, sections)}

    barrier = pltpu.get_barrier_semaphore()

    def greet_db(k, carry):
        pl.semaphore_signal(barrier, inc=1, device_id=db_at(k), device_id_type=MESH)
        return carry

    def greet_group(k, carry):
        pl.semaphore_signal(barrier, inc=1, device_id=group_at(k)[1], device_id_type=MESH)
        return carry

    lax.fori_loop(1, shards, greet_db, 0)
    lax.fori_loop(1, group, greet_group, 0)
    mine = pl.ds(pl.multiple_of(me * head, head), head)
    own_copy.wait()
    for layer in range(layers):
        wall[layer, :, :, mine] = own[layer]
    base[...] = jnp.transpose(data_ref[...], (1, 0, 2))
    pl.semaphore_wait(barrier, shards + group - 2)

    def ask(k):
        other = lax.rem(db + k, shards)
        return remote(ask_ref.at[other], asked.at[db], ask_send.at[k], ask_recv.at[k], db_at(k))

    def ask_start(k, carry):
        ask(k).start()
        return carry

    lax.fori_loop(1, shards, ask_start, 0)
    asked[pl.ds(db, 1)] = ask_ref[pl.ds(db, 1)]

    half_rows = features // 2

    def wall_place(layer, chunk, piece):
        return wall.at[
            layer,
            :,
            pl.ds(piece * half_rows, half_rows),
            pl.ds(pl.multiple_of(chunk * head, head), head),
        ]

    def wall_ship(number, layer, chunk, piece, device, local=False):
        place = wall_place(layer, chunk, piece)
        source = own.at[layer, :, pl.ds(piece * half_rows, half_rows), :] if local else place
        copy = remote(
            source, place, wall_send.at[layer, number], wall_recv.at[layer, chunk, piece], device
        )
        copy.start()
        return copy

    def wall_arrived(layer, chunk, piece):
        place = wall_place(layer, chunk, piece)
        remote(
            place, place, wall_send.at[layer, 0], wall_recv.at[layer, chunk, piece], to_twin
        ).wait_recv()

    sent = []

    def wall_own(layer):
        for piece in range(2):
            sent.append(wall_ship(piece, layer, me, piece, to_up, True))
            sent.append(wall_ship(2 + piece, layer, me, 1 - piece, to_down, True))
        for piece in range(2):
            sent.append(wall_ship(4 + piece, layer, me, piece, to_twin, True))

    def wall_near(layer):
        wall_arrived(layer, at_down, 0)
        sent.append(wall_ship(6, layer, at_down, 0, to_up))
        sent.append(wall_ship(7, layer, at_down, 0, to_twin))
        wall_arrived(layer, at_up, 1)
        sent.append(wall_ship(8, layer, at_up, 1, to_down))
        sent.append(wall_ship(9, layer, at_up, 1, to_twin))
        wall_arrived(layer, at_down, 1)
        sent.append(wall_ship(10, layer, at_down, 1, to_twin))
        wall_arrived(layer, at_up, 0)
        sent.append(wall_ship(11, layer, at_up, 0, to_twin))

    def wall_far(layer):
        for piece in range(2):
            wall_arrived(layer, at_far, piece)
            sent.append(wall_ship(12 + piece, layer, at_far, piece, to_twin))

    wall_own(0)

    def ask_wait(k, carry):
        ask(k).wait()
        return carry

    lax.fori_loop(1, shards, ask_wait, 0)
    to_scalar = pltpu.make_async_copy(asked, asked_s, asked_sem)
    to_scalar.start()
    to_scalar.wait()

    def give(k, batch):
        other = lax.rem(db + k, shards)
        return remote(
            send.at[other, pl.ds(batch * first, first)],
            both.at[db, pl.ds(first, first)] if batch else early.at[db],
            row_send.at[batch, k],
            row_recv.at[batch, k],
            db_at(k),
        )

    for batch in range(batches):

        def pick(k, carry, batch=batch):
            other = lax.rem(db + k, shards)
            for slot in range(batch * first, (batch + 1) * first):
                send[other, slot] = base[asked_s[other, 0, slot]]
            give(k, batch).start()
            return carry

        lax.fori_loop(1, shards, pick, 0)
    for slot in range(first):
        early[db, slot] = base[asked_s[db, 0, slot]]
        both[db, first + slot] = base[asked_s[db, 0, first + slot]]

    heads_local = query_ref.shape[1] // head
    tokens = query_ref.shape[0]

    def prepare(h, carry):
        lanes = pl.ds(pl.multiple_of(h * head, head), head)
        stage[pl.ds(0, tokens)] = unit(query_ref[:, lanes].astype(jnp.float32)) * scale
        stage[pl.ds(tokens, BL)] = jnp.zeros((BL, head), jnp.float32)
        shifted = stage[pl.ds(BL - 1, tokens)].astype(jnp.bfloat16)
        queries[:, :, lanes] = shifted.reshape(blocks, BL, head)
        return carry

    lax.fori_loop(0, heads_local, prepare, 0)
    kv_copy.wait()

    def split(t, carry):
        span = pl.ds(pl.multiple_of(t * 32, 32), 32)
        kv[:, span, :] = jnp.transpose(kv_raw[span], (1, 0, 2))
        return carry

    lax.fori_loop(0, features // 32, split, 0)
    enc_v[:, pl.ds(head, head)] = jnp.ones((enc_v.shape[0], head), jnp.bfloat16)
    for h in range(heads_local):
        value_s[:, pl.ds(h * pair + head, head)] = jnp.ones((value_s.shape[0], head), jnp.bfloat16)

    wall_near(0)
    wall_own(1)
    wall_far(0)

    def give_wait(batch):
        def one(k, carry):
            give(k, batch).wait()
            return carry

        lax.fori_loop(1, shards, one, 0)

    def part(k, batch):
        other, device = group_at(k)
        return remote(
            rows.at[batch, other],
            parts.at[batch, me],
            part_send.at[batch, k],
            part_recv.at[batch, k],
            device,
        )

    def chosen(batch, number):
        place = plan_ref[batch * group + number]
        holder, slot = place // cap, lax.rem(place, cap)
        return both[holder, slot] if batch else early[holder, slot]

    def keep_early(k, carry):
        both[k, pl.ds(0, first)] = early[k]
        return carry

    def part_start(batch):
        def one(k, carry):
            other = lax.rem(me + k, group)
            rows[batch, other] = chosen(batch, other)
            part(k, batch).start()
            return carry

        lax.fori_loop(1, group, one, 0)
        parts[batch, me] = chosen(batch, me)

    def part_wait(batch):
        def one(k, carry):
            part(k, batch).wait()
            return carry

        lax.fori_loop(1, group, one, 0)
        for source in range(group):
            hidden[batch, :, pl.ds(source * head, head)] = parts[batch, source].astype(jnp.float32)

    same = lax.broadcasted_iota(jnp.int32, (pair, pair), 0) // head == (
        lax.broadcasted_iota(jnp.int32, (pair, pair), 1) // head
    )
    average = jnp.where(same, 1.0 / head, 0.0).astype(jnp.bfloat16)

    def unit_pair(tensor):
        square = (tensor * tensor).astype(jnp.bfloat16)
        return tensor * lax.rsqrt(
            jnp.dot(square, average, preferred_element_type=jnp.float32) + 1e-06
        )

    def product(left, right):
        return jnp.dot(left, right, preferred_element_type=jnp.float32)

    def against(left, right):
        return lax.dot_general(
            left, right, (((1,), (1,)), ((), ())), preferred_element_type=jnp.float32
        )

    def diagonal(scores):
        rows_in, lanes_in = scores.shape[0] // 2, scores.shape[1] // 2
        empty = jnp.zeros((rows_in, lanes_in), jnp.float32)
        upper = jnp.concatenate([jnp.exp2(scores[:rows_in, :lanes_in]), empty], axis=1)
        lower = jnp.concatenate([empty, jnp.exp2(scores[rows_in:, lanes_in:])], axis=1)
        return jnp.concatenate([upper, lower], axis=0).astype(jnp.bfloat16)

    def wall_wait(layer):
        for chunk in (at_twin, up_twin, down_twin, far_twin):
            for piece in range(2):
                wall_arrived(layer, chunk, piece)

    def encode(batch, layer):
        normed[...] = (unit(hidden[batch]) * gain_ref[pl.ds(layer, 1)]).astype(jnp.bfloat16)
        for p in range(group // 2):
            lanes = pl.ds(p * pair, pair)
            query = unit_pair(product(normed[...], wall[layer, 0, :, lanes])) * scale
            key = unit_pair(product(normed[...], wall[layer, 1, :, lanes]))
            value = product(normed[...], wall[layer, 2, :, lanes])
            for h in range(2):
                here = slice(h * head, (h + 1) * head)
                stack = pl.ds((2 * p + h) * positions, positions)
                enc_q[stack] = query[:, here].astype(jnp.bfloat16)
                enc_k[stack] = key[:, here].astype(jnp.bfloat16)
                enc_v[stack, pl.ds(0, head)] = value[:, here].astype(jnp.bfloat16)
        for p in range(group // 2):
            stack = pl.ds(2 * p * positions, 2 * positions)
            mixed = product(diagonal(against(enc_q[stack], enc_k[stack])), enc_v[stack])
            mixed = (mixed[:, :head] / mixed[:, head:]).astype(jnp.bfloat16)
            attended[:, pl.ds(p * pair, head)] = mixed[:positions]
            attended[:, pl.ds(p * pair + head, head)] = mixed[positions:]
        for t in range(features // 256):
            lanes = pl.ds(t * 256, 256)
            hidden[batch, :, lanes] += product(attended[...], wout[layer, :, lanes])

    half = positions // 2

    def chunk_place(batch, chunk, piece):
        return chunks.at[
            batch, chunk // sections, pl.ds(lax.rem(chunk, sections) * positions + piece * half, half)
        ]

    def ship(number, batch, chunk, piece, device):
        place = chunk_place(batch, chunk, piece)
        remote(
            place, place, chunk_send.at[batch, number], chunk_recv.at[batch, chunk, piece], device
        ).start()

    def arrived(batch, chunk, piece):
        place = chunk_place(batch, chunk, piece)
        remote(
            place, place, chunk_send.at[batch, 0], chunk_recv.at[batch, chunk, piece], to_twin
        ).wait_recv()

    def finish(batch):
        encoded = (unit(hidden[batch]) * final_ref[...]).astype(jnp.bfloat16)
        chunks[batch, y, pl.ds(pl.multiple_of(c * positions, positions), positions)] = encoded
        for piece in range(2):
            ship(piece, batch, me, piece, to_up)
            ship(2 + piece, batch, me, 1 - piece, to_down)
        for piece in range(2):
            ship(4 + piece, batch, me, piece, to_twin)

    def relay_near(batch):
        arrived(batch, at_down, 0)
        ship(6, batch, at_down, 0, to_up)
        ship(7, batch, at_down, 0, to_twin)
        arrived(batch, at_up, 1)
        ship(8, batch, at_up, 1, to_down)
        ship(9, batch, at_up, 1, to_twin)
        arrived(batch, at_down, 1)
        ship(10, batch, at_down, 1, to_twin)
        arrived(batch, at_up, 0)
        ship(11, batch, at_up, 0, to_twin)

    def relay_far(batch):
        for piece in range(2):
            arrived(batch, at_far, piece)
            ship(12 + piece, batch, at_far, piece, to_twin)

    def twin_wait(batch, chunk):
        for piece in range(2):
            arrived(batch, chunk, piece)

    def cross(batch, chip):
        tokens_here = chunks.at[batch, chip]
        for p in range(heads_local // 2):
            lanes = pl.ds(p * pair, pair)
            key = unit_pair(product(tokens_here[...], kv[0, :, lanes]))
            key_s[:, lanes] = key.astype(jnp.bfloat16)
            value = product(tokens_here[...], kv[1, :, lanes]).astype(jnp.bfloat16)
            value_s[:, pl.ds(2 * p * pair, head)] = value[:, :head]
            value_s[:, pl.ds((2 * p + 1) * pair, head)] = value[:, head:]
        one = batch * group + chip * sections
        first_block = plan_ref[batches * group + one]
        second_block = plan_ref[batches * group + one + 1]
        for h in range(heads_local):
            lanes = pl.ds(h * head, head)
            query = jnp.concatenate(
                [queries[first_block, :, lanes], queries[second_block, :, lanes]], axis=0
            )
            mixed = product(
                diagonal(against(query, key_s[:, lanes])), value_s[:, pl.ds(h * pair, pair)]
            )
            sums[one, :, pl.ds(h * pair, pair)] = mixed[:BL]
            sums[one + 1, :, pl.ds(h * pair, pair)] = mixed[BL:]

    give_wait(0)
    part_start(0)
    out_copy.wait()
    wall_wait(0)
    part_wait(0)
    encode(0, 0)
    lax.fori_loop(0, shards, keep_early, 0)
    wall_near(1)
    wall_far(1)
    give_wait(1)
    part_start(1)
    wall_wait(1)
    encode(0, 1)
    finish(0)
    part_wait(1)
    encode(1, 0)
    relay_near(0)
    encode(1, 1)
    finish(1)
    relay_far(0)

    def step(number, carry):
        batch = number // chips
        turn = lax.rem(number, chips)

        @pl.when(number == 0)
        def _():
            twin_wait(0, at_twin)

        @pl.when(number == 1)
        def _():
            twin_wait(0, down_twin)

        @pl.when(number == 2)
        def _():
            twin_wait(0, up_twin)
            relay_near(1)

        @pl.when(number == 3)
        def _():
            twin_wait(0, far_twin)

        @pl.when(number == 4)
        def _():
            twin_wait(1, at_twin)
            relay_far(1)

        @pl.when(number == 5)
        def _():
            twin_wait(1, down_twin)

        @pl.when(number == 6)
        def _():
            twin_wait(1, up_twin)

        @pl.when(number == 7)
        def _():
            twin_wait(1, far_twin)

        chip = jnp.where(
            turn == 0, y, jnp.where(turn == 1, down, jnp.where(turn == 2, up, far))
        )
        cross(batch, chip)
        return carry

    lax.fori_loop(0, batches * chips, step, 0)

    def combine(block, carry):
        at = 2 * batches * group + 2 * block
        one, two = plan_ref[at], plan_ref[at + 1]
        alive = (live_ref[block] > 1).astype(jnp.float32)
        span = pl.ds(pl.multiple_of(block * BL, BL), BL)
        for h in range(heads_local):
            lanes = pl.ds(h * pair, pair)
            mixed = sums[one, :, lanes] + sums[two, :, lanes] * alive
            mix_ref[span, pl.ds(h * head, head)] = (mixed[:, :head] / mixed[:, head:]).astype(
                jnp.bfloat16
            )
        return carry

    lax.fori_loop(0, blocks, combine, 0)
    for batch in range(batches):
        for number in range(14):
            place = chunk_place(batch, me, 0)
            remote(
                place, place, chunk_send.at[batch, number], chunk_recv.at[batch, me, 0], to_twin
            ).wait_send()
    for copy in sent:
        copy.wait_send()


def retrieve(shards, group, cap, ask, plan, data, live, gain, final, query, own, out, kv):
    positions, per_shard, head = data.shape
    layers, features = gain.shape
    batches = 2
    blocks = live.shape[0]
    tokens = query.shape[0]
    chips = group // 2
    dma = pltpu.SemaphoreType.DMA
    bf16, f32 = jnp.bfloat16, jnp.float32
    return pl.pallas_call(
        functools.partial(kernel, shards, group, cap, 3.0 / math.sqrt(head) * math.log2(math.e)),
        out_shape=jax.ShapeDtypeStruct(query.shape, bf16),
        in_specs=[VMEM, SMEM, VMEM, SMEM, VMEM, VMEM, VMEM, ANY, ANY, ANY],
        out_specs=VMEM,
        scratch_shapes=[
            pltpu.VMEM((per_shard, positions, head), bf16),
            pltpu.VMEM((shards, 1, 128), jnp.int32),
            pltpu.SMEM((shards, 1, 128), jnp.int32),
            pltpu.VMEM((shards, cap, positions, head), bf16),
            pltpu.VMEM((shards, cap // 2, positions, head), bf16),
            pltpu.VMEM((shards, cap, positions, head), bf16),
            pltpu.VMEM((batches, group, positions, head), bf16),
            pltpu.VMEM((batches, group, positions, head), bf16),
            pltpu.VMEM(own.shape, bf16),
            pltpu.VMEM((layers, 3, features, features), bf16),
            pltpu.VMEM(out.shape, bf16),
            pltpu.VMEM(kv.shape, bf16),
            pltpu.VMEM((2, features, kv.shape[2]), bf16),
            pltpu.VMEM((batches, positions, features), f32),
            pltpu.VMEM((positions, features), bf16),
            pltpu.VMEM((positions, features), bf16),
            pltpu.VMEM((tokens + BL, head), f32),
            pltpu.VMEM((blocks, BL, query.shape[1]), bf16),
            pltpu.VMEM((group * positions, head), bf16),
            pltpu.VMEM((group * positions, head), bf16),
            pltpu.VMEM((group * positions, 2 * head), bf16),
            pltpu.VMEM((2 * positions, group * head), bf16),
            pltpu.VMEM((2 * positions, group * 2 * head), bf16),
            pltpu.VMEM((batches, chips, 2 * positions, features), bf16),
            pltpu.VMEM((batches * group, BL, 2 * query.shape[1]), f32),
            dma((shards,)),
            dma((shards,)),
            dma((batches, shards)),
            dma((batches, shards)),
            dma((batches, group)),
            dma((batches, group)),
            dma,
            dma,
            dma,
            dma,
            dma((layers, 14)),
            dma((layers, group, 2)),
            dma((batches, 14)),
            dma((batches, group, 2)),
        ],
        compiler_params=pltpu.CompilerParams(
            collective_id=0, has_side_effects=True, vmem_limit_bytes=60 * 2**20
        ),
    )(ask, plan, data, live, gain, final, query, own, out, kv)


def on_device(
    queries,
    database,
    neighbour_ids,
    live_counts,
    entry_rows,
    enc_gain,
    enc_qkv,
    enc_out,
    final_gain,
    kv_weight,
):
    shards = lax.axis_size("db")
    group = lax.axis_size(GROUP)
    per_shard = database.shape[1]
    wanted = neighbour_ids.reshape(-1)
    requests = wanted.shape[0]
    capacity = max(2, (requests + shards - 1) // shards)
    located = jnp.take(entry_rows, wanted)
    holder = located // per_shard
    within = located % per_shard
    ordinal = jnp.arange(requests)
    before = (holder[:, None] == holder[None, :]) & (ordinal[None, :] < ordinal[:, None])
    standing = jnp.sum(before.astype(jnp.int32), axis=1)
    target = holder * capacity + standing
    early = standing < capacity // 2
    earlier = jnp.sum((early[None, :] & (ordinal[None, :] < ordinal[:, None])).astype(jnp.int32), axis=1)
    batch_size = requests // 2
    place = jnp.where(
        early & (earlier < batch_size),
        earlier,
        batch_size + ordinal - jnp.minimum(earlier, batch_size),
    )
    seated = (place[None, :] == ordinal[:, None]).astype(jnp.int32)
    block_of = ordinal // neighbour_ids.shape[1]
    plan = jnp.concatenate(
        [jnp.sum(seated * target[None, :], axis=1), jnp.sum(seated * block_of[None, :], axis=1), place]
    )
    buckets = jnp.arange(shards)[:, None] * capacity + jnp.arange(128)[None, :]
    inside = jnp.arange(128)[None, :, None] < capacity
    matched = ((target[None, None, :] == buckets[:, :, None]) & inside).astype(jnp.int32)
    outgoing = jnp.sum(matched * within[None, None, :], axis=2).reshape(shards, 1, 128)
    mixed = retrieve(
        shards,
        group,
        capacity,
        outgoing,
        plan,
        database,
        live_counts,
        enc_gain,
        final_gain.reshape(1, -1),
        queries,
        enc_qkv.transpose(0, 2, 1, 3),
        enc_out,
        kv_weight,
    )
    return lax.pad(mixed, jnp.zeros((), mixed.dtype), ((BL - 1, 1 - BL, 0), (0, 0, 0)))


def solution(mesh):
    return jax.shard_map(
        on_device,
        mesh=mesh,
        in_specs=(
            P("db", GROUP),
            P(None, "db", GROUP),
            P("db", None),
            P("db"),
            P(),
            P(),
            P(None, None, None, GROUP),
            P(),
            P(),
            P(None, None, GROUP),
        ),
        out_specs=P("db", GROUP),
        check_vma=False,
    )
```

```python
import functools
import math

import jax
import jax.numpy as jnp
from jax import lax
from jax.experimental import pallas as pl
from jax.experimental.pallas import tpu as pltpu
from jax.sharding import PartitionSpec as P

BL = 64
GROUP = ("mp", "section")
MESH = pl.DeviceIdType.MESH
VMEM = pl.BlockSpec(memory_space=pltpu.VMEM)
SMEM = pl.BlockSpec(memory_space=pltpu.SMEM)
ANY = pl.BlockSpec(memory_space=pl.ANY)


def unit(tensor):
    return tensor * lax.rsqrt(jnp.mean(tensor * tensor, axis=-1, keepdims=True) + 1e-06)


def remote(src, dst, send_sem, recv_sem, device):
    return pltpu.make_async_remote_copy(
        src_ref=src,
        dst_ref=dst,
        send_sem=send_sem,
        recv_sem=recv_sem,
        device_id=device,
        device_id_type=MESH,
    )


def kernel(
    shards,
    group,
    cap,
    scale,
    ask_ref,
    plan_ref,
    data_ref,
    live_ref,
    gain_ref,
    final_ref,
    query_ref,
    own_hbm,
    out_hbm,
    kv_hbm,
    mix_ref,
    base,
    asked,
    asked_s,
    send,
    early,
    both,
    rows,
    parts,
    own,
    wall,
    wout,
    kv_raw,
    kv,
    hidden,
    normed,
    attended,
    stage,
    queries,
    enc_q,
    enc_k,
    enc_v,
    key_s,
    value_s,
    chunks,
    sums,
    ask_send,
    ask_recv,
    row_send,
    row_recv,
    part_send,
    part_recv,
    asked_sem,
    own_sem,
    out_sem,
    kv_sem,
    wall_send,
    wall_recv,
    chunk_send,
    chunk_recv,
):
    sections = 2
    chips = group // sections
    db = lax.axis_index("db")
    y = lax.axis_index("mp")
    c = lax.axis_index("section")
    me = y * sections + c
    up, down, far = lax.rem(y + 1, chips), lax.rem(y + chips - 1, chips), lax.rem(y + 2, chips)
    to_up, to_down, to_twin = {"mp": up}, {"mp": down}, {"section": 1 - c}
    at_up, at_down, at_far = up * sections + c, down * sections + c, far * sections + c
    at_twin = y * sections + 1 - c
    up_twin, down_twin, far_twin = (place * sections + 1 - c for place in (up, down, far))

    layers, features = gain_ref.shape
    positions, head = base.shape[1], base.shape[2]
    batches = rows.shape[0]
    first = cap // batches
    pair = 2 * head
    blocks = live_ref.shape[0]

    own_copy = pltpu.make_async_copy(own_hbm, own, own_sem)
    out_copy = pltpu.make_async_copy(out_hbm, wout, out_sem)
    kv_copy = pltpu.make_async_copy(kv_hbm, kv_raw, kv_sem)
    for copy in (own_copy, out_copy, kv_copy):
        copy.start()

    def db_at(k):
        return {"db": lax.rem(db + k, shards)}

    def group_at(k):
        other = lax.rem(me + k, group)
        return other, {"mp": other // sections, "section": lax.rem(other, sections)}

    barrier = pltpu.get_barrier_semaphore()

    def greet_db(k, carry):
        pl.semaphore_signal(barrier, inc=1, device_id=db_at(k), device_id_type=MESH)
        return carry

    def greet_group(k, carry):
        pl.semaphore_signal(barrier, inc=1, device_id=group_at(k)[1], device_id_type=MESH)
        return carry

    lax.fori_loop(1, shards, greet_db, 0)
    lax.fori_loop(1, group, greet_group, 0)
    mine = pl.ds(pl.multiple_of(me * head, head), head)
    own_copy.wait()
    for layer in range(layers):
        wall[layer, :, :, mine] = own[layer]
    base[...] = jnp.transpose(data_ref[...], (1, 0, 2))
    pl.semaphore_wait(barrier, shards + group - 2)

    def ask(k):
        other = lax.rem(db + k, shards)
        return remote(ask_ref.at[other], asked.at[db], ask_send.at[k], ask_recv.at[k], db_at(k))

    def ask_start(k, carry):
        ask(k).start()
        return carry

    lax.fori_loop(1, shards, ask_start, 0)
    asked[pl.ds(db, 1)] = ask_ref[pl.ds(db, 1)]

    half_rows = features // 2

    def wall_place(layer, chunk, piece):
        return wall.at[
            layer,
            :,
            pl.ds(piece * half_rows, half_rows),
            pl.ds(pl.multiple_of(chunk * head, head), head),
        ]

    def wall_ship(number, layer, chunk, piece, device, local=False):
        place = wall_place(layer, chunk, piece)
        source = own.at[layer, :, pl.ds(piece * half_rows, half_rows), :] if local else place
        copy = remote(
            source, place, wall_send.at[layer, number], wall_recv.at[layer, chunk, piece], device
        )
        copy.start()
        return copy

    def wall_arrived(layer, chunk, piece):
        place = wall_place(layer, chunk, piece)
        remote(
            place, place, wall_send.at[layer, 0], wall_recv.at[layer, chunk, piece], to_twin
        ).wait_recv()

    sent = []

    def wall_own(layer):
        for piece in range(2):
            sent.append(wall_ship(piece, layer, me, piece, to_up, True))
            sent.append(wall_ship(2 + piece, layer, me, 1 - piece, to_down, True))
        for piece in range(2):
            sent.append(wall_ship(4 + piece, layer, me, piece, to_twin, True))

    def wall_near(layer):
        wall_arrived(layer, at_down, 0)
        sent.append(wall_ship(6, layer, at_down, 0, to_up))
        sent.append(wall_ship(7, layer, at_down, 0, to_twin))
        wall_arrived(layer, at_up, 1)
        sent.append(wall_ship(8, layer, at_up, 1, to_down))
        sent.append(wall_ship(9, layer, at_up, 1, to_twin))
        wall_arrived(layer, at_down, 1)
        sent.append(wall_ship(10, layer, at_down, 1, to_twin))
        wall_arrived(layer, at_up, 0)
        sent.append(wall_ship(11, layer, at_up, 0, to_twin))

    def wall_far(layer):
        for piece in range(2):
            wall_arrived(layer, at_far, piece)
            sent.append(wall_ship(12 + piece, layer, at_far, piece, to_twin))

    wall_own(0)

    def ask_wait(k, carry):
        ask(k).wait()
        return carry

    lax.fori_loop(1, shards, ask_wait, 0)
    to_scalar = pltpu.make_async_copy(asked, asked_s, asked_sem)
    to_scalar.start()
    to_scalar.wait()

    def give(k, batch):
        other = lax.rem(db + k, shards)
        return remote(
            send.at[other, pl.ds(batch * first, first)],
            both.at[db, pl.ds(first, first)] if batch else early.at[db],
            row_send.at[batch, k],
            row_recv.at[batch, k],
            db_at(k),
        )

    for batch in range(batches):

        def pick(k, carry, batch=batch):
            other = lax.rem(db + k, shards)
            for slot in range(batch * first, (batch + 1) * first):
                send[other, slot] = base[asked_s[other, 0, slot]]
            give(k, batch).start()
            return carry

        lax.fori_loop(1, shards, pick, 0)
    for slot in range(first):
        early[db, slot] = base[asked_s[db, 0, slot]]
        both[db, first + slot] = base[asked_s[db, 0, first + slot]]

    heads_local = query_ref.shape[1] // head
    tokens = query_ref.shape[0]

    def prepare(h, carry):
        lanes = pl.ds(pl.multiple_of(h * head, head), head)
        stage[pl.ds(0, tokens)] = unit(query_ref[:, lanes].astype(jnp.float32)) * scale
        stage[pl.ds(tokens, BL)] = jnp.zeros((BL, head), jnp.float32)
        shifted = stage[pl.ds(BL - 1, tokens)].astype(jnp.bfloat16)
        queries[:, :, lanes] = shifted.reshape(blocks, BL, head)
        return carry

    lax.fori_loop(0, heads_local, prepare, 0)
    kv_copy.wait()

    def split(t, carry):
        span = pl.ds(pl.multiple_of(t * 32, 32), 32)
        kv[:, span, :] = jnp.transpose(kv_raw[span], (1, 0, 2))
        return carry

    lax.fori_loop(0, features // 32, split, 0)
    enc_v[:, pl.ds(head, head)] = jnp.ones((enc_v.shape[0], head), jnp.bfloat16)
    for h in range(heads_local):
        value_s[:, pl.ds(h * pair + head, head)] = jnp.ones((value_s.shape[0], head), jnp.bfloat16)

    wall_near(0)
    wall_own(1)
    wall_far(0)

    def give_wait(batch):
        def one(k, carry):
            give(k, batch).wait()
            return carry

        lax.fori_loop(1, shards, one, 0)

    def part(k, batch):
        other, device = group_at(k)
        return remote(
            rows.at[batch, other],
            parts.at[batch, me],
            part_send.at[batch, k],
            part_recv.at[batch, k],
            device,
        )

    def chosen(batch, number):
        place = plan_ref[batch * group + number]
        holder, slot = place // cap, lax.rem(place, cap)
        return both[holder, slot] if batch else early[holder, slot]

    def keep_early(k, carry):
        both[k, pl.ds(0, first)] = early[k]
        return carry

    def part_start(batch):
        def one(k, carry):
            other = lax.rem(me + k, group)
            rows[batch, other] = chosen(batch, other)
            part(k, batch).start()
            return carry

        lax.fori_loop(1, group, one, 0)
        parts[batch, me] = chosen(batch, me)

    def part_wait(batch):
        def one(k, carry):
            part(k, batch).wait()
            return carry

        lax.fori_loop(1, group, one, 0)
        for source in range(group):
            hidden[batch, :, pl.ds(source * head, head)] = parts[batch, source].astype(jnp.float32)

    same = lax.broadcasted_iota(jnp.int32, (pair, pair), 0) // head == (
        lax.broadcasted_iota(jnp.int32, (pair, pair), 1) // head
    )
    average = jnp.where(same, 1.0 / head, 0.0).astype(jnp.bfloat16)

    def unit_pair(tensor):
        square = (tensor * tensor).astype(jnp.bfloat16)
        return tensor * lax.rsqrt(
            jnp.dot(square, average, preferred_element_type=jnp.float32) + 1e-06
        )

    def product(left, right):
        return jnp.dot(left, right, preferred_element_type=jnp.float32)

    def against(left, right):
        return lax.dot_general(
            left, right, (((1,), (1,)), ((), ())), preferred_element_type=jnp.float32
        )

    def diagonal(scores):
        rows_in, lanes_in = scores.shape[0] // 2, scores.shape[1] // 2
        empty = jnp.zeros((rows_in, lanes_in), jnp.float32)
        upper = jnp.concatenate([jnp.exp2(scores[:rows_in, :lanes_in]), empty], axis=1)
        lower = jnp.concatenate([empty, jnp.exp2(scores[rows_in:, lanes_in:])], axis=1)
        return jnp.concatenate([upper, lower], axis=0).astype(jnp.bfloat16)

    def wall_wait(layer):
        for chunk in (at_twin, up_twin, down_twin, far_twin):
            for piece in range(2):
                wall_arrived(layer, chunk, piece)

    def encode(batch, layer):
        normed[...] = (unit(hidden[batch]) * gain_ref[pl.ds(layer, 1)]).astype(jnp.bfloat16)
        for p in range(group // 2):
            lanes = pl.ds(p * pair, pair)
            query = unit_pair(product(normed[...], wall[layer, 0, :, lanes])) * scale
            key = unit_pair(product(normed[...], wall[layer, 1, :, lanes]))
            value = product(normed[...], wall[layer, 2, :, lanes])
            for h in range(2):
                here = slice(h * head, (h + 1) * head)
                stack = pl.ds((2 * p + h) * positions, positions)
                enc_q[stack] = query[:, here].astype(jnp.bfloat16)
                enc_k[stack] = key[:, here].astype(jnp.bfloat16)
                enc_v[stack, pl.ds(0, head)] = value[:, here].astype(jnp.bfloat16)
        for p in range(group // 2):
            stack = pl.ds(2 * p * positions, 2 * positions)
            mixed = product(diagonal(against(enc_q[stack], enc_k[stack])), enc_v[stack])
            mixed = (mixed[:, :head] / mixed[:, head:]).astype(jnp.bfloat16)
            attended[:, pl.ds(p * pair, head)] = mixed[:positions]
            attended[:, pl.ds(p * pair + head, head)] = mixed[positions:]
        for t in range(features // 256):
            lanes = pl.ds(t * 256, 256)
            hidden[batch, :, lanes] += product(attended[...], wout[layer, :, lanes])

    half = positions // 2

    def chunk_place(batch, chunk, piece):
        return chunks.at[
            batch, chunk // sections, pl.ds(lax.rem(chunk, sections) * positions + piece * half, half)
        ]

    def ship(number, batch, chunk, piece, device):
        place = chunk_place(batch, chunk, piece)
        remote(
            place, place, chunk_send.at[batch, number], chunk_recv.at[batch, chunk, piece], device
        ).start()

    def arrived(batch, chunk, piece):
        place = chunk_place(batch, chunk, piece)
        remote(
            place, place, chunk_send.at[batch, 0], chunk_recv.at[batch, chunk, piece], to_twin
        ).wait_recv()

    def finish(batch):
        encoded = (unit(hidden[batch]) * final_ref[...]).astype(jnp.bfloat16)
        chunks[batch, y, pl.ds(pl.multiple_of(c * positions, positions), positions)] = encoded
        for piece in range(2):
            ship(piece, batch, me, piece, to_up)
            ship(2 + piece, batch, me, 1 - piece, to_down)
        for piece in range(2):
            ship(4 + piece, batch, me, piece, to_twin)

    def relay_near(batch):
        arrived(batch, at_down, 0)
        ship(6, batch, at_down, 0, to_up)
        ship(7, batch, at_down, 0, to_twin)
        arrived(batch, at_up, 1)
        ship(8, batch, at_up, 1, to_down)
        ship(9, batch, at_up, 1, to_twin)
        arrived(batch, at_down, 1)
        ship(10, batch, at_down, 1, to_twin)
        arrived(batch, at_up, 0)
        ship(11, batch, at_up, 0, to_twin)

    def relay_far(batch):
        for piece in range(2):
            arrived(batch, at_far, piece)
            ship(12 + piece, batch, at_far, piece, to_twin)

    def twin_wait(batch, chunk):
        for piece in range(2):
            arrived(batch, chunk, piece)

    def cross(batch, chip):
        tokens_here = chunks.at[batch, chip]
        for p in range(heads_local // 2):
            lanes = pl.ds(p * pair, pair)
            key = unit_pair(product(tokens_here[...], kv[0, :, lanes]))
            key_s[:, lanes] = key.astype(jnp.bfloat16)
            value = product(tokens_here[...], kv[1, :, lanes]).astype(jnp.bfloat16)
            value_s[:, pl.ds(2 * p * pair, head)] = value[:, :head]
            value_s[:, pl.ds((2 * p + 1) * pair, head)] = value[:, head:]
        one = batch * group + chip * sections
        first_block = plan_ref[batches * group + one]
        second_block = plan_ref[batches * group + one + 1]
        for h in range(heads_local):
            lanes = pl.ds(h * head, head)
            query = jnp.concatenate(
                [queries[first_block, :, lanes], queries[second_block, :, lanes]], axis=0
            )
            mixed = product(
                diagonal(against(query, key_s[:, lanes])), value_s[:, pl.ds(h * pair, pair)]
            )
            sums[one, :, pl.ds(h * pair, pair)] = mixed[:BL]
            sums[one + 1, :, pl.ds(h * pair, pair)] = mixed[BL:]

    give_wait(0)
    part_start(0)
    wall_near(1)
    out_copy.wait()
    wall_wait(0)
    part_wait(0)
    encode(0, 0)
    lax.fori_loop(0, shards, keep_early, 0)
    wall_far(1)
    give_wait(1)
    part_start(1)
    wall_wait(1)
    encode(0, 1)
    finish(0)
    part_wait(1)
    encode(1, 0)
    encode(1, 1)
    finish(1)

    def step(number, carry):
        @pl.when(number == 0)
        def _():
            twin_wait(0, at_twin)

        @pl.when(number == 1)
        def _():
            relay_near(0)
            twin_wait(1, at_twin)

        @pl.when(number == 2)
        def _():
            twin_wait(0, down_twin)

        @pl.when(number == 3)
        def _():
            twin_wait(0, up_twin)
            relay_far(0)

        @pl.when(number == 4)
        def _():
            relay_near(1)
            twin_wait(0, far_twin)

        @pl.when(number == 5)
        def _():
            twin_wait(1, down_twin)

        @pl.when(number == 6)
        def _():
            relay_far(1)
            twin_wait(1, up_twin)

        @pl.when(number == 7)
        def _():
            twin_wait(1, far_twin)

        batch = jnp.where(number == 1, 1, jnp.where(number >= 5, 1, 0))
        turn = jnp.where(number < 2, 0, jnp.where(number < 5, number - 1, number - 4))
        chip = jnp.where(
            turn == 0, y, jnp.where(turn == 1, down, jnp.where(turn == 2, up, far))
        )
        cross(batch, chip)
        return carry

    lax.fori_loop(0, batches * chips, step, 0)

    def combine(block, carry):
        at = 2 * batches * group + 2 * block
        one, two = plan_ref[at], plan_ref[at + 1]
        alive = (live_ref[block] > 1).astype(jnp.float32)
        span = pl.ds(pl.multiple_of(block * BL, BL), BL)
        for h in range(heads_local):
            lanes = pl.ds(h * pair, pair)
            mixed = sums[one, :, lanes] + sums[two, :, lanes] * alive
            mix_ref[span, pl.ds(h * head, head)] = (mixed[:, :head] / mixed[:, head:]).astype(
                jnp.bfloat16
            )
        return carry

    lax.fori_loop(0, blocks, combine, 0)
    for batch in range(batches):
        for number in range(14):
            place = chunk_place(batch, me, 0)
            remote(
                place, place, chunk_send.at[batch, number], chunk_recv.at[batch, me, 0], to_twin
            ).wait_send()
    for copy in sent:
        copy.wait_send()


def retrieve(shards, group, cap, ask, plan, data, live, gain, final, query, own, out, kv):
    positions, per_shard, head = data.shape
    layers, features = gain.shape
    batches = 2
    blocks = live.shape[0]
    tokens = query.shape[0]
    chips = group // 2
    dma = pltpu.SemaphoreType.DMA
    bf16, f32 = jnp.bfloat16, jnp.float32
    return pl.pallas_call(
        functools.partial(kernel, shards, group, cap, 3.0 / math.sqrt(head) * math.log2(math.e)),
        out_shape=jax.ShapeDtypeStruct(query.shape, bf16),
        in_specs=[VMEM, SMEM, VMEM, SMEM, VMEM, VMEM, VMEM, ANY, ANY, ANY],
        out_specs=VMEM,
        scratch_shapes=[
            pltpu.VMEM((per_shard, positions, head), bf16),
            pltpu.VMEM((shards, 1, 128), jnp.int32),
            pltpu.SMEM((shards, 1, 128), jnp.int32),
            pltpu.VMEM((shards, cap, positions, head), bf16),
            pltpu.VMEM((shards, cap // 2, positions, head), bf16),
            pltpu.VMEM((shards, cap, positions, head), bf16),
            pltpu.VMEM((batches, group, positions, head), bf16),
            pltpu.VMEM((batches, group, positions, head), bf16),
            pltpu.VMEM(own.shape, bf16),
            pltpu.VMEM((layers, 3, features, features), bf16),
            pltpu.VMEM(out.shape, bf16),
            pltpu.VMEM(kv.shape, bf16),
            pltpu.VMEM((2, features, kv.shape[2]), bf16),
            pltpu.VMEM((batches, positions, features), f32),
            pltpu.VMEM((positions, features), bf16),
            pltpu.VMEM((positions, features), bf16),
            pltpu.VMEM((tokens + BL, head), f32),
            pltpu.VMEM((blocks, BL, query.shape[1]), bf16),
            pltpu.VMEM((group * positions, head), bf16),
            pltpu.VMEM((group * positions, head), bf16),
            pltpu.VMEM((group * positions, 2 * head), bf16),
            pltpu.VMEM((2 * positions, group * head), bf16),
            pltpu.VMEM((2 * positions, group * 2 * head), bf16),
            pltpu.VMEM((batches, chips, 2 * positions, features), bf16),
            pltpu.VMEM((batches * group, BL, 2 * query.shape[1]), f32),
            dma((shards,)),
            dma((shards,)),
            dma((batches, shards)),
            dma((batches, shards)),
            dma((batches, group)),
            dma((batches, group)),
            dma,
            dma,
            dma,
            dma,
            dma((layers, 14)),
            dma((layers, group, 2)),
            dma((batches, 14)),
            dma((batches, group, 2)),
        ],
        compiler_params=pltpu.CompilerParams(
            collective_id=0, has_side_effects=True, vmem_limit_bytes=60 * 2**20
        ),
    )(ask, plan, data, live, gain, final, query, own, out, kv)


def on_device(
    queries,
    database,
    neighbour_ids,
    live_counts,
    entry_rows,
    enc_gain,
    enc_qkv,
    enc_out,
    final_gain,
    kv_weight,
):
    shards = lax.axis_size("db")
    group = lax.axis_size(GROUP)
    per_shard = database.shape[1]
    wanted = neighbour_ids.reshape(-1)
    requests = wanted.shape[0]
    capacity = max(2, (requests + shards - 1) // shards)
    located = jnp.take(entry_rows, wanted)
    holder = located // per_shard
    within = located % per_shard
    ordinal = jnp.arange(requests)
    before = (holder[:, None] == holder[None, :]) & (ordinal[None, :] < ordinal[:, None])
    standing = jnp.sum(before.astype(jnp.int32), axis=1)
    target = holder * capacity + standing
    early = standing < capacity // 2
    earlier = jnp.sum((early[None, :] & (ordinal[None, :] < ordinal[:, None])).astype(jnp.int32), axis=1)
    batch_size = requests // 2
    place = jnp.where(
        early & (earlier < batch_size),
        earlier,
        batch_size + ordinal - jnp.minimum(earlier, batch_size),
    )
    seated = (place[None, :] == ordinal[:, None]).astype(jnp.int32)
    block_of = ordinal // neighbour_ids.shape[1]
    plan = jnp.concatenate(
        [jnp.sum(seated * target[None, :], axis=1), jnp.sum(seated * block_of[None, :], axis=1), place]
    )
    buckets = jnp.arange(shards)[:, None] * capacity + jnp.arange(128)[None, :]
    inside = jnp.arange(128)[None, :, None] < capacity
    matched = ((target[None, None, :] == buckets[:, :, None]) & inside).astype(jnp.int32)
    outgoing = jnp.sum(matched * within[None, None, :], axis=2).reshape(shards, 1, 128)
    mixed = retrieve(
        shards,
        group,
        capacity,
        outgoing,
        plan,
        database,
        live_counts,
        enc_gain,
        final_gain.reshape(1, -1),
        queries,
        enc_qkv.transpose(0, 2, 1, 3),
        enc_out,
        kv_weight,
    )
    return lax.pad(mixed, jnp.zeros((), mixed.dtype), ((BL - 1, 1 - BL, 0), (0, 0, 0)))


def solution(mesh):
    return jax.shard_map(
        on_device,
        mesh=mesh,
        in_specs=(
            P("db", GROUP),
            P(None, "db", GROUP),
            P("db", None),
            P("db"),
            P(),
            P(),
            P(None, None, None, GROUP),
            P(),
            P(),
            P(None, None, GROUP),
        ),
        out_specs=P("db", GROUP),
        check_vma=False,
    )
```

```python
import functools
import math

import jax
import jax.numpy as jnp
from jax import lax
from jax.experimental import pallas as pl
from jax.experimental.pallas import tpu as pltpu
from jax.sharding import PartitionSpec as P

BL = 64
GROUP = ("mp", "section")
MESH = pl.DeviceIdType.MESH
VMEM = pl.BlockSpec(memory_space=pltpu.VMEM)
SMEM = pl.BlockSpec(memory_space=pltpu.SMEM)
ANY = pl.BlockSpec(memory_space=pl.ANY)


def unit(tensor):
    return tensor * lax.rsqrt(jnp.mean(tensor * tensor, axis=-1, keepdims=True) + 1e-06)


def remote(src, dst, send_sem, recv_sem, device):
    return pltpu.make_async_remote_copy(
        src_ref=src,
        dst_ref=dst,
        send_sem=send_sem,
        recv_sem=recv_sem,
        device_id=device,
        device_id_type=MESH,
    )


def kernel(
    shards,
    group,
    cap,
    scale,
    ask_ref,
    plan_ref,
    data_ref,
    live_ref,
    gain_ref,
    final_ref,
    query_ref,
    own_hbm,
    out_hbm,
    kv_hbm,
    mix_ref,
    base,
    asked,
    asked_s,
    send,
    early,
    both,
    rows,
    parts,
    own,
    wall,
    wout,
    kv_raw,
    kv,
    hidden,
    normed,
    attended,
    stage,
    queries,
    enc_q,
    enc_k,
    enc_v,
    key_s,
    value_s,
    chunks,
    sums,
    ask_send,
    ask_recv,
    row_send,
    row_recv,
    part_send,
    part_recv,
    asked_sem,
    own_sem,
    out_sem,
    kv_sem,
    wall_send,
    wall_recv,
    side_send,
    side_recv,
    chunk_send,
    chunk_recv,
):
    sections = 2
    chips = group // sections
    db = lax.axis_index("db")
    y = lax.axis_index("mp")
    c = lax.axis_index("section")
    me = y * sections + c
    up, down, far = lax.rem(y + 1, chips), lax.rem(y + chips - 1, chips), lax.rem(y + 2, chips)
    to_up, to_down, to_twin = {"mp": up}, {"mp": down}, {"section": 1 - c}
    at_up, at_down, at_far = up * sections + c, down * sections + c, far * sections + c
    at_twin = y * sections + 1 - c
    up_twin, down_twin, far_twin = (place * sections + 1 - c for place in (up, down, far))

    layers, features = gain_ref.shape
    positions, head = base.shape[1], base.shape[2]
    batches = rows.shape[0]
    first = cap // batches
    pair = 2 * head
    blocks = live_ref.shape[0]

    own_copy = pltpu.make_async_copy(own_hbm, own, own_sem)
    out_copy = pltpu.make_async_copy(out_hbm, wout, out_sem)
    kv_copy = pltpu.make_async_copy(kv_hbm, kv_raw, kv_sem)
    for copy in (own_copy, out_copy, kv_copy):
        copy.start()

    def db_at(k):
        return {"db": lax.rem(db + k, shards)}

    def group_at(k):
        other = lax.rem(me + k, group)
        return other, {"mp": other // sections, "section": lax.rem(other, sections)}

    barrier = pltpu.get_barrier_semaphore()

    def greet_db(k, carry):
        pl.semaphore_signal(barrier, inc=1, device_id=db_at(k), device_id_type=MESH)
        return carry

    def greet_group(k, carry):
        pl.semaphore_signal(barrier, inc=1, device_id=group_at(k)[1], device_id_type=MESH)
        return carry

    lax.fori_loop(1, shards, greet_db, 0)
    lax.fori_loop(1, group, greet_group, 0)
    mine = pl.ds(pl.multiple_of(me * head, head), head)
    own_copy.wait()
    for layer in range(layers):
        wall[layer, :, :, mine] = own[layer]
    base[...] = jnp.transpose(data_ref[...], (1, 0, 2))
    pl.semaphore_wait(barrier, shards + group - 2)

    def ask(k):
        other = lax.rem(db + k, shards)
        return remote(ask_ref.at[other], asked.at[db], ask_send.at[k], ask_recv.at[k], db_at(k))

    def ask_start(k, carry):
        ask(k).start()
        return carry

    lax.fori_loop(1, shards, ask_start, 0)
    asked[pl.ds(db, 1)] = ask_ref[pl.ds(db, 1)]

    half_rows = features // 2

    def ring_types(layer):
        return pl.ds(2, 1) if layer else pl.ds(0, 3)

    def wall_place(layer, chunk, piece):
        return wall.at[
            layer,
            ring_types(layer),
            pl.ds(piece * half_rows, half_rows),
            pl.ds(pl.multiple_of(chunk * head, head), head),
        ]

    def wall_ship(number, layer, chunk, piece, device, local=False):
        place = wall_place(layer, chunk, piece)
        source = own.at[layer, ring_types(layer), pl.ds(piece * half_rows, half_rows), :] if local else place
        copy = remote(
            source, place, wall_send.at[layer, number], wall_recv.at[layer, chunk, piece], device
        )
        copy.start()
        return copy

    def wall_arrived(layer, chunk, piece):
        place = wall_place(layer, chunk, piece)
        remote(
            place, place, wall_send.at[layer, 0], wall_recv.at[layer, chunk, piece], to_twin
        ).wait_recv()

    sent = []

    def wall_own(layer):
        for piece in range(2):
            sent.append(wall_ship(piece, layer, me, piece, to_up, True))
            sent.append(wall_ship(2 + piece, layer, me, 1 - piece, to_down, True))
        for piece in range(2):
            sent.append(wall_ship(4 + piece, layer, me, piece, to_twin, True))

    def wall_near(layer):
        wall_arrived(layer, at_down, 0)
        sent.append(wall_ship(6, layer, at_down, 0, to_up))
        sent.append(wall_ship(7, layer, at_down, 0, to_twin))
        wall_arrived(layer, at_up, 1)
        sent.append(wall_ship(8, layer, at_up, 1, to_down))
        sent.append(wall_ship(9, layer, at_up, 1, to_twin))
        wall_arrived(layer, at_down, 1)
        sent.append(wall_ship(10, layer, at_down, 1, to_twin))
        wall_arrived(layer, at_up, 0)
        sent.append(wall_ship(11, layer, at_up, 0, to_twin))

    def wall_far(layer):
        for piece in range(2):
            wall_arrived(layer, at_far, piece)
            sent.append(wall_ship(12 + piece, layer, at_far, piece, to_twin))

    depth = max(1, shards // 4)
    columns = shards // depth
    x, z = db // depth, lax.rem(db, depth)
    quarter_rows = features // columns

    def side_place(chunk, quarter):
        return wall.at[
            1,
            pl.ds(0, 2),
            pl.ds(quarter * quarter_rows, quarter_rows),
            pl.ds(pl.multiple_of(chunk * head, head), head),
        ]

    def side_ship(number, chunk, quarter, device, local=False):
        place = side_place(chunk, quarter)
        source = place
        if local:
            source = own.at[1, pl.ds(0, 2), pl.ds(quarter * quarter_rows, quarter_rows), :]
        copy = remote(source, place, side_send.at[number], side_recv.at[chunk, quarter], device)
        copy.start()
        sent.append(copy)

    def side_arrived(chunk, quarter):
        place = side_place(chunk, quarter)
        remote(place, place, side_send.at[0], side_recv.at[chunk, quarter], to_twin).wait_recv()

    def side_own():
        for k in range(1, chips):
            side_ship(k - 1, me, x, {"mp": lax.rem(y + k, chips)}, True)
        for quarter in range(columns):
            side_ship(chips - 1 + quarter, me, quarter, to_twin, True)

    side_base = chips - 1 + columns

    def side_spread():
        number = side_base
        for k in range(1, chips):
            chunk = lax.rem(y + k, chips) * sections + c
            side_arrived(chunk, x)
            for step in range(1, columns):
                device = {"db": lax.rem(x + step, columns) * depth + z}
                side_ship(number, chunk, x, device)
                number += 1
            side_ship(number, chunk, x, to_twin)
            number += 1

    def side_relay():
        number = side_base + (chips - 1) * columns
        for k in range(1, chips):
            chunk = lax.rem(y + k, chips) * sections + c
            for step in range(1, columns):
                quarter = lax.rem(x + step, columns)
                side_arrived(chunk, quarter)
                side_ship(number, chunk, quarter, to_twin)
                number += 1

    def side_wait():
        for k in range(chips):
            for quarter in range(columns):
                side_arrived(lax.rem(y + k, chips) * sections + 1 - c, quarter)

    side_own()
    wall_own(0)

    def ask_wait(k, carry):
        ask(k).wait()
        return carry

    lax.fori_loop(1, shards, ask_wait, 0)
    to_scalar = pltpu.make_async_copy(asked, asked_s, asked_sem)
    to_scalar.start()
    to_scalar.wait()

    def give(k, batch):
        other = lax.rem(db + k, shards)
        return remote(
            send.at[other, pl.ds(batch * first, first)],
            both.at[db, pl.ds(first, first)] if batch else early.at[db],
            row_send.at[batch, k],
            row_recv.at[batch, k],
            db_at(k),
        )

    for batch in range(batches):

        def pick(k, carry, batch=batch):
            other = lax.rem(db + k, shards)
            for slot in range(batch * first, (batch + 1) * first):
                send[other, slot] = base[asked_s[other, 0, slot]]
            give(k, batch).start()
            return carry

        lax.fori_loop(1, shards, pick, 0)
        if batch == 0:
            side_spread()
    for slot in range(first):
        early[db, slot] = base[asked_s[db, 0, slot]]
        both[db, first + slot] = base[asked_s[db, 0, first + slot]]

    heads_local = query_ref.shape[1] // head
    tokens = query_ref.shape[0]

    def prepare(h, carry):
        lanes = pl.ds(pl.multiple_of(h * head, head), head)
        stage[pl.ds(0, tokens)] = unit(query_ref[:, lanes].astype(jnp.float32)) * scale
        stage[pl.ds(tokens, BL)] = jnp.zeros((BL, head), jnp.float32)
        shifted = stage[pl.ds(BL - 1, tokens)].astype(jnp.bfloat16)
        queries[:, :, lanes] = shifted.reshape(blocks, BL, head)
        return carry

    lax.fori_loop(0, heads_local, prepare, 0)
    kv_copy.wait()

    def split(t, carry):
        span = pl.ds(pl.multiple_of(t * 32, 32), 32)
        kv[:, span, :] = jnp.transpose(kv_raw[span], (1, 0, 2))
        return carry

    lax.fori_loop(0, features // 32, split, 0)
    enc_v[:, pl.ds(head, head)] = jnp.ones((enc_v.shape[0], head), jnp.bfloat16)
    for h in range(heads_local):
        value_s[:, pl.ds(h * pair + head, head)] = jnp.ones((value_s.shape[0], head), jnp.bfloat16)

    wall_near(0)
    wall_own(1)
    wall_far(0)

    def give_wait(batch):
        def one(k, carry):
            give(k, batch).wait()
            return carry

        lax.fori_loop(1, shards, one, 0)

    def part(k, batch):
        other, device = group_at(k)
        return remote(
            rows.at[batch, other],
            parts.at[batch, me],
            part_send.at[batch, k],
            part_recv.at[batch, k],
            device,
        )

    def chosen(batch, number):
        place = plan_ref[batch * group + number]
        holder, slot = place // cap, lax.rem(place, cap)
        return both[holder, slot] if batch else early[holder, slot]

    def keep_early(k, carry):
        both[k, pl.ds(0, first)] = early[k]
        return carry

    def part_start(batch):
        def one(k, carry):
            other = lax.rem(me + k, group)
            rows[batch, other] = chosen(batch, other)
            part(k, batch).start()
            return carry

        lax.fori_loop(1, group, one, 0)
        parts[batch, me] = chosen(batch, me)

    def part_wait(batch):
        def one(k, carry):
            part(k, batch).wait()
            return carry

        lax.fori_loop(1, group, one, 0)
        for source in range(group):
            hidden[batch, :, pl.ds(source * head, head)] = parts[batch, source].astype(jnp.float32)

    same = lax.broadcasted_iota(jnp.int32, (pair, pair), 0) // head == (
        lax.broadcasted_iota(jnp.int32, (pair, pair), 1) // head
    )
    average = jnp.where(same, 1.0 / head, 0.0).astype(jnp.bfloat16)

    def unit_pair(tensor):
        square = (tensor * tensor).astype(jnp.bfloat16)
        return tensor * lax.rsqrt(
            jnp.dot(square, average, preferred_element_type=jnp.float32) + 1e-06
        )

    def product(left, right):
        return jnp.dot(left, right, preferred_element_type=jnp.float32)

    def against(left, right):
        return lax.dot_general(
            left, right, (((1,), (1,)), ((), ())), preferred_element_type=jnp.float32
        )

    def diagonal(scores):
        rows_in, lanes_in = scores.shape[0] // 2, scores.shape[1] // 2
        empty = jnp.zeros((rows_in, lanes_in), jnp.float32)
        upper = jnp.concatenate([jnp.exp2(scores[:rows_in, :lanes_in]), empty], axis=1)
        lower = jnp.concatenate([empty, jnp.exp2(scores[rows_in:, lanes_in:])], axis=1)
        return jnp.concatenate([upper, lower], axis=0).astype(jnp.bfloat16)

    def wall_wait(layer):
        for chunk in (at_twin, up_twin, down_twin, far_twin):
            for piece in range(2):
                wall_arrived(layer, chunk, piece)

    def encode(batch, layer):
        normed[...] = (unit(hidden[batch]) * gain_ref[pl.ds(layer, 1)]).astype(jnp.bfloat16)
        for p in range(group // 2):
            lanes = pl.ds(p * pair, pair)
            query = unit_pair(product(normed[...], wall[layer, 0, :, lanes])) * scale
            key = unit_pair(product(normed[...], wall[layer, 1, :, lanes]))
            value = product(normed[...], wall[layer, 2, :, lanes])
            for h in range(2):
                here = slice(h * head, (h + 1) * head)
                stack = pl.ds((2 * p + h) * positions, positions)
                enc_q[stack] = query[:, here].astype(jnp.bfloat16)
                enc_k[stack] = key[:, here].astype(jnp.bfloat16)
                enc_v[stack, pl.ds(0, head)] = value[:, here].astype(jnp.bfloat16)
        for p in range(group // 2):
            stack = pl.ds(2 * p * positions, 2 * positions)
            mixed = product(diagonal(against(enc_q[stack], enc_k[stack])), enc_v[stack])
            mixed = (mixed[:, :head] / mixed[:, head:]).astype(jnp.bfloat16)
            attended[:, pl.ds(p * pair, head)] = mixed[:positions]
            attended[:, pl.ds(p * pair + head, head)] = mixed[positions:]
        for t in range(features // 256):
            lanes = pl.ds(t * 256, 256)
            hidden[batch, :, lanes] += product(attended[...], wout[layer, :, lanes])

    half = positions // 2

    def chunk_place(batch, chunk, piece):
        return chunks.at[
            batch, chunk // sections, pl.ds(lax.rem(chunk, sections) * positions + piece * half, half)
        ]

    def ship(number, batch, chunk, piece, device):
        place = chunk_place(batch, chunk, piece)
        remote(
            place, place, chunk_send.at[batch, number], chunk_recv.at[batch, chunk, piece], device
        ).start()

    def arrived(batch, chunk, piece):
        place = chunk_place(batch, chunk, piece)
        remote(
            place, place, chunk_send.at[batch, 0], chunk_recv.at[batch, chunk, piece], to_twin
        ).wait_recv()

    def finish(batch):
        encoded = (unit(hidden[batch]) * final_ref[...]).astype(jnp.bfloat16)
        chunks[batch, y, pl.ds(pl.multiple_of(c * positions, positions), positions)] = encoded
        for piece in range(2):
            ship(piece, batch, me, piece, to_up)
            ship(2 + piece, batch, me, 1 - piece, to_down)
        for piece in range(2):
            ship(4 + piece, batch, me, piece, to_twin)

    def relay_near(batch):
        arrived(batch, at_down, 0)
        ship(6, batch, at_down, 0, to_up)
        ship(7, batch, at_down, 0, to_twin)
        arrived(batch, at_up, 1)
        ship(8, batch, at_up, 1, to_down)
        ship(9, batch, at_up, 1, to_twin)
        arrived(batch, at_down, 1)
        ship(10, batch, at_down, 1, to_twin)
        arrived(batch, at_up, 0)
        ship(11, batch, at_up, 0, to_twin)

    def relay_far(batch):
        for piece in range(2):
            arrived(batch, at_far, piece)
            ship(12 + piece, batch, at_far, piece, to_twin)

    def twin_wait(batch, chunk):
        for piece in range(2):
            arrived(batch, chunk, piece)

    def cross(batch, chip):
        tokens_here = chunks.at[batch, chip]
        for p in range(heads_local // 2):
            lanes = pl.ds(p * pair, pair)
            key = unit_pair(product(tokens_here[...], kv[0, :, lanes]))
            key_s[:, lanes] = key.astype(jnp.bfloat16)
            value = product(tokens_here[...], kv[1, :, lanes]).astype(jnp.bfloat16)
            value_s[:, pl.ds(2 * p * pair, head)] = value[:, :head]
            value_s[:, pl.ds((2 * p + 1) * pair, head)] = value[:, head:]
        one = batch * group + chip * sections
        first_block = plan_ref[batches * group + one]
        second_block = plan_ref[batches * group + one + 1]
        for h in range(heads_local):
            lanes = pl.ds(h * head, head)
            query = jnp.concatenate(
                [queries[first_block, :, lanes], queries[second_block, :, lanes]], axis=0
            )
            mixed = product(
                diagonal(against(query, key_s[:, lanes])), value_s[:, pl.ds(h * pair, pair)]
            )
            sums[one, :, pl.ds(h * pair, pair)] = mixed[:BL]
            sums[one + 1, :, pl.ds(h * pair, pair)] = mixed[BL:]

    side_relay()
    give_wait(0)
    part_start(0)
    wall_near(1)
    out_copy.wait()
    wall_wait(0)
    part_wait(0)
    encode(0, 0)
    lax.fori_loop(0, shards, keep_early, 0)
    wall_far(1)
    side_wait()
    wall_wait(1)
    encode(0, 1)
    finish(0)

    def step(number, carry):
        @pl.when(number == 0)
        def _():
            twin_wait(0, at_twin)

        @pl.when(number == 1)
        def _():
            relay_near(0)
            twin_wait(0, down_twin)

        @pl.when(number == 2)
        def _():
            give_wait(1)
            part_start(1)
            twin_wait(0, up_twin)

        @pl.when(number == 3)
        def _():
            relay_far(0)
            part_wait(1)
            encode(1, 0)
            encode(1, 1)
            finish(1)
            twin_wait(0, far_twin)

        @pl.when(number == 4)
        def _():
            twin_wait(1, at_twin)

        @pl.when(number == 5)
        def _():
            relay_near(1)
            twin_wait(1, down_twin)

        @pl.when(number == 6)
        def _():
            relay_far(1)
            twin_wait(1, up_twin)

        @pl.when(number == 7)
        def _():
            twin_wait(1, far_twin)

        batch = number // chips
        turn = lax.rem(number, chips)
        chip = jnp.where(
            turn == 0, y, jnp.where(turn == 1, down, jnp.where(turn == 2, up, far))
        )
        cross(batch, chip)
        return carry

    lax.fori_loop(0, batches * chips, step, 0)

    def combine(block, carry):
        at = 2 * batches * group + 2 * block
        one, two = plan_ref[at], plan_ref[at + 1]
        alive = (live_ref[block] > 1).astype(jnp.float32)
        span = pl.ds(pl.multiple_of(block * BL, BL), BL)
        for h in range(heads_local):
            lanes = pl.ds(h * pair, pair)
            mixed = sums[one, :, lanes] + sums[two, :, lanes] * alive
            mix_ref[span, pl.ds(h * head, head)] = (mixed[:, :head] / mixed[:, head:]).astype(
                jnp.bfloat16
            )
        return carry

    lax.fori_loop(0, blocks, combine, 0)
    for batch in range(batches):
        for number in range(14):
            place = chunk_place(batch, me, 0)
            remote(
                place, place, chunk_send.at[batch, number], chunk_recv.at[batch, me, 0], to_twin
            ).wait_send()
    for copy in sent:
        copy.wait_send()


def retrieve(shards, group, cap, ask, plan, data, live, gain, final, query, own, out, kv):
    positions, per_shard, head = data.shape
    layers, features = gain.shape
    batches = 2
    blocks = live.shape[0]
    tokens = query.shape[0]
    chips = group // 2
    columns = shards // max(1, shards // 4)
    dma = pltpu.SemaphoreType.DMA
    bf16, f32 = jnp.bfloat16, jnp.float32
    return pl.pallas_call(
        functools.partial(kernel, shards, group, cap, 3.0 / math.sqrt(head) * math.log2(math.e)),
        out_shape=jax.ShapeDtypeStruct(query.shape, bf16),
        in_specs=[VMEM, SMEM, VMEM, SMEM, VMEM, VMEM, VMEM, ANY, ANY, ANY],
        out_specs=VMEM,
        scratch_shapes=[
            pltpu.VMEM((per_shard, positions, head), bf16),
            pltpu.VMEM((shards, 1, 128), jnp.int32),
            pltpu.SMEM((shards, 1, 128), jnp.int32),
            pltpu.VMEM((shards, cap, positions, head), bf16),
            pltpu.VMEM((shards, cap // 2, positions, head), bf16),
            pltpu.VMEM((shards, cap, positions, head), bf16),
            pltpu.VMEM((batches, group, positions, head), bf16),
            pltpu.VMEM((batches, group, positions, head), bf16),
            pltpu.VMEM(own.shape, bf16),
            pltpu.VMEM((layers, 3, features, features), bf16),
            pltpu.VMEM(out.shape, bf16),
            pltpu.VMEM(kv.shape, bf16),
            pltpu.VMEM((2, features, kv.shape[2]), bf16),
            pltpu.VMEM((batches, positions, features), f32),
            pltpu.VMEM((positions, features), bf16),
            pltpu.VMEM((positions, features), bf16),
            pltpu.VMEM((tokens + BL, head), f32),
            pltpu.VMEM((blocks, BL, query.shape[1]), bf16),
            pltpu.VMEM((group * positions, head), bf16),
            pltpu.VMEM((group * positions, head), bf16),
            pltpu.VMEM((group * positions, 2 * head), bf16),
            pltpu.VMEM((2 * positions, group * head), bf16),
            pltpu.VMEM((2 * positions, group * 2 * head), bf16),
            pltpu.VMEM((batches, chips, 2 * positions, features), bf16),
            pltpu.VMEM((batches * group, BL, 2 * query.shape[1]), f32),
            dma((shards,)),
            dma((shards,)),
            dma((batches, shards)),
            dma((batches, shards)),
            dma((batches, group)),
            dma((batches, group)),
            dma,
            dma,
            dma,
            dma,
            dma((layers, 14)),
            dma((layers, group, 2)),
            dma((chips - 1 + columns + (chips - 1) * (2 * columns - 1),)),
            dma((group, columns)),
            dma((batches, 14)),
            dma((batches, group, 2)),
        ],
        compiler_params=pltpu.CompilerParams(
            collective_id=0, has_side_effects=True, vmem_limit_bytes=60 * 2**20
        ),
    )(ask, plan, data, live, gain, final, query, own, out, kv)


def on_device(
    queries,
    database,
    neighbour_ids,
    live_counts,
    entry_rows,
    enc_gain,
    enc_qkv,
    enc_out,
    final_gain,
    kv_weight,
):
    shards = lax.axis_size("db")
    group = lax.axis_size(GROUP)
    per_shard = database.shape[1]
    wanted = neighbour_ids.reshape(-1)
    requests = wanted.shape[0]
    capacity = max(2, (requests + shards - 1) // shards)
    located = jnp.take(entry_rows, wanted)
    holder = located // per_shard
    within = located % per_shard
    ordinal = jnp.arange(requests)
    before = (holder[:, None] == holder[None, :]) & (ordinal[None, :] < ordinal[:, None])
    standing = jnp.sum(before.astype(jnp.int32), axis=1)
    target = holder * capacity + standing
    early = standing < capacity // 2
    earlier = jnp.sum((early[None, :] & (ordinal[None, :] < ordinal[:, None])).astype(jnp.int32), axis=1)
    batch_size = requests // 2
    place = jnp.where(
        early & (earlier < batch_size),
        earlier,
        batch_size + ordinal - jnp.minimum(earlier, batch_size),
    )
    seated = (place[None, :] == ordinal[:, None]).astype(jnp.int32)
    block_of = ordinal // neighbour_ids.shape[1]
    plan = jnp.concatenate(
        [jnp.sum(seated * target[None, :], axis=1), jnp.sum(seated * block_of[None, :], axis=1), place]
    )
    buckets = jnp.arange(shards)[:, None] * capacity + jnp.arange(128)[None, :]
    inside = jnp.arange(128)[None, :, None] < capacity
    matched = ((target[None, None, :] == buckets[:, :, None]) & inside).astype(jnp.int32)
    outgoing = jnp.sum(matched * within[None, None, :], axis=2).reshape(shards, 1, 128)
    mixed = retrieve(
        shards,
        group,
        capacity,
        outgoing,
        plan,
        database,
        live_counts,
        enc_gain,
        final_gain.reshape(1, -1),
        queries,
        enc_qkv.transpose(0, 2, 1, 3),
        enc_out,
        kv_weight,
    )
    return lax.pad(mixed, jnp.zeros((), mixed.dtype), ((BL - 1, 1 - BL, 0), (0, 0, 0)))


def solution(mesh):
    return jax.shard_map(
        on_device,
        mesh=mesh,
        in_specs=(
            P("db", GROUP),
            P(None, "db", GROUP),
            P("db", None),
            P("db"),
            P(),
            P(),
            P(None, None, None, GROUP),
            P(),
            P(),
            P(None, None, GROUP),
        ),
        out_specs=P("db", GROUP),
        check_vma=False,
    )
```

```python
import functools
import math

import jax
import jax.numpy as jnp
from jax import lax
from jax.experimental import pallas as pl
from jax.experimental.pallas import tpu as pltpu
from jax.sharding import PartitionSpec as P

BL = 64
GROUP = ("mp", "section")
MESH = pl.DeviceIdType.MESH
VMEM = pl.BlockSpec(memory_space=pltpu.VMEM)
SMEM = pl.BlockSpec(memory_space=pltpu.SMEM)
ANY = pl.BlockSpec(memory_space=pl.ANY)


def unit(tensor):
    return tensor * lax.rsqrt(jnp.mean(tensor * tensor, axis=-1, keepdims=True) + 1e-06)


def remote(src, dst, send_sem, recv_sem, device):
    return pltpu.make_async_remote_copy(
        src_ref=src,
        dst_ref=dst,
        send_sem=send_sem,
        recv_sem=recv_sem,
        device_id=device,
        device_id_type=MESH,
    )


def kernel(
    shards,
    group,
    cap,
    scale,
    ids_ref,
    entry_ref,
    data_ref,
    live_ref,
    gain_ref,
    final_ref,
    query_ref,
    own_hbm,
    out_hbm,
    kv_hbm,
    mix_ref,
    ask_ref,
    plan_ref,
    base,
    asked,
    asked_s,
    send,
    early,
    both,
    rows,
    parts,
    own,
    wall,
    wout,
    kv_raw,
    kv,
    hidden,
    normed,
    attended,
    stage,
    queries,
    enc_q,
    enc_k,
    enc_v,
    key_s,
    value_s,
    chunks,
    sums,
    ask_send,
    ask_recv,
    row_send,
    row_recv,
    part_send,
    part_recv,
    asked_sem,
    own_sem,
    out_sem,
    kv_sem,
    wall_send,
    wall_recv,
    chunk_send,
    chunk_recv,
):
    sections = 2
    chips = group // sections
    db = lax.axis_index("db")
    y = lax.axis_index("mp")
    c = lax.axis_index("section")
    me = y * sections + c
    up, down, far = lax.rem(y + 1, chips), lax.rem(y + chips - 1, chips), lax.rem(y + 2, chips)
    to_up, to_down, to_twin = {"mp": up}, {"mp": down}, {"section": 1 - c}
    at_up, at_down, at_far = up * sections + c, down * sections + c, far * sections + c
    at_twin = y * sections + 1 - c
    up_twin, down_twin, far_twin = (place * sections + 1 - c for place in (up, down, far))

    layers, features = gain_ref.shape
    positions, head = base.shape[1], base.shape[2]
    batches = rows.shape[0]
    first = cap // batches
    pair = 2 * head
    blocks = live_ref.shape[0]

    own_copy = pltpu.make_async_copy(own_hbm, own, own_sem)
    out_copy = pltpu.make_async_copy(out_hbm, wout, out_sem)
    kv_copy = pltpu.make_async_copy(kv_hbm, kv_raw, kv_sem)
    for copy in (own_copy, out_copy, kv_copy):
        copy.start()

    def db_at(k):
        return {"db": lax.rem(db + k, shards)}

    def group_at(k):
        other = lax.rem(me + k, group)
        return other, {"mp": other // sections, "section": lax.rem(other, sections)}

    barrier = pltpu.get_barrier_semaphore()

    def greet_db(k, carry):
        pl.semaphore_signal(barrier, inc=1, device_id=db_at(k), device_id_type=MESH)
        return carry

    def greet_group(k, carry):
        pl.semaphore_signal(barrier, inc=1, device_id=group_at(k)[1], device_id_type=MESH)
        return carry

    lax.fori_loop(1, shards, greet_db, 0)
    lax.fori_loop(1, group, greet_group, 0)
    mine = pl.ds(pl.multiple_of(me * head, head), head)
    own_copy.wait()
    for layer in range(layers):
        wall[layer, :, :, mine] = own[layer]
    base[...] = jnp.transpose(data_ref[...], (1, 0, 2))
    per_shard = base.shape[0]
    slots = ids_ref.shape[1]
    requests = ids_ref.shape[0] * slots
    size = requests // batches
    holders, targets, places = [], [], []
    earlier = jnp.int32(0)
    shard_of = lax.broadcasted_iota(jnp.int32, ask_ref.shape, 0)
    lane_of = lax.broadcasted_iota(jnp.int32, ask_ref.shape, 2)
    table = jnp.zeros(ask_ref.shape, jnp.int32)
    for n in range(requests):
        located = entry_ref[ids_ref[n // slots, n % slots]]
        holder, within = lax.div(located, per_shard), lax.rem(located, per_shard)
        standing = jnp.int32(0)
        for other in holders:
            standing += jnp.where(other == holder, 1, 0)
        is_early = jnp.where(standing < first, jnp.where(earlier < size, 1, 0), 0)
        places.append(
            jnp.minimum(
                jnp.where(is_early == 1, earlier, size + n - jnp.minimum(earlier, size)),
                requests - 1,
            )
        )
        earlier += jnp.where(standing < first, 1, 0)
        holders.append(holder)
        targets.append(holder * cap + jnp.minimum(standing, cap - 1))
        table = jnp.where((shard_of == holder) & (lane_of == standing), within, table)
    ask_ref[...] = table
    for spot in range(requests):
        target, block = jnp.int32(0), jnp.int32(0)
        for n in range(requests):
            target = jnp.where(places[n] == spot, targets[n], target)
            block = jnp.where(places[n] == spot, n // slots, block)
        plan_ref[spot] = target
        plan_ref[requests + spot] = block
        plan_ref[2 * requests + spot] = places[spot]
    pl.semaphore_wait(barrier, shards + group - 2)

    def ask(k):
        other = lax.rem(db + k, shards)
        return remote(ask_ref.at[other], asked.at[db], ask_send.at[k], ask_recv.at[k], db_at(k))

    def ask_start(k, carry):
        ask(k).start()
        return carry

    lax.fori_loop(1, shards, ask_start, 0)
    asked[pl.ds(db, 1)] = ask_ref[pl.ds(db, 1)]

    half_rows = features // 2

    def wall_place(layer, chunk, piece):
        return wall.at[
            layer,
            :,
            pl.ds(piece * half_rows, half_rows),
            pl.ds(pl.multiple_of(chunk * head, head), head),
        ]

    def wall_ship(number, layer, chunk, piece, device, local=False):
        place = wall_place(layer, chunk, piece)
        source = own.at[layer, :, pl.ds(piece * half_rows, half_rows), :] if local else place
        copy = remote(
            source, place, wall_send.at[layer, number], wall_recv.at[layer, chunk, piece], device
        )
        copy.start()
        return copy

    def wall_arrived(layer, chunk, piece):
        place = wall_place(layer, chunk, piece)
        remote(
            place, place, wall_send.at[layer, 0], wall_recv.at[layer, chunk, piece], to_twin
        ).wait_recv()

    sent = []

    def wall_own(layer):
        for piece in range(2):
            sent.append(wall_ship(piece, layer, me, piece, to_up, True))
            sent.append(wall_ship(2 + piece, layer, me, 1 - piece, to_down, True))
        for piece in range(2):
            sent.append(wall_ship(4 + piece, layer, me, piece, to_twin, True))

    def wall_near(layer):
        wall_arrived(layer, at_down, 0)
        sent.append(wall_ship(6, layer, at_down, 0, to_up))
        sent.append(wall_ship(7, layer, at_down, 0, to_twin))
        wall_arrived(layer, at_up, 1)
        sent.append(wall_ship(8, layer, at_up, 1, to_down))
        sent.append(wall_ship(9, layer, at_up, 1, to_twin))
        wall_arrived(layer, at_down, 1)
        sent.append(wall_ship(10, layer, at_down, 1, to_twin))
        wall_arrived(layer, at_up, 0)
        sent.append(wall_ship(11, layer, at_up, 0, to_twin))

    def wall_far(layer):
        for piece in range(2):
            wall_arrived(layer, at_far, piece)
            sent.append(wall_ship(12 + piece, layer, at_far, piece, to_twin))

    wall_own(0)

    def ask_wait(k, carry):
        ask(k).wait()
        return carry

    lax.fori_loop(1, shards, ask_wait, 0)
    to_scalar = pltpu.make_async_copy(asked, asked_s, asked_sem)
    to_scalar.start()
    to_scalar.wait()

    def give(k, batch):
        other = lax.rem(db + k, shards)
        return remote(
            send.at[other, pl.ds(batch * first, first)],
            both.at[db, pl.ds(first, first)] if batch else early.at[db],
            row_send.at[batch, k],
            row_recv.at[batch, k],
            db_at(k),
        )

    for batch in range(batches):

        def pick(k, carry, batch=batch):
            other = lax.rem(db + k, shards)
            for slot in range(batch * first, (batch + 1) * first):
                send[other, slot] = base[asked_s[other, 0, slot]]
            give(k, batch).start()
            return carry

        lax.fori_loop(1, shards, pick, 0)
    for slot in range(first):
        early[db, slot] = base[asked_s[db, 0, slot]]
        both[db, first + slot] = base[asked_s[db, 0, first + slot]]

    heads_local = query_ref.shape[1] // head
    tokens = query_ref.shape[0]

    def prepare(h, carry):
        lanes = pl.ds(pl.multiple_of(h * head, head), head)
        stage[pl.ds(0, tokens)] = unit(query_ref[:, lanes].astype(jnp.float32)) * scale
        stage[pl.ds(tokens, BL)] = jnp.zeros((BL, head), jnp.float32)
        shifted = stage[pl.ds(BL - 1, tokens)].astype(jnp.bfloat16)
        queries[:, :, lanes] = shifted.reshape(blocks, BL, head)
        return carry

    lax.fori_loop(0, heads_local, prepare, 0)
    kv_copy.wait()

    def split(t, carry):
        span = pl.ds(pl.multiple_of(t * 32, 32), 32)
        kv[:, span, :] = jnp.transpose(kv_raw[span], (1, 0, 2))
        return carry

    lax.fori_loop(0, features // 32, split, 0)
    enc_v[:, pl.ds(head, head)] = jnp.ones((enc_v.shape[0], head), jnp.bfloat16)
    for h in range(heads_local):
        value_s[:, pl.ds(h * pair + head, head)] = jnp.ones((value_s.shape[0], head), jnp.bfloat16)

    wall_near(0)
    wall_own(1)
    wall_far(0)

    def give_wait(batch):
        def one(k, carry):
            give(k, batch).wait()
            return carry

        lax.fori_loop(1, shards, one, 0)

    def part(k, batch):
        other, device = group_at(k)
        return remote(
            rows.at[batch, other],
            parts.at[batch, me],
            part_send.at[batch, k],
            part_recv.at[batch, k],
            device,
        )

    def chosen(batch, number):
        place = plan_ref[batch * group + number]
        holder, slot = place // cap, lax.rem(place, cap)
        return both[holder, slot] if batch else early[holder, jnp.minimum(slot, first - 1)]

    def keep_early(k, carry):
        both[k, pl.ds(0, first)] = early[k]
        return carry

    def part_start(batch):
        def one(k, carry):
            other = lax.rem(me + k, group)
            rows[batch, other] = chosen(batch, other)
            part(k, batch).start()
            return carry

        lax.fori_loop(1, group, one, 0)
        parts[batch, me] = chosen(batch, me)

    def part_wait(batch):
        def one(k, carry):
            part(k, batch).wait()
            return carry

        lax.fori_loop(1, group, one, 0)
        for source in range(group):
            hidden[batch, :, pl.ds(source * head, head)] = parts[batch, source].astype(jnp.float32)

    same = lax.broadcasted_iota(jnp.int32, (pair, pair), 0) // head == (
        lax.broadcasted_iota(jnp.int32, (pair, pair), 1) // head
    )
    average = jnp.where(same, 1.0 / head, 0.0).astype(jnp.bfloat16)

    def unit_pair(tensor):
        square = (tensor * tensor).astype(jnp.bfloat16)
        return tensor * lax.rsqrt(
            jnp.dot(square, average, preferred_element_type=jnp.float32) + 1e-06
        )

    def product(left, right):
        return jnp.dot(left, right, preferred_element_type=jnp.float32)

    def against(left, right):
        return lax.dot_general(
            left, right, (((1,), (1,)), ((), ())), preferred_element_type=jnp.float32
        )

    def diagonal(scores):
        rows_in, lanes_in = scores.shape[0] // 2, scores.shape[1] // 2
        empty = jnp.zeros((rows_in, lanes_in), jnp.float32)
        upper = jnp.concatenate([jnp.exp2(scores[:rows_in, :lanes_in]), empty], axis=1)
        lower = jnp.concatenate([empty, jnp.exp2(scores[rows_in:, lanes_in:])], axis=1)
        return jnp.concatenate([upper, lower], axis=0).astype(jnp.bfloat16)

    def wall_wait(layer):
        for chunk in (at_twin, up_twin, down_twin, far_twin):
            for piece in range(2):
                wall_arrived(layer, chunk, piece)

    def encode(batch, layer):
        normed[...] = (unit(hidden[batch]) * gain_ref[pl.ds(layer, 1)]).astype(jnp.bfloat16)
        for p in range(group // 2):
            lanes = pl.ds(p * pair, pair)
            query = unit_pair(product(normed[...], wall[layer, 0, :, lanes])) * scale
            key = unit_pair(product(normed[...], wall[layer, 1, :, lanes]))
            value = product(normed[...], wall[layer, 2, :, lanes])
            for h in range(2):
                here = slice(h * head, (h + 1) * head)
                stack = pl.ds((2 * p + h) * positions, positions)
                enc_q[stack] = query[:, here].astype(jnp.bfloat16)
                enc_k[stack] = key[:, here].astype(jnp.bfloat16)
                enc_v[stack, pl.ds(0, head)] = value[:, here].astype(jnp.bfloat16)
        for p in range(group // 2):
            stack = pl.ds(2 * p * positions, 2 * positions)
            mixed = product(diagonal(against(enc_q[stack], enc_k[stack])), enc_v[stack])
            mixed = (mixed[:, :head] / mixed[:, head:]).astype(jnp.bfloat16)
            attended[:, pl.ds(p * pair, head)] = mixed[:positions]
            attended[:, pl.ds(p * pair + head, head)] = mixed[positions:]
        for t in range(features // 256):
            lanes = pl.ds(t * 256, 256)
            hidden[batch, :, lanes] += product(attended[...], wout[layer, :, lanes])

    half = positions // 2

    def chunk_place(batch, chunk, piece):
        return chunks.at[
            batch, chunk // sections, pl.ds(lax.rem(chunk, sections) * positions + piece * half, half)
        ]

    def ship(number, batch, chunk, piece, device):
        place = chunk_place(batch, chunk, piece)
        remote(
            place, place, chunk_send.at[batch, number], chunk_recv.at[batch, chunk, piece], device
        ).start()

    def arrived(batch, chunk, piece):
        place = chunk_place(batch, chunk, piece)
        remote(
            place, place, chunk_send.at[batch, 0], chunk_recv.at[batch, chunk, piece], to_twin
        ).wait_recv()

    def finish(batch):
        encoded = (unit(hidden[batch]) * final_ref[...]).astype(jnp.bfloat16)
        chunks[batch, y, pl.ds(pl.multiple_of(c * positions, positions), positions)] = encoded
        for piece in range(2):
            ship(piece, batch, me, piece, to_up)
            ship(2 + piece, batch, me, 1 - piece, to_down)
        for piece in range(2):
            ship(4 + piece, batch, me, piece, to_twin)

    def relay_near(batch):
        arrived(batch, at_down, 0)
        ship(6, batch, at_down, 0, to_up)
        ship(7, batch, at_down, 0, to_twin)
        arrived(batch, at_up, 1)
        ship(8, batch, at_up, 1, to_down)
        ship(9, batch, at_up, 1, to_twin)
        arrived(batch, at_down, 1)
        ship(10, batch, at_down, 1, to_twin)
        arrived(batch, at_up, 0)
        ship(11, batch, at_up, 0, to_twin)

    def relay_far(batch):
        for piece in range(2):
            arrived(batch, at_far, piece)
            ship(12 + piece, batch, at_far, piece, to_twin)

    def twin_wait(batch, chunk):
        for piece in range(2):
            arrived(batch, chunk, piece)

    def cross(batch, chip):
        tokens_here = chunks.at[batch, chip]
        for p in range(heads_local // 2):
            lanes = pl.ds(p * pair, pair)
            key = unit_pair(product(tokens_here[...], kv[0, :, lanes]))
            key_s[:, lanes] = key.astype(jnp.bfloat16)
            value = product(tokens_here[...], kv[1, :, lanes]).astype(jnp.bfloat16)
            value_s[:, pl.ds(2 * p * pair, head)] = value[:, :head]
            value_s[:, pl.ds((2 * p + 1) * pair, head)] = value[:, head:]
        one = batch * group + chip * sections
        first_block = plan_ref[batches * group + one]
        second_block = plan_ref[batches * group + one + 1]
        for h in range(heads_local):
            lanes = pl.ds(h * head, head)
            query = jnp.concatenate(
                [queries[first_block, :, lanes], queries[second_block, :, lanes]], axis=0
            )
            mixed = product(
                diagonal(against(query, key_s[:, lanes])), value_s[:, pl.ds(h * pair, pair)]
            )
            sums[one, :, pl.ds(h * pair, pair)] = mixed[:BL]
            sums[one + 1, :, pl.ds(h * pair, pair)] = mixed[BL:]

    give_wait(0)
    part_start(0)
    wall_near(1)
    out_copy.wait()
    wall_wait(0)
    part_wait(0)
    encode(0, 0)
    lax.fori_loop(0, shards, keep_early, 0)
    wall_far(1)
    give_wait(1)
    part_start(1)
    wall_wait(1)
    encode(0, 1)
    finish(0)
    part_wait(1)
    encode(1, 0)
    encode(1, 1)
    finish(1)

    def step(number, carry):
        @pl.when(number == 0)
        def _():
            twin_wait(0, at_twin)

        @pl.when(number == 1)
        def _():
            relay_near(0)
            twin_wait(1, at_twin)

        @pl.when(number == 2)
        def _():
            twin_wait(0, down_twin)

        @pl.when(number == 3)
        def _():
            twin_wait(0, up_twin)
            relay_far(0)

        @pl.when(number == 4)
        def _():
            relay_near(1)
            twin_wait(0, far_twin)

        @pl.when(number == 5)
        def _():
            twin_wait(1, down_twin)

        @pl.when(number == 6)
        def _():
            relay_far(1)
            twin_wait(1, up_twin)

        @pl.when(number == 7)
        def _():
            twin_wait(1, far_twin)

        batch = jnp.where(number == 1, 1, jnp.where(number >= 5, 1, 0))
        turn = jnp.where(number < 2, 0, jnp.where(number < 5, number - 1, number - 4))
        chip = jnp.where(
            turn == 0, y, jnp.where(turn == 1, down, jnp.where(turn == 2, up, far))
        )
        cross(batch, chip)
        return carry

    lax.fori_loop(0, batches * chips, step, 0)

    def combine(h, carry):
        wide = pl.ds(pl.multiple_of(h * pair, pair), pair)
        stage[pl.ds(0, BL)] = jnp.zeros((BL, head), jnp.float32)
        for block in range(blocks):
            one = plan_ref[2 * requests + slots * block]
            two = plan_ref[2 * requests + slots * block + 1]
            alive = (live_ref[block] > 1).astype(jnp.float32)
            mixed = sums[one, :, wide] + sums[two, :, wide] * alive
            stage[pl.ds(BL - 1 + block * BL, BL)] = mixed[:, :head] / mixed[:, head:]
        mix_ref[:, pl.ds(pl.multiple_of(h * head, head), head)] = stage[pl.ds(0, tokens)].astype(
            jnp.bfloat16
        )
        return carry

    lax.fori_loop(0, heads_local, combine, 0)
    for batch in range(batches):
        for number in range(14):
            place = chunk_place(batch, me, 0)
            remote(
                place, place, chunk_send.at[batch, number], chunk_recv.at[batch, me, 0], to_twin
            ).wait_send()
    for copy in sent:
        copy.wait_send()


def retrieve(shards, group, cap, ids, entry_rows, data, live, gain, final, query, own, out, kv):
    positions, per_shard, head = data.shape
    layers, features = gain.shape
    batches = 2
    blocks = live.shape[0]
    tokens = query.shape[0]
    chips = group // 2
    dma = pltpu.SemaphoreType.DMA
    bf16, f32 = jnp.bfloat16, jnp.float32
    return pl.pallas_call(
        functools.partial(kernel, shards, group, cap, 3.0 / math.sqrt(head) * math.log2(math.e)),
        out_shape=jax.ShapeDtypeStruct(query.shape, bf16),
        in_specs=[SMEM, SMEM, VMEM, SMEM, VMEM, VMEM, VMEM, ANY, ANY, ANY],
        out_specs=VMEM,
        scratch_shapes=[
            pltpu.VMEM((shards, 1, 128), jnp.int32),
            pltpu.SMEM((3 * ids.shape[0] * ids.shape[1],), jnp.int32),
            pltpu.VMEM((per_shard, positions, head), bf16),
            pltpu.VMEM((shards, 1, 128), jnp.int32),
            pltpu.SMEM((shards, 1, 128), jnp.int32),
            pltpu.VMEM((shards, cap, positions, head), bf16),
            pltpu.VMEM((shards, cap // 2, positions, head), bf16),
            pltpu.VMEM((shards, cap, positions, head), bf16),
            pltpu.VMEM((batches, group, positions, head), bf16),
            pltpu.VMEM((batches, group, positions, head), bf16),
            pltpu.VMEM(own.shape, bf16),
            pltpu.VMEM((layers, 3, features, features), bf16),
            pltpu.VMEM(out.shape, bf16),
            pltpu.VMEM(kv.shape, bf16),
            pltpu.VMEM((2, features, kv.shape[2]), bf16),
            pltpu.VMEM((batches, positions, features), f32),
            pltpu.VMEM((positions, features), bf16),
            pltpu.VMEM((positions, features), bf16),
            pltpu.VMEM((tokens + BL, head), f32),
            pltpu.VMEM((blocks, BL, query.shape[1]), bf16),
            pltpu.VMEM((group * positions, head), bf16),
            pltpu.VMEM((group * positions, head), bf16),
            pltpu.VMEM((group * positions, 2 * head), bf16),
            pltpu.VMEM((2 * positions, group * head), bf16),
            pltpu.VMEM((2 * positions, group * 2 * head), bf16),
            pltpu.VMEM((batches, chips, 2 * positions, features), bf16),
            pltpu.VMEM((batches * group, BL, 2 * query.shape[1]), f32),
            dma((shards,)),
            dma((shards,)),
            dma((batches, shards)),
            dma((batches, shards)),
            dma((batches, group)),
            dma((batches, group)),
            dma,
            dma,
            dma,
            dma,
            dma((layers, 14)),
            dma((layers, group, 2)),
            dma((batches, 14)),
            dma((batches, group, 2)),
        ],
        compiler_params=pltpu.CompilerParams(
            collective_id=0, has_side_effects=True, vmem_limit_bytes=60 * 2**20
        ),
    )(ids, entry_rows, data, live, gain, final, query, own, out, kv)


def on_device(
    queries,
    database,
    neighbour_ids,
    live_counts,
    entry_rows,
    enc_gain,
    enc_qkv,
    enc_out,
    final_gain,
    kv_weight,
):
    shards = lax.axis_size("db")
    group = lax.axis_size(GROUP)
    requests = neighbour_ids.shape[0] * neighbour_ids.shape[1]
    capacity = max(2, (requests + shards - 1) // shards)
    return retrieve(
        shards,
        group,
        capacity,
        neighbour_ids,
        entry_rows,
        database,
        live_counts,
        enc_gain,
        final_gain.reshape(1, -1),
        queries,
        enc_qkv.transpose(0, 2, 1, 3),
        enc_out,
        kv_weight,
    )


def solution(mesh):
    return jax.shard_map(
        on_device,
        mesh=mesh,
        in_specs=(
            P("db", GROUP),
            P(None, "db", GROUP),
            P("db", None),
            P("db"),
            P(),
            P(),
            P(None, None, None, GROUP),
            P(),
            P(),
            P(None, None, GROUP),
        ),
        out_specs=P("db", GROUP),
        check_vma=False,
    )
```

```python
import functools
import math

import jax
import jax.numpy as jnp
from jax import lax
from jax.experimental import pallas as pl
from jax.experimental.pallas import tpu as pltpu
from jax.sharding import PartitionSpec as P

BL = 64
GROUP = ("mp", "section")
MESH = pl.DeviceIdType.MESH
VMEM = pl.BlockSpec(memory_space=pltpu.VMEM)
SMEM = pl.BlockSpec(memory_space=pltpu.SMEM)
ANY = pl.BlockSpec(memory_space=pl.ANY)


def unit(tensor):
    return tensor * lax.rsqrt(jnp.mean(tensor * tensor, axis=-1, keepdims=True) + 1e-06)


def remote(src, dst, send_sem, recv_sem, device):
    return pltpu.make_async_remote_copy(
        src_ref=src,
        dst_ref=dst,
        send_sem=send_sem,
        recv_sem=recv_sem,
        device_id=device,
        device_id_type=MESH,
    )


def kernel(
    shards,
    group,
    cap,
    scale,
    ids_ref,
    entry_ref,
    data_ref,
    live_ref,
    gain_ref,
    final_ref,
    query_ref,
    own_hbm,
    out_hbm,
    kv_hbm,
    mix_ref,
    ask_ref,
    plan_ref,
    base,
    asked,
    asked_s,
    send,
    early,
    both,
    rows,
    parts,
    own,
    wall,
    wout,
    kv_raw,
    kv,
    hidden,
    normed,
    attended,
    stage,
    queries,
    enc_q,
    enc_k,
    enc_v,
    key_s,
    value_s,
    chunks,
    sums,
    ask_send,
    ask_recv,
    row_send,
    row_recv,
    part_send,
    part_recv,
    asked_sem,
    own_sem,
    out_sem,
    kv_sem,
    wall_send,
    wall_recv,
    chunk_send,
    chunk_recv,
):
    sections = 2
    chips = group // sections
    db = lax.axis_index("db")
    y = lax.axis_index("mp")
    c = lax.axis_index("section")
    me = y * sections + c
    up, down, far = lax.rem(y + 1, chips), lax.rem(y + chips - 1, chips), lax.rem(y + 2, chips)
    to_up, to_down, to_twin = {"mp": up}, {"mp": down}, {"section": 1 - c}
    at_up, at_down, at_far = up * sections + c, down * sections + c, far * sections + c
    at_twin = y * sections + 1 - c
    up_twin, down_twin, far_twin = (place * sections + 1 - c for place in (up, down, far))

    layers, features = gain_ref.shape
    positions, head = base.shape[1], base.shape[2]
    batches = rows.shape[0]
    first = cap // batches
    pair = 2 * head
    blocks = live_ref.shape[0]

    own_copy = pltpu.make_async_copy(own_hbm, own, own_sem)
    out_copy = pltpu.make_async_copy(out_hbm, wout, out_sem)
    kv_copy = pltpu.make_async_copy(kv_hbm, kv_raw, kv_sem)
    for copy in (own_copy, out_copy, kv_copy):
        copy.start()

    def db_at(k):
        return {"db": lax.rem(db + k, shards)}

    def group_at(k):
        other = lax.rem(me + k, group)
        return other, {"mp": other // sections, "section": lax.rem(other, sections)}

    barrier = pltpu.get_barrier_semaphore()

    def greet_db(k, carry):
        pl.semaphore_signal(barrier, inc=1, device_id=db_at(k), device_id_type=MESH)
        return carry

    def greet_group(k, carry):
        pl.semaphore_signal(barrier, inc=1, device_id=group_at(k)[1], device_id_type=MESH)
        return carry

    lax.fori_loop(1, shards, greet_db, 0)
    lax.fori_loop(1, group, greet_group, 0)
    mine = pl.ds(pl.multiple_of(me * head, head), head)
    own_copy.wait()
    for layer in range(layers):
        wall[layer, :, :, mine] = own[layer]
    base[...] = jnp.transpose(data_ref[...], (1, 0, 2))
    per_shard = base.shape[0]
    slots = ids_ref.shape[1]
    requests = ids_ref.shape[0] * slots
    size = requests // batches
    holders, targets, places = [], [], []
    earlier = jnp.int32(0)
    shard_of = lax.broadcasted_iota(jnp.int32, ask_ref.shape, 0)
    lane_of = lax.broadcasted_iota(jnp.int32, ask_ref.shape, 2)
    table = jnp.zeros(ask_ref.shape, jnp.int32)
    for n in range(requests):
        located = entry_ref[ids_ref[n // slots, n % slots]]
        holder, within = lax.div(located, per_shard), lax.rem(located, per_shard)
        standing = jnp.int32(0)
        for other in holders:
            standing += jnp.where(other == holder, 1, 0)
        is_early = jnp.where(standing < first, jnp.where(earlier < size, 1, 0), 0)
        places.append(
            jnp.minimum(
                jnp.where(is_early == 1, earlier, size + n - jnp.minimum(earlier, size)),
                requests - 1,
            )
        )
        earlier += jnp.where(standing < first, 1, 0)
        holders.append(holder)
        targets.append(holder * cap + jnp.minimum(standing, cap - 1))
        table = jnp.where((shard_of == holder) & (lane_of == standing), within, table)
    ask_ref[...] = table
    for spot in range(requests):
        target, block = jnp.int32(0), jnp.int32(0)
        for n in range(requests):
            target = jnp.where(places[n] == spot, targets[n], target)
            block = jnp.where(places[n] == spot, n // slots, block)
        plan_ref[spot] = target
        plan_ref[requests + spot] = block
        plan_ref[2 * requests + spot] = places[spot]
    pl.semaphore_wait(barrier, shards + group - 2)

    def ask(k):
        other = lax.rem(db + k, shards)
        return remote(ask_ref.at[other], asked.at[db], ask_send.at[k], ask_recv.at[k], db_at(k))

    def ask_start(k, carry):
        ask(k).start()
        return carry

    lax.fori_loop(1, shards, ask_start, 0)
    asked[pl.ds(db, 1)] = ask_ref[pl.ds(db, 1)]

    half_rows = features // 2

    def wall_place(layer, chunk, piece):
        return wall.at[
            layer,
            :,
            pl.ds(piece * half_rows, half_rows),
            pl.ds(pl.multiple_of(chunk * head, head), head),
        ]

    def wall_ship(number, layer, chunk, piece, device, local=False):
        place = wall_place(layer, chunk, piece)
        source = own.at[layer, :, pl.ds(piece * half_rows, half_rows), :] if local else place
        copy = remote(
            source, place, wall_send.at[layer, number], wall_recv.at[layer, chunk, piece], device
        )
        copy.start()
        return copy

    def wall_arrived(layer, chunk, piece):
        place = wall_place(layer, chunk, piece)
        remote(
            place, place, wall_send.at[layer, 0], wall_recv.at[layer, chunk, piece], to_twin
        ).wait_recv()

    sent = []

    def wall_own(layer):
        for piece in range(2):
            sent.append(wall_ship(piece, layer, me, piece, to_up, True))
            sent.append(wall_ship(2 + piece, layer, me, 1 - piece, to_down, True))
        for piece in range(2):
            sent.append(wall_ship(4 + piece, layer, me, piece, to_twin, True))

    def wall_near(layer):
        wall_arrived(layer, at_down, 0)
        sent.append(wall_ship(6, layer, at_down, 0, to_up))
        sent.append(wall_ship(7, layer, at_down, 0, to_twin))
        wall_arrived(layer, at_up, 1)
        sent.append(wall_ship(8, layer, at_up, 1, to_down))
        sent.append(wall_ship(9, layer, at_up, 1, to_twin))
        wall_arrived(layer, at_down, 1)
        sent.append(wall_ship(10, layer, at_down, 1, to_twin))
        wall_arrived(layer, at_up, 0)
        sent.append(wall_ship(11, layer, at_up, 0, to_twin))

    def wall_far(layer):
        for piece in range(2):
            wall_arrived(layer, at_far, piece)
            sent.append(wall_ship(12 + piece, layer, at_far, piece, to_twin))

    wall_own(0)

    def ask_wait(k, carry):
        ask(k).wait()
        return carry

    lax.fori_loop(1, shards, ask_wait, 0)
    to_scalar = pltpu.make_async_copy(asked, asked_s, asked_sem)
    to_scalar.start()
    to_scalar.wait()

    def give(k, batch):
        other = lax.rem(db + k, shards)
        return remote(
            send.at[other, pl.ds(batch * first, first)],
            both.at[db, pl.ds(first, first)] if batch else early.at[db],
            row_send.at[batch, k],
            row_recv.at[batch, k],
            db_at(k),
        )

    for batch in range(batches):

        def pick(k, carry, batch=batch):
            other = lax.rem(db + k, shards)
            for slot in range(batch * first, (batch + 1) * first):
                send[other, slot] = base[asked_s[other, 0, slot]]
            give(k, batch).start()
            return carry

        lax.fori_loop(1, shards, pick, 0)
    for slot in range(first):
        early[db, slot] = base[asked_s[db, 0, slot]]
        both[db, first + slot] = base[asked_s[db, 0, first + slot]]

    heads_local = query_ref.shape[1] // head
    tokens = query_ref.shape[0]

    def prepare(h, carry):
        lanes = pl.ds(pl.multiple_of(h * head, head), head)
        stage[pl.ds(0, tokens)] = unit(query_ref[:, lanes].astype(jnp.float32)) * scale
        stage[pl.ds(tokens, BL)] = jnp.zeros((BL, head), jnp.float32)
        shifted = stage[pl.ds(BL - 1, tokens)].astype(jnp.bfloat16)
        queries[:, :, lanes] = shifted.reshape(blocks, BL, head)
        return carry

    lax.fori_loop(0, heads_local, prepare, 0)
    kv_copy.wait()

    def split(t, carry):
        span = pl.ds(pl.multiple_of(t * 32, 32), 32)
        kv[:, span, :] = jnp.transpose(kv_raw[span], (1, 0, 2))
        return carry

    lax.fori_loop(0, features // 32, split, 0)
    enc_v[:, pl.ds(head, head)] = jnp.ones((enc_v.shape[0], head), jnp.bfloat16)
    for h in range(heads_local):
        value_s[:, pl.ds(h * pair + head, head)] = jnp.ones((value_s.shape[0], head), jnp.bfloat16)

    wall_near(0)
    wall_own(1)
    wall_far(0)

    def give_wait(batch):
        def one(k, carry):
            give(k, batch).wait()
            return carry

        lax.fori_loop(1, shards, one, 0)

    def part(k, batch):
        other, device = group_at(k)
        return remote(
            rows.at[batch, other],
            parts.at[batch, me],
            part_send.at[batch, k],
            part_recv.at[batch, k],
            device,
        )

    def chosen(batch, number):
        place = plan_ref[batch * group + number]
        holder, slot = place // cap, lax.rem(place, cap)
        return both[holder, slot] if batch else early[holder, jnp.minimum(slot, first - 1)]

    def keep_early(k, carry):
        both[k, pl.ds(0, first)] = early[k]
        return carry

    def part_start(batch):
        def one(k, carry):
            other = lax.rem(me + k, group)
            rows[batch, other] = chosen(batch, other)
            part(k, batch).start()
            return carry

        lax.fori_loop(1, group, one, 0)
        parts[batch, me] = chosen(batch, me)

    def part_wait(batch):
        def one(k, carry):
            part(k, batch).wait()
            return carry

        lax.fori_loop(1, group, one, 0)
        for source in range(group):
            hidden[batch, :, pl.ds(source * head, head)] = parts[batch, source].astype(jnp.float32)

    same = lax.broadcasted_iota(jnp.int32, (pair, pair), 0) // head == (
        lax.broadcasted_iota(jnp.int32, (pair, pair), 1) // head
    )
    average = jnp.where(same, 1.0 / head, 0.0).astype(jnp.bfloat16)

    def unit_pair(tensor):
        square = (tensor * tensor).astype(jnp.bfloat16)
        return tensor * lax.rsqrt(
            jnp.dot(square, average, preferred_element_type=jnp.float32) + 1e-06
        )

    def product(left, right):
        return jnp.dot(left, right, preferred_element_type=jnp.float32)

    def against(left, right):
        return lax.dot_general(
            left, right, (((1,), (1,)), ((), ())), preferred_element_type=jnp.float32
        )

    def diagonal(scores):
        rows_in, lanes_in = scores.shape[0] // 2, scores.shape[1] // 2
        empty = jnp.zeros((rows_in, lanes_in), jnp.float32)
        upper = jnp.concatenate([jnp.exp2(scores[:rows_in, :lanes_in]), empty], axis=1)
        lower = jnp.concatenate([empty, jnp.exp2(scores[rows_in:, lanes_in:])], axis=1)
        return jnp.concatenate([upper, lower], axis=0).astype(jnp.bfloat16)

    def wall_wait(layer):
        for chunk in (at_twin, up_twin, down_twin, far_twin):
            for piece in range(2):
                wall_arrived(layer, chunk, piece)

    def encode(batch, layer):
        normed[...] = (unit(hidden[batch]) * gain_ref[pl.ds(layer, 1)]).astype(jnp.bfloat16)
        for p in range(group // 2):
            lanes = pl.ds(p * pair, pair)
            query = unit_pair(product(normed[...], wall[layer, 0, :, lanes])) * scale
            key = unit_pair(product(normed[...], wall[layer, 1, :, lanes]))
            value = product(normed[...], wall[layer, 2, :, lanes])
            for h in range(2):
                here = slice(h * head, (h + 1) * head)
                stack = pl.ds((2 * p + h) * positions, positions)
                enc_q[stack] = query[:, here].astype(jnp.bfloat16)
                enc_k[stack] = key[:, here].astype(jnp.bfloat16)
                enc_v[stack, pl.ds(0, head)] = value[:, here].astype(jnp.bfloat16)
        for p in range(group // 2):
            stack = pl.ds(2 * p * positions, 2 * positions)
            mixed = product(diagonal(against(enc_q[stack], enc_k[stack])), enc_v[stack])
            mixed = (mixed[:, :head] / mixed[:, head:]).astype(jnp.bfloat16)
            attended[:, pl.ds(p * pair, head)] = mixed[:positions]
            attended[:, pl.ds(p * pair + head, head)] = mixed[positions:]
        for t in range(features // 256):
            lanes = pl.ds(t * 256, 256)
            hidden[batch, :, lanes] += product(attended[...], wout[layer, :, lanes])

    half = positions // 2

    def chunk_place(batch, chunk, piece):
        return chunks.at[
            batch, chunk // sections, pl.ds(lax.rem(chunk, sections) * positions + piece * half, half)
        ]

    def ship(number, batch, chunk, piece, device):
        place = chunk_place(batch, chunk, piece)
        remote(
            place, place, chunk_send.at[batch, number], chunk_recv.at[batch, chunk, piece], device
        ).start()

    def arrived(batch, chunk, piece):
        place = chunk_place(batch, chunk, piece)
        remote(
            place, place, chunk_send.at[batch, 0], chunk_recv.at[batch, chunk, piece], to_twin
        ).wait_recv()

    def finish(batch):
        encoded = (unit(hidden[batch]) * final_ref[...]).astype(jnp.bfloat16)
        chunks[batch, y, pl.ds(pl.multiple_of(c * positions, positions), positions)] = encoded
        for piece in range(2):
            ship(piece, batch, me, piece, to_up)
            ship(2 + piece, batch, me, 1 - piece, to_down)
        for piece in range(2):
            ship(4 + piece, batch, me, piece, to_twin)

    def relay_near(batch):
        arrived(batch, at_down, 0)
        ship(6, batch, at_down, 0, to_up)
        ship(7, batch, at_down, 0, to_twin)
        arrived(batch, at_up, 1)
        ship(8, batch, at_up, 1, to_down)
        ship(9, batch, at_up, 1, to_twin)
        arrived(batch, at_down, 1)
        ship(10, batch, at_down, 1, to_twin)
        arrived(batch, at_up, 0)
        ship(11, batch, at_up, 0, to_twin)

    def relay_far(batch):
        for piece in range(2):
            arrived(batch, at_far, piece)
            ship(12 + piece, batch, at_far, piece, to_twin)

    def twin_wait(batch, chunk):
        for piece in range(2):
            arrived(batch, chunk, piece)

    def cross(batch, chip):
        tokens_here = chunks.at[batch, chip]
        for p in range(heads_local // 2):
            lanes = pl.ds(p * pair, pair)
            key = unit_pair(product(tokens_here[...], kv[0, :, lanes]))
            key_s[:, lanes] = key.astype(jnp.bfloat16)
            value = product(tokens_here[...], kv[1, :, lanes]).astype(jnp.bfloat16)
            value_s[:, pl.ds(2 * p * pair, head)] = value[:, :head]
            value_s[:, pl.ds((2 * p + 1) * pair, head)] = value[:, head:]
        one = batch * group + chip * sections
        first_block = plan_ref[batches * group + one]
        second_block = plan_ref[batches * group + one + 1]
        for h in range(heads_local):
            lanes = pl.ds(h * head, head)
            query = jnp.concatenate(
                [queries[first_block, :, lanes], queries[second_block, :, lanes]], axis=0
            )
            mixed = product(
                diagonal(against(query, key_s[:, lanes])), value_s[:, pl.ds(h * pair, pair)]
            )
            sums[one, :, pl.ds(h * pair, pair)] = mixed[:BL]
            sums[one + 1, :, pl.ds(h * pair, pair)] = mixed[BL:]

    give_wait(0)
    part_start(0)
    wall_near(1)
    out_copy.wait()
    wall_wait(0)
    part_wait(0)
    encode(0, 0)
    lax.fori_loop(0, shards, keep_early, 0)
    wall_far(1)
    give_wait(1)
    part_start(1)
    wall_wait(1)
    encode(0, 1)
    finish(0)
    part_wait(1)
    encode(1, 0)
    encode(1, 1)
    finish(1)

    def step(number, carry):
        @pl.when(number == 0)
        def _():
            twin_wait(0, at_twin)

        @pl.when(number == 1)
        def _():
            relay_near(0)
            twin_wait(1, at_twin)

        @pl.when(number == 2)
        def _():
            twin_wait(0, down_twin)

        @pl.when(number == 3)
        def _():
            twin_wait(0, up_twin)

        @pl.when(number == 4)
        def _():
            relay_near(1)
            relay_far(0)
            twin_wait(1, down_twin)

        @pl.when(number == 5)
        def _():
            twin_wait(1, up_twin)

        @pl.when(number == 6)
        def _():
            relay_far(1)
            twin_wait(0, far_twin)

        @pl.when(number == 7)
        def _():
            twin_wait(1, far_twin)

        batch = jnp.where(number < 2, number, jnp.where(number < 6, number // 2 - 1, number - 6))
        turn = jnp.where(number < 2, 0, jnp.where(number < 6, 1 + lax.rem(number, 2), 3))
        chip = jnp.where(
            turn == 0, y, jnp.where(turn == 1, down, jnp.where(turn == 2, up, far))
        )
        cross(batch, chip)
        return carry

    lax.fori_loop(0, batches * chips, step, 0)

    def combine(h, carry):
        wide = pl.ds(pl.multiple_of(h * pair, pair), pair)
        stage[pl.ds(0, BL)] = jnp.zeros((BL, head), jnp.float32)
        for block in range(blocks):
            one = plan_ref[2 * requests + slots * block]
            two = plan_ref[2 * requests + slots * block + 1]
            alive = (live_ref[block] > 1).astype(jnp.float32)
            mixed = sums[one, :, wide] + sums[two, :, wide] * alive
            stage[pl.ds(BL - 1 + block * BL, BL)] = mixed[:, :head] / mixed[:, head:]
        mix_ref[:, pl.ds(pl.multiple_of(h * head, head), head)] = stage[pl.ds(0, tokens)].astype(
            jnp.bfloat16
        )
        return carry

    lax.fori_loop(0, heads_local, combine, 0)
    for batch in range(batches):
        for number in range(14):
            place = chunk_place(batch, me, 0)
            remote(
                place, place, chunk_send.at[batch, number], chunk_recv.at[batch, me, 0], to_twin
            ).wait_send()
    for copy in sent:
        copy.wait_send()


def retrieve(shards, group, cap, ids, entry_rows, data, live, gain, final, query, own, out, kv):
    positions, per_shard, head = data.shape
    layers, features = gain.shape
    batches = 2
    blocks = live.shape[0]
    tokens = query.shape[0]
    chips = group // 2
    dma = pltpu.SemaphoreType.DMA
    bf16, f32 = jnp.bfloat16, jnp.float32
    return pl.pallas_call(
        functools.partial(kernel, shards, group, cap, 3.0 / math.sqrt(head) * math.log2(math.e)),
        out_shape=jax.ShapeDtypeStruct(query.shape, bf16),
        in_specs=[SMEM, SMEM, VMEM, SMEM, VMEM, VMEM, VMEM, ANY, ANY, ANY],
        out_specs=VMEM,
        scratch_shapes=[
            pltpu.VMEM((shards, 1, 128), jnp.int32),
            pltpu.SMEM((3 * ids.shape[0] * ids.shape[1],), jnp.int32),
            pltpu.VMEM((per_shard, positions, head), bf16),
            pltpu.VMEM((shards, 1, 128), jnp.int32),
            pltpu.SMEM((shards, 1, 128), jnp.int32),
            pltpu.VMEM((shards, cap, positions, head), bf16),
            pltpu.VMEM((shards, cap // 2, positions, head), bf16),
            pltpu.VMEM((shards, cap, positions, head), bf16),
            pltpu.VMEM((batches, group, positions, head), bf16),
            pltpu.VMEM((batches, group, positions, head), bf16),
            pltpu.VMEM(own.shape, bf16),
            pltpu.VMEM((layers, 3, features, features), bf16),
            pltpu.VMEM(out.shape, bf16),
            pltpu.VMEM(kv.shape, bf16),
            pltpu.VMEM((2, features, kv.shape[2]), bf16),
            pltpu.VMEM((batches, positions, features), f32),
            pltpu.VMEM((positions, features), bf16),
            pltpu.VMEM((positions, features), bf16),
            pltpu.VMEM((tokens + BL, head), f32),
            pltpu.VMEM((blocks, BL, query.shape[1]), bf16),
            pltpu.VMEM((group * positions, head), bf16),
            pltpu.VMEM((group * positions, head), bf16),
            pltpu.VMEM((group * positions, 2 * head), bf16),
            pltpu.VMEM((2 * positions, group * head), bf16),
            pltpu.VMEM((2 * positions, group * 2 * head), bf16),
            pltpu.VMEM((batches, chips, 2 * positions, features), bf16),
            pltpu.VMEM((batches * group, BL, 2 * query.shape[1]), f32),
            dma((shards,)),
            dma((shards,)),
            dma((batches, shards)),
            dma((batches, shards)),
            dma((batches, group)),
            dma((batches, group)),
            dma,
            dma,
            dma,
            dma,
            dma((layers, 14)),
            dma((layers, group, 2)),
            dma((batches, 14)),
            dma((batches, group, 2)),
        ],
        compiler_params=pltpu.CompilerParams(
            collective_id=0, has_side_effects=True, vmem_limit_bytes=60 * 2**20
        ),
    )(ids, entry_rows, data, live, gain, final, query, own, out, kv)


def on_device(
    queries,
    database,
    neighbour_ids,
    live_counts,
    entry_rows,
    enc_gain,
    enc_qkv,
    enc_out,
    final_gain,
    kv_weight,
):
    shards = lax.axis_size("db")
    group = lax.axis_size(GROUP)
    requests = neighbour_ids.shape[0] * neighbour_ids.shape[1]
    capacity = max(2, (requests + shards - 1) // shards)
    return retrieve(
        shards,
        group,
        capacity,
        neighbour_ids,
        entry_rows,
        database,
        live_counts,
        enc_gain,
        final_gain.reshape(1, -1),
        queries,
        enc_qkv.transpose(0, 2, 1, 3),
        enc_out,
        kv_weight,
    )


def solution(mesh):
    return jax.shard_map(
        on_device,
        mesh=mesh,
        in_specs=(
            P("db", GROUP),
            P(None, "db", GROUP),
            P("db", None),
            P("db"),
            P(),
            P(),
            P(None, None, None, GROUP),
            P(),
            P(),
            P(None, None, GROUP),
        ),
        out_specs=P("db", GROUP),
        check_vma=False,
    )
```
